256 devices in a mesh: seq: 64 (over z, y, core), head: 4 (over x).
Axes of the slice: x: 4, y: 4, z: 8, core: 2. Of those that a mesh axis runs over, the one named last changes fastest.
Arguments:
- tokens: bfloat16 [8192, 8192], P('seq', 'head'), may hold values from -6 to 6
- in_blocks: bfloat16 [1536, 4096], P('head'), may hold values from -0.21875 to 0.21875
- in_rows: int32 [1536], P('head'), may hold values from 0 to 127, as said below
- in_cols: int32 [1536], P('head'), may hold values from 0 to 35
- in_count: int32 [4], P('head'), may hold values from 128 to 384, as said below
- dt_weight: bfloat16 [64, 8192], P('head'), may hold values from -0.0625 to 0.0625
- dt_bias: float32 [64], P('head'), may hold values from -4.5 to -3.5
- a_log: float32 [64], P('head'), as said below
- conv_weight: float32 [4, 5120], P(None, 'head'), may hold values from -3 to 3
- conv_bias: float32 [5120], P('head'), may hold values from -1.5 to 1.5
- skip_gain: float32 [64], P('head'), may hold values from 0.5 to 2
- norm_gain: float32 [4096], P('head'), may hold values from 0.5 to 1.5
- out_blocks: bfloat16 [512, 4096], P('head'), may hold values from -0.375 to 0.375
- out_rows: int32 [512], P('head'), may hold values from 0 to 15, as said below
- out_cols: int32 [512], P('head'), may hold values from 0 to 127
- out_count: int32 [4], P('head'), may hold values from 42 to 128, as said below
Outputs:
- mixed_out: bfloat16 [8192, 8192], P('seq', 'head')
The draws below stay inside these ranges and needn't reach their ends.
Inputs may be any that keep to these rules, and one draw needn't show every extreme that they name: Row blocks of the in-projection slots. In each group the (in_rows, in_cols) pairs of all 384 slots are distinct; slots at or past in_count of the group are unused. `in_count`: some group uses all 384 slots. Row blocks of the out-projection slots. In each group the (out_rows, out_cols) pairs of all 128 slots are distinct; slots at or past out_count of the group are unused. `out_count`: some group uses all 128 slots. a_log lies between the logarithms of 25 / 8192 and 1.25.
All inputs are finite; a program needn't handle non-finite values.
Results may differ from the reference program's by a relative error of at most 0.017.
Values may be sent and summed in bfloat16 or wider, within the bound.
A program may use at most 128 MiB of HBM per device.

```python
import math
import jax
import jax.numpy as jnp
from jax import lax

D = 8192
P_SIZE = 64
NSTATE = 128
HPG = 16
CONV = 4
BLOCK = 64
MAXIN = 384
MAXOUT = 128
TOK_DEV = 128
GROUPS = 4
HEADS = 64
SEQLEN = 8192
N_HEAD = 4


def block_layout(key, row_blocks, col_blocks, slot_total):
    shard_keys = jax.random.split(key, N_HEAD)

    def pick_slots(shard_key):
        return jax.random.permutation(shard_key, row_blocks * col_blocks)[:slot_total]
    chosen = jax.vmap(pick_slots)(shard_keys)
    return ((chosen // col_blocks).reshape(-1).astype(jnp.int32), (chosen % col_blocks).reshape(-1).astype(jnp.int32))


def slot_counts(key, slot_total):
    counts = jax.random.randint(key, (N_HEAD,), slot_total // 3, slot_total + 1)
    fullest = jax.random.randint(jax.random.fold_in(key, 12), (), 0, N_HEAD)
    counts = jnp.where(jnp.arange(N_HEAD) == fullest, slot_total, counts)
    return counts.astype(jnp.int32)


def in_layout(key):
    return block_layout(key, D // BLOCK, (2 * HPG * P_SIZE + 2 * NSTATE) // BLOCK, MAXIN)


def out_layout(key):
    return block_layout(jax.random.fold_in(key, 5), HPG * P_SIZE // BLOCK, D // BLOCK, MAXOUT)


def draw_in_rows(key, part):
    return in_layout(key)[0]


def draw_in_cols(key, part):
    return in_layout(key)[1]


def draw_in_count(key, part):
    key = jax.random.fold_in(key, 21)
    return slot_counts(key, MAXIN)


def draw_out_rows(key, part):
    return out_layout(key)[0]


def draw_out_cols(key, part):
    return out_layout(key)[1]


def draw_out_count(key, part):
    key = jax.random.fold_in(key, 22)
    return slot_counts(key, MAXOUT)


def draw_a_log(key, part):
    key = jax.random.fold_in(key, 3)
    slowest = math.log(25.0 / SEQLEN)
    fastest = math.log(1.25)
    portion = jax.random.uniform(key, (HEADS,), jnp.float32, 0.0, 1.0)
    return (slowest + portion * (fastest - slowest)).astype(jnp.float32)


def levels(own_key, extent, shards, least, high):
    level = 1.0
    for dim, parts in shards:
        draws = jax.random.uniform(jax.random.fold_in(jax.random.fold_in(own_key, 6), dim), (parts,), jnp.float32, least / len(shards), high / len(shards))
        level = level * jnp.repeat(jnp.exp(draws), extent[dim] // parts).reshape((-1,) + (1,) * (len(extent) - 1 - dim))
    return level


def centred(key, shape, width, bound, shards=(), kind=jnp.bfloat16):
    level = levels(key, shape, shards, -0.22, 0.18) if shards else 1.0
    values = jax.random.normal(key, shape, jnp.float32) * width * level
    return jnp.minimum(jnp.maximum(values, -bound), bound).astype(kind)


def setup_inputs(seed: int = 0) -> dict:
    keys = jax.random.split(jax.random.key(seed), 17)
    return {
        "tokens": centred(keys[0], (SEQLEN, D), 1.0, 6.0, ((0, 64), (1, 4))),
        "in_blocks": centred(keys[1], (N_HEAD * MAXIN, BLOCK * BLOCK), (MAXIN * BLOCK // ((2 * HPG * P_SIZE + 2 * NSTATE) // BLOCK)) ** -0.5, 0.21875, ((0, 4),)),
        "in_rows": draw_in_rows(jax.random.fold_in(keys[16], 71), 0),
        "in_cols": draw_in_cols(jax.random.fold_in(keys[16], 71), 0),
        "in_count": draw_in_count(jax.random.fold_in(keys[16], 71), 0),
        "dt_weight": centred(keys[5], (HEADS, D), D ** -0.5, 0.0625, ((0, 4),)),
        "dt_bias": jnp.clip(-4.5 + 1.0 * jax.random.uniform(keys[6], (HEADS,), jnp.float32) ** levels(keys[6], (HEADS,), ((0, 4),), -0.2, 0.2), -4.5, -3.5),
        "a_log": draw_a_log(jax.random.fold_in(keys[16], 71), 0),
        "conv_weight": centred(keys[8], (CONV, GROUPS * (HPG * P_SIZE + 2 * NSTATE)), CONV ** -0.5, 3.0, ((1, 4),), jnp.float32),
        "conv_bias": centred(keys[9], (GROUPS * (HPG * P_SIZE + 2 * NSTATE),), 0.3, 1.5, ((0, 4),), jnp.float32),
        "skip_gain": jnp.clip(0.5 + 1.5 * jax.random.uniform(keys[10], (HEADS,), jnp.float32) ** levels(keys[10], (HEADS,), ((0, 4),), -0.2, 0.2), 0.5, 2.0),
        "norm_gain": jnp.clip(1.0 + 0.1 * jax.random.normal(keys[11], (HEADS * P_SIZE,), jnp.float32), 0.5, 1.5),
        "out_blocks": centred(keys[12], (N_HEAD * MAXOUT, BLOCK * BLOCK), (N_HEAD * MAXOUT * BLOCK // (D // BLOCK)) ** -0.5, 0.375, ((0, 4),)),
        "out_rows": draw_out_rows(jax.random.fold_in(keys[16], 71), 0),
        "out_cols": draw_out_cols(jax.random.fold_in(keys[16], 71), 0),
        "out_count": draw_out_count(jax.random.fold_in(keys[16], 71), 0),
    }


norm_epsilon = 1e-05

def rounded(value):
    return lax.optimization_barrier(value.astype(jnp.bfloat16)).astype(jnp.float32)

def block_product(matrix, block_list, row_ids, col_ids, used_slots, accumulator):
    live_mask = (jnp.arange(block_list.shape[0]) < used_slots).astype(jnp.float32)

    def one_block(running_total, block_item):
        flat_block, row_id, col_id, keep_flag = block_item
        weights_block = flat_block.reshape(BLOCK, BLOCK)
        columns = lax.dynamic_slice_in_dim(matrix, (row_id * BLOCK).astype(jnp.int32), BLOCK, 1)
        product = jnp.dot(columns, weights_block, preferred_element_type=jnp.float32) * keep_flag
        offset = (col_id * BLOCK).astype(jnp.int32)
        current = lax.dynamic_slice_in_dim(running_total, offset, BLOCK, 1)
        return (lax.dynamic_update_slice_in_dim(running_total, current + product, offset, 1), None)
    return lax.scan(one_block, accumulator, (block_list, row_ids, col_ids, live_mask))[0]

def stretch_terms(x_heads, b_matrix, c_matrix, step_size, decay_rate):
    length = x_heads.shape[0]
    running = jnp.cumsum(step_size * decay_rate[None, :], axis=0)
    scores = jnp.dot(c_matrix, b_matrix.T, preferred_element_type=jnp.float32)
    position = jnp.arange(length)
    causal = position[:, None] >= position[None, :]
    running_heads = running.T
    gap_log = running_heads[:, :, None] - running_heads[:, None, :]
    decay_factor = jnp.exp(jnp.where(causal[None], gap_log, -jnp.inf))
    weights = scores[None] * decay_factor * step_size.T[:, None, :]
    inner_part = jnp.einsum('hts,shp->thp', rounded(weights), x_heads.astype(jnp.float32))
    tail_factor = jnp.exp(running[-1][None, :] - running) * step_size
    scaled = x_heads.astype(jnp.float32) * tail_factor[:, :, None]
    stretch_state = jnp.einsum('shp,sn->hpn', rounded(scaled), b_matrix.astype(jnp.float32))
    return (inner_part, running, stretch_state)

def reference(tokens, in_blocks, in_rows, in_cols, in_count, dt_weight, dt_bias, a_log, conv_weight, conv_bias, skip_gain, norm_gain, out_blocks, out_rows, out_cols, out_count):
    channels = HPG * P_SIZE
    in_width = 2 * channels + 2 * NSTATE
    conv_span = channels + 2 * NSTATE
    stretch_count = SEQLEN // TOK_DEV
    raw_all = jnp.dot(tokens, dt_weight.T, preferred_element_type=jnp.float32)
    mixed_all = jnp.zeros((SEQLEN, D), jnp.float32)
    for group_index in range(GROUPS):
        in_start = group_index * MAXIN
        in_stop = in_start + MAXIN
        projected = block_product(tokens, in_blocks[in_start:in_stop], in_rows[in_start:in_stop], in_cols[in_start:in_stop], in_count[group_index], jnp.zeros((SEQLEN, in_width), jnp.float32)).astype(jnp.bfloat16)
        gate_part = projected[:, :channels]
        mixed_in = projected[:, channels:]
        padded = jnp.concatenate([jnp.zeros((CONV - 1, conv_span), jnp.bfloat16), mixed_in], axis=0)
        conv_start = group_index * conv_span
        convolved = conv_bias[conv_start:conv_start + conv_span][None, :] + jnp.zeros((SEQLEN, conv_span), jnp.float32)
        for tap_index in range(CONV):
            convolved = convolved + conv_weight[tap_index, conv_start:conv_start + conv_span][None, :] * padded[tap_index:tap_index + SEQLEN].astype(jnp.float32)
        activated = jax.nn.silu(convolved).astype(jnp.bfloat16)
        head_start = group_index * HPG
        x_all = activated[:, :channels].reshape(stretch_count, TOK_DEV, HPG, P_SIZE)
        b_all = activated[:, channels:channels + NSTATE].reshape(stretch_count, TOK_DEV, NSTATE)
        c_all = activated[:, channels + NSTATE:].reshape(stretch_count, TOK_DEV, NSTATE)
        gate_all = gate_part.reshape(stretch_count, TOK_DEV, channels)
        step_all = jax.nn.softplus(raw_all[:, head_start:head_start + HPG] + dt_bias[head_start:head_start + HPG][None, :]).reshape(stretch_count, TOK_DEV, HPG)
        decay_rate = -jnp.exp(a_log[head_start:head_start + HPG])
        skip_part = skip_gain[head_start:head_start + HPG]
        gain_part = norm_gain[group_index * channels:(group_index + 1) * channels]

        def one_stretch(entering, stretch_item):
            x_part, b_part, c_part, gate_piece, step_part = stretch_item
            inner_part, running, stretch_state = stretch_terms(x_part, b_part, c_part, step_part, decay_rate)
            carried = jnp.einsum('tn,hpn->thp', c_part.astype(jnp.float32), rounded(entering)) * jnp.exp(running)[:, :, None]
            output_heads = inner_part + carried + skip_part[None, :, None] * x_part.astype(jnp.float32)
            gated_out = output_heads.reshape(TOK_DEV, channels) * jax.nn.silu(gate_piece.astype(jnp.float32))
            mean_square = lax.optimization_barrier(jnp.mean(gated_out * gated_out, axis=1, keepdims=True))
            normed = (gated_out * lax.rsqrt(mean_square + norm_epsilon) * gain_part[None, :]).astype(jnp.bfloat16)
            leaving = jnp.exp(running[-1])[:, None, None] * entering + stretch_state
            return (leaving, normed)
        normed_all = lax.scan(one_stretch, jnp.zeros((HPG, P_SIZE, NSTATE), jnp.float32), (x_all, b_all, c_all, gate_all, step_all))[1].reshape(SEQLEN, channels)
        full_rows = jnp.zeros((SEQLEN, HEADS * P_SIZE), jnp.bfloat16)
        full_rows = lax.dynamic_update_slice_in_dim(full_rows, normed_all, group_index * channels, 1)
        out_start = group_index * MAXOUT
        out_stop = out_start + MAXOUT
        shifted_rows = out_rows[out_start:out_stop] + group_index * (channels // BLOCK)
        mixed_all = block_product(full_rows, out_blocks[out_start:out_stop], shifted_rows, out_cols[out_start:out_stop], out_count[group_index], mixed_all)
    return mixed_all.astype(jnp.bfloat16)
```

```python
import functools

import jax
import jax.numpy as jnp
from jax import lax
from jax.experimental import pallas as pl
from jax.experimental.pallas import tpu as pltpu
from jax.sharding import PartitionSpec as P

MESH = pl.DeviceIdType.MESH
BF = jnp.bfloat16
F32 = jnp.float32
BLOCK = 64
TOK = 128
UNROLL = 8
EPS = 1e-05
VMEM = pl.BlockSpec(memory_space=pltpu.VMEM)
SMEM = pl.BlockSpec(memory_space=pltpu.SMEM)


def sds(shape, dtype):
    return jax.ShapeDtypeStruct(shape, dtype)


def dot(a, b, ca=1, cb=0, precision=None):
    return lax.dot_general(
        a, b, (((ca,), (cb,)), ((), ())), preferred_element_type=F32, precision=precision
    )


def lists_kernel(
    in_total, out_total, in_rows, in_cols, in_count, out_rows, out_cols, out_count, in_list, out_list, in_n, out_n
):
    in_len = in_total + UNROLL
    out_len = out_total + UNROLL
    for q in range(4):
        in_n[q] = 0
        out_n[q] = 0

    def one_in(k, carry):
        r = in_rows[k]
        q = r // 32
        n = in_n[q]
        in_list[q * in_len + n] = (k // 2) * 16384 + (k % 2) * 4096 + (r % 32) * 64 + in_cols[k]
        in_n[q] = n + 1
        return carry

    lax.fori_loop(0, in_count[0], one_in, 0)

    def one_out(k, carry):
        c = out_cols[k]
        q = c // 32
        n = out_n[q]
        out_list[q * out_len + n] = (k // 2) * 16384 + (k % 2) * 4096 + out_rows[k] * 64 + c % 32
        out_n[q] = n + 1
        return carry

    lax.fori_loop(0, out_count[0], one_out, 0)
    for q in range(4):
        for u in range(UNROLL):
            in_list[q * in_len + in_n[q] + u] = 2 * 4096
            out_list[q * out_len + out_n[q] + u] = 2 * 4096


def make_lists(in_rows, in_cols, in_count, out_rows, out_cols, out_count):
    a, b = in_rows.shape[0], out_rows.shape[0]
    return pl.pallas_call(
        functools.partial(lists_kernel, a, b),
        out_shape=[
            sds((4 * (a + UNROLL),), jnp.int32),
            sds((4 * (b + UNROLL),), jnp.int32),
            sds((4,), jnp.int32),
            sds((4,), jnp.int32),
        ],
        in_specs=[SMEM] * 6,
        out_specs=[SMEM] * 4,
        cost_estimate=pl.CostEstimate(flops=1000000, bytes_accessed=4000000, transcendentals=0),
    )(in_rows, in_cols, in_count, out_rows, out_cols, out_count)


def accumulate(x_ref, w_ref, mask_ref, list_ref, base, count, acc_ref):
    def turn(i, carry):
        parts = []
        for u in range(UNROLL):
            e = list_ref[base + i * UNROLL + u]
            pair = e // 16384
            which = (e // 4096) % 4
            r = pl.multiple_of(((e // 64) % 64) * BLOCK, BLOCK)
            c = pl.multiple_of((e % 64) * BLOCK, BLOCK)
            w = w_ref[pair] * mask_ref[which]
            x = x_ref[pl.ds(r, BLOCK), :]
            parts.append((c, dot(w, jnp.concatenate([x, x], axis=0))))
        for c, product in parts:
            acc_ref[pl.ds(c, BLOCK), :] += product
        return carry

    lax.fori_loop(0, (count + UNROLL - 1) // UNROLL, turn, 0)


def in_kernel(offsets, halves, first, me_ref, list_ref, n_ref, w_ref, mask_ref, dt_ref, *rest):
    x_refs = rest[: len(offsets) * (2 if halves else 1)]
    rest = rest[len(x_refs) :]
    if first:
        acc_ref, raw_ref = rest[:2]
        acc_ref[...] = jnp.zeros_like(acc_ref)
        raw_ref[...] = jnp.zeros_like(raw_ref)
    else:
        acc_in, raw_in, acc_ref, raw_ref = rest[:4]
        acc_ref[...] = acc_in[...]
        raw_ref[...] = raw_in[...]
    in_len = list_ref.shape[0] // 4
    if halves:
        joined = rest[-1]
        joined[pl.ds(0, 1024), :] = x_refs[0][...]
        joined[pl.ds(1024, 1024), :] = x_refs[1][...]
        x_refs = [joined]
    for x_ref, offset in zip(x_refs, offsets):
        q = lax.rem(me_ref[0] + offset, 4)
        columns = pl.ds(pl.multiple_of(q * 2048, 2048), 2048)
        raw_ref[...] += dot(dt_ref[:, columns], x_ref[...])
        accumulate(x_ref, w_ref, mask_ref, list_ref, q * in_len, n_ref[q], acc_ref)


def in_projection(me, in_list, in_n, w, mask, dt_weight, xs, offsets, acc=None, halves=False, cost=1):
    first = acc is None
    width = 2304
    previous = () if first else acc
    return pl.pallas_call(
        functools.partial(in_kernel, offsets, halves, first),
        out_shape=[sds((width, TOK), F32), sds((16, TOK), F32)],
        in_specs=[SMEM] * 3 + [VMEM] * (3 + len(xs) + len(previous)),
        out_specs=[VMEM] * 2,
        scratch_shapes=[pltpu.VMEM((2048, TOK), BF)] if halves else [],
        compiler_params=pltpu.CompilerParams(vmem_limit_bytes=32 * 1024 * 1024),
        cost_estimate=pl.CostEstimate(flops=cost * 1000000000, bytes_accessed=cost * 8000000, transcendentals=0),
    )(me, in_list, in_n, w, mask, dt_weight, *xs, *previous)


def out_kernel(offsets, me_ref, list_ref, n_ref, w_ref, mask_ref, x_ref, *acc_refs):
    out_len = list_ref.shape[0] // 4
    for offset, acc_ref in zip(offsets, acc_refs):
        acc_ref[...] = jnp.zeros_like(acc_ref)
        q = lax.rem(me_ref[0] + offset, 4)
        accumulate(x_ref, w_ref, mask_ref, list_ref, q * out_len, n_ref[q], acc_ref)


def out_projection(me, out_list, out_n, w, mask, normed, offsets, cost):
    return pl.pallas_call(
        functools.partial(out_kernel, offsets),
        out_shape=[sds((2048, TOK), F32)] * len(offsets),
        in_specs=[SMEM] * 3 + [VMEM] * 3,
        out_specs=[VMEM] * len(offsets),
        compiler_params=pltpu.CompilerParams(vmem_limit_bytes=32 * 1024 * 1024),
        cost_estimate=pl.CostEstimate(flops=cost * 1000000000, bytes_accessed=cost * 8000000, transcendentals=0),
    )(me, out_list, out_n, w, mask, normed)


def silu(v):
    return v / (1.0 + jnp.exp(-v))


def pack_log(value):
    high = value.astype(BF)
    low = (value - high.astype(F32)).astype(BF)
    return high, low


def mixer_kernel(
    acc_ref,
    raw_ref,
    chan_ref,
    head_ref,
    out_ref,
    mixed,
    x_ref,
    inner,
    gate_ref,
    rim_out,
    rim_in,
    own_state,
    send0,
    recv0,
    send1,
    recv1,
    logs1,
    send2,
    recv2,
    send3,
    recv3,
    recv4,
    prior,
    rim_sems,
    sems0,
    ssem1,
    rsem1,
    sems2,
    ssem3,
    rsem3,
    sems4,
):
    s = lax.axis_index("seq")
    g = lax.axis_index("head")
    core = s % 2
    y = (s // 2) % 4
    z = s // 8

    def at_y(v):
        return z * 8 + ((y + v) % 4) * 2 + core

    def at_z(v):
        return ((z + v) % 8) * 8 + s % 8

    mate = s + 1 - 2 * core
    after = (s + 1) % 64
    before = (s + 63) % 64
    barrier = pltpu.get_barrier_semaphore()
    partners = [after, before, mate, at_y(1), at_y(2), at_y(3)] + [at_z(v) for v in (1, 2, 4, 6, 7)]
    for partner in partners:
        pl.semaphore_signal(barrier, inc=1, device_id=(partner, g), device_id_type=MESH)

    def copy(src, dst, send_sem, recv_sem, to):
        return pltpu.make_async_remote_copy(
            src_ref=src,
            dst_ref=dst,
            send_sem=send_sem,
            recv_sem=recv_sem,
            device_id=(to, g),
            device_id_type=MESH,
        )

    own_mixed = acc_ref[pl.ds(1024, 1280), :].astype(BF)
    mixed[...] = own_mixed.astype(F32)
    row16 = lax.broadcasted_iota(jnp.int32, (16, TOK), 0)
    lane16 = lax.broadcasted_iota(jnp.int32, (16, TOK), 1)
    pick = jnp.where((lane16 == row16 + 125) & (row16 < 3), 1.0, 0.0).astype(BF)
    rim_out[...] = dot(pick, own_mixed, 1, 1).astype(BF)
    pl.semaphore_wait(barrier, len(partners))
    rim_copy = copy(rim_out, rim_in, rim_sems.at[0], rim_sems.at[1], after)
    rim_copy.start()

    lane = lax.broadcasted_iota(jnp.int32, (TOK, TOK), 1)
    row = lax.broadcasted_iota(jnp.int32, (TOK, TOK), 0)
    v = raw_ref[...] + head_ref[0]
    step = jnp.maximum(v, 0.0) + jnp.log1p(jnp.exp(-jnp.abs(v)))
    rate = -jnp.exp(head_ref[1])
    pace = step * rate
    causal = row <= lane
    running = dot(pace, jnp.where(causal, 1.0, 0.0), precision=lax.Precision.HIGHEST)
    total = dot(pace, jnp.ones((TOK, TOK), F32), precision=lax.Precision.HIGHEST)
    tail = jnp.exp(total - running) * step
    lead = jnp.exp(running)
    columns = jnp.concatenate([running, step, jnp.zeros((96, TOK), F32)], axis=0).T
    gate_ref[...] = silu(acc_ref[pl.ds(0, 1024), :].astype(BF).astype(F32))

    rim_copy.wait_recv()
    keep = jnp.where(s > 0, 1.0, 0.0)
    place = jnp.where((lane16 == row16 + 125) & (row16 < 3), keep, 0.0).astype(BF)
    b_t = None
    c_t = None
    for part in range(10):
        rows = pl.ds(part * 128, 128)
        own = mixed[rows, :]
        rim = dot(rim_in[:, rows], place, 0, 0)
        total_v = jnp.broadcast_to(chan_ref[rows, 4:5], (128, TOK))
        for tap in range(4):
            shift = 3 - tap
            if shift:
                moved = pltpu.roll(jnp.where(lane >= TOK - shift, rim, own), shift, 1)
            else:
                moved = own
            total_v = total_v + chan_ref[rows, tap : tap + 1] * moved
        active = silu(total_v).astype(BF)
        if part < 8:
            x_ref[rows, :] = active
            for k in range(2):
                h = part * 2 + k
                piece = active[k * 64 : k * 64 + 64, :].astype(F32)
                send0[pl.ds(h * 64, 64), :] = (piece * tail[h : h + 1, :]).astype(BF)
        elif part == 8:
            b_t = active
        else:
            c_t = active
    own_state[...] = dot(send0[pl.ds(0, 1024), :], b_t, 1, 1)

    send0[pl.ds(0, 1024), :] = own_state[...].astype(BF)
    high, low = pack_log(total)
    send0[pl.ds(1024, 16), :] = high
    send0[pl.ds(1040, 16), :] = low
    copy0 = copy(send0, recv0, sems0.at[0], sems0.at[1], mate)
    copy0.start()

    scores = dot(b_t, c_t, 0, 0)

    def inner_heads(first, last):
        for h in range(first, last):
            gap = running[h : h + 1, :] - columns[:, h : h + 1]
            factor = jnp.exp(jnp.where(causal, gap, -jnp.inf))
            weights = (scores * factor * columns[:, 16 + h : 17 + h]).astype(BF)
            rows = pl.ds(h * 64, 64)
            xh = x_ref[rows, :]
            inner[rows, :] = dot(xh, weights) + chan_ref[rows, 6:7] * xh.astype(F32)

    inner_heads(0, 4)
    copy0.wait_recv()
    mate_log = recv0[pl.ds(1024, 16), :].astype(F32) + recv0[pl.ds(1040, 16), :].astype(F32)
    is_first = core == 0
    own_by = jnp.where(is_first, jnp.exp(mate_log), 1.0)
    mate_by = jnp.where(is_first, 1.0, jnp.exp(total))
    chip_log = total + mate_log
    high, low = pack_log(chip_log)
    logs1[4] = own_by
    logs1[5] = mate_by
    for j in range(4):
        for k in range(2):
            h = core * 8 + j * 2 + k
            rows = pl.ds(pl.multiple_of(h * 64, 64), 64)
            chip_state = logs1[4, pl.ds(h, 1), :] * own_state[rows, :] + logs1[5, pl.ds(h, 1), :] * recv0[
                rows, :
            ].astype(F32)
            send1[j, pl.ds(k * 64, 64), :] = chip_state.astype(BF)
        send1[j, pl.ds(128, 16), :] = high
        send1[j, pl.ds(144, 16), :] = low
    copies1 = []
    for v in range(1, 4):
        to = (y + v) % 4
        c = copy(send1.at[to], recv1.at[y], ssem1.at[v - 1], rsem1.at[v - 1], at_y(v))
        c.start()
        copies1.append(c)
    recv1[y] = send1[y]
    inner_heads(4, 6)
    for c in copies1:
        c.wait_recv()
    rows_log = []
    states = []
    first_head = core * 8 + y * 2
    for j in range(4):
        logs1[j] = recv1[j, pl.ds(128, 16), :].astype(F32) + recv1[j, pl.ds(144, 16), :].astype(F32)
        pair = [logs1[j, pl.ds(first_head + k, 1), :] for k in range(2)]
        rows_log.append(jnp.concatenate([jnp.broadcast_to(p, (64, TOK)) for p in pair], axis=0))
        states.append(recv1[j, pl.ds(0, 128), :].astype(F32))
    window = states[0]
    window_log = rows_log[0]
    for j in range(1, 4):
        window = jnp.exp(rows_log[j]) * window + states[j]
        window_log = window_log + rows_log[j]

    entering = jnp.zeros((128, TOK), F32)
    entering_log = jnp.zeros((128, TOK), F32)
    copies2 = []
    for i, distance in enumerate((1, 2, 4)):
        high, low = pack_log(window_log)
        send2[i, pl.ds(0, 128), :] = window.astype(BF)
        for k in range(2):
            send2[i, pl.ds(128 + 32 * k, 16), :] = high[64 * k : 64 * k + 16, :]
            send2[i, pl.ds(144 + 32 * k, 16), :] = low[64 * k : 64 * k + 16, :]
        c = copy(send2.at[i], recv2.at[i], sems2.at[0, i], sems2.at[1, i], at_z(distance))
        c.start()
        copies2.append(c)
        inner_heads(6 + 3 * i, 9 + 3 * i)
        c.wait_recv()
        valid = z >= distance
        came = jnp.where(valid, recv2[i, pl.ds(0, 128), :].astype(F32), 0.0)
        came_log = []
        for k in range(2):
            part = recv2[i, pl.ds(128 + 32 * k, 16), :].astype(F32) + recv2[
                i, pl.ds(144 + 32 * k, 16), :
            ].astype(F32)
            came_log += [part] * 4
        came_log = jnp.where(valid, jnp.concatenate(came_log, axis=0), 0.0)
        entering = jnp.exp(entering_log) * came + entering
        entering_log = entering_log + came_log
        if distance < 4:
            window = jnp.exp(window_log) * came + window
            window_log = window_log + came_log

    for j in range(4):
        send3[j] = entering.astype(BF)
        if j < 3:
            entering = jnp.exp(rows_log[j]) * entering + states[j]
    copies3 = []
    for v in range(1, 4):
        to = (y + v) % 4
        c = copy(send3.at[to], recv3.at[y], ssem3.at[v - 1], rsem3.at[v - 1], at_y(v))
        c.start()
        copies3.append(c)
    recv3[y] = send3[y]
    inner_heads(15, 16)
    for c in copies3:
        c.wait_recv()
    copy4 = copy(recv3, recv4, sems4.at[0], sems4.at[1], mate)
    copy4.start()
    logs1[4] = jnp.where(is_first, 1.0, jnp.exp(mate_log))
    with_state = jnp.where(is_first, 0.0, 1.0)

    def to_prior(half, source):
        for j in range(4):
            for k in range(2):
                h = half * 8 + j * 2 + k
                rows = pl.ds(pl.multiple_of(h * 64, 64), 64)
                value = source[j, pl.ds(k * 64, 64), :].astype(F32)
                value = logs1[4, pl.ds(h, 1), :] * value + with_state * recv0[rows, :].astype(F32)
                prior[rows, :] = value.astype(BF)

    to_prior(core, recv3)
    copy4.wait_recv()
    to_prior(1 - core, recv4)

    squares = jnp.zeros((8, TOK), F32)
    for h in range(16):
        rows = pl.ds(h * 64, 64)
        carried = dot(prior[rows, :], c_t) * lead[h : h + 1, :]
        gated = (inner[rows, :] + carried) * gate_ref[rows, :]
        inner[rows, :] = gated
        squares = squares + jnp.sum((gated * gated).reshape(8, 8, TOK), axis=0)
    mean = jnp.sum(squares, axis=0, keepdims=True) * (1.0 / 1024.0)
    scale = lax.rsqrt(mean + EPS)
    for h in range(16):
        rows = pl.ds(h * 64, 64)
        out_ref[rows, :] = (inner[rows, :] * scale * chan_ref[rows, 5:6]).astype(BF)

    rim_copy.wait_send()
    copy0.wait_send()
    copy4.wait_send()
    for c in copies1 + copies2 + copies3:
        c.wait_send()


def mixer(acc, raw, chan, heads):
    dma = pltpu.SemaphoreType.DMA
    return pl.pallas_call(
        mixer_kernel,
        out_shape=sds((1024, TOK), BF),
        in_specs=[VMEM] * 4,
        out_specs=VMEM,
        scratch_shapes=[
            pltpu.VMEM((1280, TOK), F32),
            pltpu.VMEM((1024, TOK), BF),
            pltpu.VMEM((1024, TOK), F32),
            pltpu.VMEM((1024, TOK), F32),
            pltpu.VMEM((16, 1280), BF),
            pltpu.VMEM((16, 1280), BF),
            pltpu.VMEM((1024, TOK), F32),
            pltpu.VMEM((1056, TOK), BF),
            pltpu.VMEM((1056, TOK), BF),
            pltpu.VMEM((4, 160, TOK), BF),
            pltpu.VMEM((4, 160, TOK), BF),
            pltpu.VMEM((6, 16, TOK), F32),
            pltpu.VMEM((3, 192, TOK), BF),
            pltpu.VMEM((3, 192, TOK), BF),
            pltpu.VMEM((4, 128, TOK), BF),
            pltpu.VMEM((4, 128, TOK), BF),
            pltpu.VMEM((4, 128, TOK), BF),
            pltpu.VMEM((1024, TOK), BF),
            dma((2,)),
            dma((2,)),
            dma((3,)),
            dma((3,)),
            dma((2, 3)),
            dma((3,)),
            dma((3,)),
            dma((2,)),
        ],
        compiler_params=pltpu.CompilerParams(
            collective_id=0, has_side_effects=True, vmem_limit_bytes=32 * 1024 * 1024
        ),
        cost_estimate=pl.CostEstimate(flops=1000000000, bytes_accessed=8000000, transcendentals=0),
    )(acc, raw, chan, heads)


def turned(value, steps):
    count = lax.axis_size("head")
    return lax.ppermute(value, "head", [(i, (i + steps) % count) for i in range(count)])


def paired(blocks):
    pairs = blocks.shape[0] // 2
    return blocks.reshape(pairs, 2, BLOCK, BLOCK).transpose(0, 3, 1, 2).reshape(pairs, BLOCK, 2 * BLOCK)


def per_device(
    tokens,
    in_blocks,
    in_rows,
    in_cols,
    in_count,
    dt_weight,
    dt_bias,
    a_log,
    conv_weight,
    conv_bias,
    skip_gain,
    norm_gain,
    out_blocks,
    out_rows,
    out_cols,
    out_count,
):
    me = lax.axis_index("head").astype(jnp.int32).reshape(1)
    x = tokens.T
    from_left = turned(x, 1)
    from_right = turned(x, -1)

    in_list, out_list, in_n, out_n = make_lists(in_rows, in_cols, in_count, out_rows, out_cols, out_count)
    w_in = paired(in_blocks)
    w_out = paired(out_blocks)
    half = jnp.arange(2 * BLOCK) // BLOCK
    mask = jnp.stack([half == 0, half == 1, half == 2]).astype(BF)
    mask = jnp.broadcast_to(mask[:, None, :], (3, BLOCK, 2 * BLOCK))
    gain = jnp.pad(norm_gain, (0, 256))
    skip = jnp.pad(jnp.repeat(skip_gain, BLOCK), (0, 256))
    chan = jnp.concatenate([conv_weight, jnp.stack([conv_bias, gain, skip, skip])], axis=0).T
    heads = jnp.broadcast_to(jnp.stack([dt_bias, a_log])[:, :, None], (2, 16, TOK))

    common = (me, in_list, in_n, w_in, mask, dt_weight)
    acc = in_projection(*common, [x], [0], cost=2)
    opposite_a = turned(from_left[:1024], 1)
    opposite_b = turned(from_right[1024:], -1)
    acc = in_projection(*common, [from_left, from_right], [3, 1], acc=acc, cost=2)
    acc, raw = in_projection(*common, [opposite_a, opposite_b], [2], acc=acc, halves=True)

    normed = mixer(acc, raw, chan, heads)

    common = (me, out_list, out_n, w_out, mask, normed)
    (far,) = out_projection(*common, [2], 1)
    far = far.astype(BF)
    far_left = turned(far[:1024], 1)
    far_right = turned(far[1024:], -1)
    right, left = out_projection(*common, [1, 3], 2)
    right = jnp.concatenate([right[:1024] + far_left.astype(F32), right[1024:]], axis=0).astype(BF)
    left = jnp.concatenate([left[:1024], left[1024:] + far_right.astype(F32)], axis=0).astype(BF)
    near_left = turned(right, 1)
    near_right = turned(left, -1)
    (own,) = out_projection(*common, [0], 2)
    return (own + near_left.astype(F32) + near_right.astype(F32)).astype(BF).T


def solution(mesh):
    return jax.shard_map(
        per_device,
        mesh=mesh,
        in_specs=(
            P("seq", "head"),
            P("head", None),
            P("head"),
            P("head"),
            P("head"),
            P("head", None),
            P("head"),
            P("head"),
            P(None, "head"),
            P("head"),
            P("head"),
            P("head"),
            P("head", None),
            P("head"),
            P("head"),
            P("head"),
        ),
        out_specs=P("seq", "head"),
        check_vma=False,
    )
```

```python
import functools

import jax
import jax.numpy as jnp
from jax import lax
from jax.experimental import pallas as pl
from jax.experimental.pallas import tpu as pltpu
from jax.sharding import PartitionSpec as P

MESH = pl.DeviceIdType.MESH
BF = jnp.bfloat16
F32 = jnp.float32
BLOCK = 64
TOK = 128
UNROLL = 8
EPS = 1e-05
VMEM = pl.BlockSpec(memory_space=pltpu.VMEM)
SMEM = pl.BlockSpec(memory_space=pltpu.SMEM)


def sds(shape, dtype):
    return jax.ShapeDtypeStruct(shape, dtype)


def dot(a, b, ca=1, cb=0, precision=None):
    return lax.dot_general(
        a, b, (((ca,), (cb,)), ((), ())), preferred_element_type=F32, precision=precision
    )


def block_order(size):
    place = lax.broadcasted_iota(jnp.int32, (size, size), 0)
    feature = lax.broadcasted_iota(jnp.int32, (size, size), 1)
    source = (place & ~63) + 2 * (place & 31) + ((place >> 5) & 1)
    return jnp.where(feature == source, 1.0, 0.0).astype(BF)


def turn_kernel(x_ref, o_ref):
    order = block_order(128)
    for i in range(x_ref.shape[1] // 128):
        rows = pl.ds(128 * i, 128)
        o_ref[rows, :] = dot(order, x_ref[:, rows], 1, 1).astype(BF)


def turn(tokens):
    return pl.pallas_call(
        turn_kernel,
        out_shape=sds((tokens.shape[1], TOK), BF),
        in_specs=[VMEM],
        out_specs=VMEM,
    )(tokens)


def to_tiles(src, dst, unroll=1):
    lane = lax.broadcasted_iota(jnp.int32, (64, 128), 1)
    low = lane < 64

    def sixteen(g, carry):
        v = src[pl.ds(pl.multiple_of(g * 16, 16), 16), :].astype(F32)
        for s0 in (0, 8):
            t = jnp.swapaxes(jnp.stack([v[s0 : s0 + 8, 128 * j : 128 * j + 128] for j in range(32)], axis=0), 0, 1)
            for i in (0, 4):
                m = t[i : i + 4].reshape(128, 128).astype(BF).T.astype(F32)
                even, odd = m[:64], m[64:]
                k = g * 8 + (s0 + i) // 2
                dst[k] = jnp.where(low, even, pltpu.roll(odd, 64, 1)).astype(BF)
                dst[k + 1] = jnp.where(low, pltpu.roll(even, 64, 1), odd).astype(BF)
        return carry

    lax.fori_loop(0, src.shape[0] // 16, sixteen, 0, unroll=unroll)


def to_list(quarter, value, count, length, list_ref, n_ref):
    slots = quarter.shape[1]
    lists = list_ref.shape[0]
    live = lax.broadcasted_iota(jnp.int32, (1, slots), 1) < count
    one_of = lambda n, v: lax.broadcasted_iota(jnp.int32, (n, slots), 0) == v
    member = jnp.where(one_of(8, quarter) & live, 1.0, 0.0)
    before = jnp.where(
        lax.broadcasted_iota(jnp.int32, (slots, slots), 0) < lax.broadcasted_iota(jnp.int32, (slots, slots), 1), 1.0, 0.0
    ).astype(BF)
    order = dot(member.astype(BF), before)
    position = quarter * length + jnp.sum(member * order, axis=0, keepdims=True).astype(jnp.int32)
    row = jnp.where(one_of(lists, position >> 7) & live, 1.0, 0.0)
    lane = jnp.where(one_of(128, position & 127), 1.0, 0.0).astype(BF)
    filled = dot(row.astype(BF), lane, 1, 1)
    total = jnp.zeros((lists, 128), jnp.int32)
    for shift in (0, 8, 16):
        byte = ((value >> shift) & 255).astype(F32)
        total = total + (dot((row * byte).astype(BF), lane, 1, 1).astype(jnp.int32) << shift)
    list_ref[...] = jnp.where(filled > 0.5, total, 2 << 12)
    n_ref[...] = jnp.broadcast_to(jnp.sum(member, axis=1, keepdims=True), (8, 128)).astype(jnp.int32)


def prepare_kernel(
    in_count, out_count, in_rows, in_cols, out_rows, out_cols, in_blocks, out_blocks, dt_ref, in_list, in_n, out_list, out_n, w_in, w_out, dt_out
):
    slots = in_rows.shape[1]
    k = lax.broadcasted_iota(jnp.int32, (1, slots), 1)
    value = ((k >> 1) << 14) + ((k & 1) << 12) + ((in_rows[...] & 31) << 6) + in_cols[...]
    to_list(in_rows[...] >> 5, value, in_count[0], slots + UNROLL, in_list, in_n)
    slots = out_rows.shape[1]
    k = lax.broadcasted_iota(jnp.int32, (1, slots), 1)
    value = ((k >> 1) << 14) + ((k & 1) << 12) + (out_rows[...] << 6) + (out_cols[...] & 31)
    to_list(out_cols[...] >> 5, value, out_count[0], slots + UNROLL, out_list, out_n)
    to_tiles(in_blocks, w_in, 2)
    to_tiles(out_blocks, w_out, 2)
    order = block_order(128)
    for i in range(dt_ref.shape[1] // 128):
        rows = pl.ds(128 * i, 128)
        dt_out[:, rows] = dot(dt_ref[:, rows], order, 1, 1).astype(BF)


def prepare(in_blocks, in_rows, in_cols, in_count, out_blocks, out_rows, out_cols, out_count, dt_weight):
    a, b = in_rows.shape[0], out_rows.shape[0]
    return pl.pallas_call(
        prepare_kernel,
        out_shape=[
            sds((16, 128), jnp.int32),
            sds((8, 128), jnp.int32),
            sds((8, 128), jnp.int32),
            sds((8, 128), jnp.int32),
            sds((a // 2, BLOCK, 2 * BLOCK), BF),
            sds((b // 2, BLOCK, 2 * BLOCK), BF),
            sds(dt_weight.shape, BF),
        ],
        in_specs=[SMEM] * 2 + [VMEM] * 7,
        out_specs=[VMEM] * 7,
        compiler_params=pltpu.CompilerParams(vmem_limit_bytes=40 * 1024 * 1024),
        cost_estimate=pl.CostEstimate(flops=1000000000, bytes_accessed=12000000, transcendentals=0),
    )(
        in_count,
        out_count,
        in_rows.reshape(1, a),
        in_cols.reshape(1, a),
        out_rows.reshape(1, b),
        out_cols.reshape(1, b),
        in_blocks,
        out_blocks,
        dt_weight,
    )


def accumulate(x_ref, w_ref, mask_ref, list_ref, base, count, acc_ref):
    def turn(i, carry):
        parts = []
        for u in range(UNROLL):
            at = base + i * UNROLL + u
            e = list_ref[at >> 7, at & 127]
            r = pl.multiple_of(((e >> 6) & 63) * BLOCK, BLOCK)
            c = pl.multiple_of((e & 63) * BLOCK, BLOCK)
            w = w_ref[e >> 14] * mask_ref[(e >> 12) & 3]
            even = x_ref[pl.ds(r, BLOCK // 2), :]
            odd = x_ref[pl.ds(r + BLOCK // 2, BLOCK // 2), :]
            parts.append((c, dot(w, jnp.concatenate([even, even, odd, odd], axis=0))))
        for c, product in parts:
            acc_ref[pl.ds(c, BLOCK), :] += product
        return carry

    lax.fori_loop(0, (count + UNROLL - 1) // UNROLL, turn, 0)


def in_kernel(offsets, halves, first, me_ref, list_ref, n_ref, w_ref, mask_ref, dt_ref, *rest):
    x_refs = rest[: len(offsets) * (2 if halves else 1)]
    rest = rest[len(x_refs) :]
    if first:
        acc_ref, raw_ref = rest[:2]
        acc_ref[...] = jnp.zeros_like(acc_ref)
        raw_ref[...] = jnp.zeros_like(raw_ref)
    else:
        acc_in, raw_in, acc_ref, raw_ref = rest[:4]
        acc_ref[...] = acc_in[...]
        raw_ref[...] = raw_in[...]
    in_len = 2 * w_ref.shape[0] + UNROLL
    if halves:
        joined = rest[-1]
        joined[pl.ds(0, 1024), :] = x_refs[0][...]
        joined[pl.ds(1024, 1024), :] = x_refs[1][...]
        x_refs = [joined]
    for x_ref, offset in zip(x_refs, offsets):
        q = lax.rem(me_ref[0] + offset, 4)
        columns = pl.ds(pl.multiple_of(q * 2048, 2048), 2048)
        raw_ref[...] += dot(dt_ref[:, columns], x_ref[...])
        accumulate(x_ref, w_ref, mask_ref, list_ref, q * in_len, n_ref[q, 0], acc_ref)


def in_projection(me, in_list, in_n, w, mask, dt_weight, xs, offsets, acc=None, halves=False, cost=1):
    first = acc is None
    width = 2304
    previous = () if first else acc
    return pl.pallas_call(
        functools.partial(in_kernel, offsets, halves, first),
        out_shape=[sds((width, TOK), F32), sds((16, TOK), F32)],
        in_specs=[SMEM] * 3 + [VMEM] * (3 + len(xs) + len(previous)),
        out_specs=[VMEM] * 2,
        scratch_shapes=[pltpu.VMEM((2048, TOK), BF)] if halves else [],
        compiler_params=pltpu.CompilerParams(vmem_limit_bytes=32 * 1024 * 1024),
        cost_estimate=pl.CostEstimate(flops=cost * 1000000000, bytes_accessed=cost * 8000000, transcendentals=0),
    )(me, in_list, in_n, w, mask, dt_weight, *xs, *previous)


def out_kernel(offsets, me_ref, list_ref, n_ref, w_ref, mask_ref, x_ref, *acc_refs):
    out_len = 2 * w_ref.shape[0] + UNROLL
    for offset, acc_ref in zip(offsets, acc_refs):
        acc_ref[...] = jnp.zeros_like(acc_ref)
        q = lax.rem(me_ref[0] + offset, 4)
        accumulate(x_ref, w_ref, mask_ref, list_ref, q * out_len, n_ref[q, 0], acc_ref)


def out_projection(me, out_list, out_n, w, mask, normed, offsets, cost):
    return pl.pallas_call(
        functools.partial(out_kernel, offsets),
        out_shape=[sds((2048, TOK), F32)] * len(offsets),
        in_specs=[SMEM] * 3 + [VMEM] * 3,
        out_specs=[VMEM] * len(offsets),
        compiler_params=pltpu.CompilerParams(vmem_limit_bytes=32 * 1024 * 1024),
        cost_estimate=pl.CostEstimate(flops=cost * 1000000000, bytes_accessed=cost * 8000000, transcendentals=0),
    )(me, out_list, out_n, w, mask, normed)


def silu(v):
    return v / (1.0 + jnp.exp(-v))


def pack_log(value):
    high = value.astype(BF)
    low = (value - high.astype(F32)).astype(BF)
    return high, low


def mixer_kernel(
    acc_ref,
    raw_ref,
    chan_ref,
    head_ref,
    out_ref,
    mixed,
    x_ref,
    inner,
    gate_ref,
    rim_out,
    rim_in,
    own_state,
    send0,
    recv0,
    send1,
    recv1,
    logs1,
    send2,
    recv2,
    send3,
    recv3,
    recv4,
    prior,
    rim_sems,
    sems0,
    ssem1,
    rsem1,
    sems2,
    ssem3,
    rsem3,
    sems4,
):
    s = lax.axis_index("seq")
    g = lax.axis_index("head")
    core = s % 2
    y = (s // 2) % 4
    z = s // 8

    def at_y(v):
        return z * 8 + ((y + v) % 4) * 2 + core

    def at_z(v):
        return ((z + v) % 8) * 8 + s % 8

    mate = s + 1 - 2 * core
    after = (s + 1) % 64
    before = (s + 63) % 64
    barrier = pltpu.get_barrier_semaphore()
    partners = [after, before, mate, at_y(1), at_y(2), at_y(3)] + [at_z(v) for v in (1, 2, 4, 6, 7)]
    for partner in partners:
        pl.semaphore_signal(barrier, inc=1, device_id=(partner, g), device_id_type=MESH)

    def copy(src, dst, send_sem, recv_sem, to):
        return pltpu.make_async_remote_copy(
            src_ref=src,
            dst_ref=dst,
            send_sem=send_sem,
            recv_sem=recv_sem,
            device_id=(to, g),
            device_id_type=MESH,
        )

    own_mixed = acc_ref[pl.ds(1024, 1280), :].astype(BF)
    mixed[...] = own_mixed.astype(F32)
    row16 = lax.broadcasted_iota(jnp.int32, (16, TOK), 0)
    lane16 = lax.broadcasted_iota(jnp.int32, (16, TOK), 1)
    pick = jnp.where((lane16 == row16 + 125) & (row16 < 3), 1.0, 0.0).astype(BF)
    rim_out[...] = dot(pick, own_mixed, 1, 1).astype(BF)
    pl.semaphore_wait(barrier, len(partners))
    rim_copy = copy(rim_out, rim_in, rim_sems.at[0], rim_sems.at[1], after)
    rim_copy.start()

    lane = lax.broadcasted_iota(jnp.int32, (TOK, TOK), 1)
    row = lax.broadcasted_iota(jnp.int32, (TOK, TOK), 0)
    v = raw_ref[...] + head_ref[0]
    step = jnp.maximum(v, 0.0) + jnp.log1p(jnp.exp(-jnp.abs(v)))
    rate = -jnp.exp(head_ref[1])
    pace = step * rate
    causal = row <= lane
    running = dot(pace, jnp.where(causal, 1.0, 0.0), precision=lax.Precision.HIGHEST)
    total = dot(pace, jnp.ones((TOK, TOK), F32), precision=lax.Precision.HIGHEST)
    tail = jnp.exp(total - running) * step
    lead = jnp.exp(running)
    columns = jnp.concatenate([running, step, jnp.zeros((96, TOK), F32)], axis=0).T
    gate_ref[...] = silu(acc_ref[pl.ds(0, 1024), :].astype(BF).astype(F32))

    rim_copy.wait_recv()
    keep = jnp.where(s > 0, 1.0, 0.0)
    place = jnp.where((lane16 == row16 + 125) & (row16 < 3), keep, 0.0).astype(BF)
    b_t = None
    c_t = None
    for part in range(10):
        rows = pl.ds(part * 128, 128)
        own = mixed[rows, :]
        rim = dot(rim_in[:, rows], place, 0, 0)
        total_v = jnp.broadcast_to(chan_ref[rows, 4:5], (128, TOK))
        for tap in range(4):
            shift = 3 - tap
            if shift:
                moved = pltpu.roll(jnp.where(lane >= TOK - shift, rim, own), shift, 1)
            else:
                moved = own
            total_v = total_v + chan_ref[rows, tap : tap + 1] * moved
        active = silu(total_v).astype(BF)
        if part < 8:
            x_ref[rows, :] = active
            for k in range(2):
                h = part * 2 + k
                piece = active[k * 64 : k * 64 + 64, :].astype(F32)
                send0[pl.ds(h * 64, 64), :] = (piece * tail[h : h + 1, :]).astype(BF)
        elif part == 8:
            b_t = active
        else:
            c_t = active
    own_state[...] = dot(send0[pl.ds(0, 1024), :], b_t, 1, 1)

    send0[pl.ds(0, 1024), :] = own_state[...].astype(BF)
    high, low = pack_log(total)
    send0[pl.ds(1024, 16), :] = high
    send0[pl.ds(1040, 16), :] = low
    copy0 = copy(send0, recv0, sems0.at[0], sems0.at[1], mate)
    copy0.start()

    scores = dot(b_t, c_t, 0, 0)

    def inner_heads(first, last):
        for h in range(first, last):
            gap = running[h : h + 1, :] - columns[:, h : h + 1]
            factor = jnp.exp(jnp.where(causal, gap, -jnp.inf))
            weights = (scores * factor * columns[:, 16 + h : 17 + h]).astype(BF)
            rows = pl.ds(h * 64, 64)
            xh = x_ref[rows, :]
            inner[rows, :] = dot(xh, weights) + chan_ref[rows, 6:7] * xh.astype(F32)

    inner_heads(0, 4)
    copy0.wait_recv()
    mate_log = recv0[pl.ds(1024, 16), :].astype(F32) + recv0[pl.ds(1040, 16), :].astype(F32)
    is_first = core == 0
    own_by = jnp.where(is_first, jnp.exp(mate_log), 1.0)
    mate_by = jnp.where(is_first, 1.0, jnp.exp(total))
    chip_log = total + mate_log
    high, low = pack_log(chip_log)
    logs1[4] = own_by
    logs1[5] = mate_by
    for j in range(4):
        for k in range(2):
            h = core * 8 + j * 2 + k
            rows = pl.ds(pl.multiple_of(h * 64, 64), 64)
            chip_state = logs1[4, pl.ds(h, 1), :] * own_state[rows, :] + logs1[5, pl.ds(h, 1), :] * recv0[
                rows, :
            ].astype(F32)
            send1[j, pl.ds(k * 64, 64), :] = chip_state.astype(BF)
        send1[j, pl.ds(128, 16), :] = high
        send1[j, pl.ds(144, 16), :] = low
    copies1 = []
    for v in range(1, 4):
        to = (y + v) % 4
        c = copy(send1.at[to], recv1.at[y], ssem1.at[v - 1], rsem1.at[v - 1], at_y(v))
        c.start()
        copies1.append(c)
    recv1[y] = send1[y]
    inner_heads(4, 6)
    for c in copies1:
        c.wait_recv()
    rows_log = []
    states = []
    first_head = core * 8 + y * 2
    for j in range(4):
        logs1[j] = recv1[j, pl.ds(128, 16), :].astype(F32) + recv1[j, pl.ds(144, 16), :].astype(F32)
        pair = [logs1[j, pl.ds(first_head + k, 1), :] for k in range(2)]
        rows_log.append(jnp.concatenate([jnp.broadcast_to(p, (64, TOK)) for p in pair], axis=0))
        states.append(recv1[j, pl.ds(0, 128), :].astype(F32))
    window = states[0]
    window_log = rows_log[0]
    for j in range(1, 4):
        window = jnp.exp(rows_log[j]) * window + states[j]
        window_log = window_log + rows_log[j]

    entering = jnp.zeros((128, TOK), F32)
    entering_log = jnp.zeros((128, TOK), F32)
    copies2 = []
    for i, distance in enumerate((1, 2, 4)):
        high, low = pack_log(window_log)
        send2[i, pl.ds(0, 128), :] = window.astype(BF)
        for k in range(2):
            send2[i, pl.ds(128 + 32 * k, 16), :] = high[64 * k : 64 * k + 16, :]
            send2[i, pl.ds(144 + 32 * k, 16), :] = low[64 * k : 64 * k + 16, :]
        c = copy(send2.at[i], recv2.at[i], sems2.at[0, i], sems2.at[1, i], at_z(distance))
        c.start()
        copies2.append(c)
        inner_heads(6 + 3 * i, 9 + 3 * i)
        c.wait_recv()
        valid = z >= distance
        came = jnp.where(valid, recv2[i, pl.ds(0, 128), :].astype(F32), 0.0)
        came_log = []
        for k in range(2):
            part = recv2[i, pl.ds(128 + 32 * k, 16), :].astype(F32) + recv2[
                i, pl.ds(144 + 32 * k, 16), :
            ].astype(F32)
            came_log += [part] * 4
        came_log = jnp.where(valid, jnp.concatenate(came_log, axis=0), 0.0)
        entering = jnp.exp(entering_log) * came + entering
        entering_log = entering_log + came_log
        if distance < 4:
            window = jnp.exp(window_log) * came + window
            window_log = window_log + came_log

    for j in range(4):
        send3[j] = entering.astype(BF)
        if j < 3:
            entering = jnp.exp(rows_log[j]) * entering + states[j]
    copies3 = []
    for v in range(1, 4):
        to = (y + v) % 4
        c = copy(send3.at[to], recv3.at[y], ssem3.at[v - 1], rsem3.at[v - 1], at_y(v))
        c.start()
        copies3.append(c)
    recv3[y] = send3[y]
    inner_heads(15, 16)
    for c in copies3:
        c.wait_recv()
    copy4 = copy(recv3, recv4, sems4.at[0], sems4.at[1], mate)
    copy4.start()
    logs1[4] = jnp.where(is_first, 1.0, jnp.exp(mate_log))
    with_state = jnp.where(is_first, 0.0, 1.0)

    def to_prior(half, source):
        for j in range(4):
            for k in range(2):
                h = half * 8 + j * 2 + k
                rows = pl.ds(pl.multiple_of(h * 64, 64), 64)
                value = source[j, pl.ds(k * 64, 64), :].astype(F32)
                value = logs1[4, pl.ds(h, 1), :] * value + with_state * recv0[rows, :].astype(F32)
                prior[rows, :] = value.astype(BF)

    to_prior(core, recv3)
    copy4.wait_recv()
    to_prior(1 - core, recv4)

    squares = jnp.zeros((8, TOK), F32)
    for h in range(16):
        rows = pl.ds(h * 64, 64)
        carried = dot(prior[rows, :], c_t) * lead[h : h + 1, :]
        gated = (inner[rows, :] + carried) * gate_ref[rows, :]
        inner[rows, :] = gated
        squares = squares + jnp.sum((gated * gated).reshape(8, 8, TOK), axis=0)
    mean = jnp.sum(squares, axis=0, keepdims=True) * (1.0 / 1024.0)
    scale = lax.rsqrt(mean + EPS)
    order = block_order(64)
    for h in range(16):
        rows = pl.ds(h * 64, 64)
        normed = (inner[rows, :] * scale * chan_ref[rows, 5:6]).astype(BF)
        out_ref[rows, :] = dot(order, normed).astype(BF)

    rim_copy.wait_send()
    copy0.wait_send()
    copy4.wait_send()
    for c in copies1 + copies2 + copies3:
        c.wait_send()


def mixer(acc, raw, chan, heads):
    dma = pltpu.SemaphoreType.DMA
    return pl.pallas_call(
        mixer_kernel,
        out_shape=sds((1024, TOK), BF),
        in_specs=[VMEM] * 4,
        out_specs=VMEM,
        scratch_shapes=[
            pltpu.VMEM((1280, TOK), F32),
            pltpu.VMEM((1024, TOK), BF),
            pltpu.VMEM((1024, TOK), F32),
            pltpu.VMEM((1024, TOK), F32),
            pltpu.VMEM((16, 1280), BF),
            pltpu.VMEM((16, 1280), BF),
            pltpu.VMEM((1024, TOK), F32),
            pltpu.VMEM((1056, TOK), BF),
            pltpu.VMEM((1056, TOK), BF),
            pltpu.VMEM((4, 160, TOK), BF),
            pltpu.VMEM((4, 160, TOK), BF),
            pltpu.VMEM((6, 16, TOK), F32),
            pltpu.VMEM((3, 192, TOK), BF),
            pltpu.VMEM((3, 192, TOK), BF),
            pltpu.VMEM((4, 128, TOK), BF),
            pltpu.VMEM((4, 128, TOK), BF),
            pltpu.VMEM((4, 128, TOK), BF),
            pltpu.VMEM((1024, TOK), BF),
            dma((2,)),
            dma((2,)),
            dma((3,)),
            dma((3,)),
            dma((2, 3)),
            dma((3,)),
            dma((3,)),
            dma((2,)),
        ],
        compiler_params=pltpu.CompilerParams(
            collective_id=0, has_side_effects=True, vmem_limit_bytes=32 * 1024 * 1024
        ),
        cost_estimate=pl.CostEstimate(flops=1000000000, bytes_accessed=8000000, transcendentals=0),
    )(acc, raw, chan, heads)


def turned(value, steps):
    count = lax.axis_size("head")
    return lax.ppermute(value, "head", [(i, (i + steps) % count) for i in range(count)])


def per_device(
    tokens,
    in_blocks,
    in_rows,
    in_cols,
    in_count,
    dt_weight,
    dt_bias,
    a_log,
    conv_weight,
    conv_bias,
    skip_gain,
    norm_gain,
    out_blocks,
    out_rows,
    out_cols,
    out_count,
):
    me = lax.axis_index("head").astype(jnp.int32).reshape(1)
    x = turn(tokens)
    from_left = turned(x, 1)
    from_right = turned(x, -1)

    in_list, in_n, out_list, out_n, w_in, w_out, dt_weight = prepare(
        in_blocks, in_rows, in_cols, in_count, out_blocks, out_rows, out_cols, out_count, dt_weight
    )
    half = (jnp.arange(2 * BLOCK) // 32) % 2
    mask = jnp.stack([half == 0, half == 1, half == 2]).astype(BF)
    mask = jnp.broadcast_to(mask[:, None, :], (3, BLOCK, 2 * BLOCK))
    gain = jnp.pad(norm_gain, (0, 256))
    skip = jnp.pad(jnp.repeat(skip_gain, BLOCK), (0, 256))
    chan = jnp.concatenate([conv_weight, jnp.stack([conv_bias, gain, skip, skip])], axis=0).T
    heads = jnp.broadcast_to(jnp.stack([dt_bias, a_log])[:, :, None], (2, 16, TOK))

    common = (me, in_list, in_n, w_in, mask, dt_weight)
    acc = in_projection(*common, [x], [0], cost=2)
    opposite_a = turned(from_left[:1024], 1)
    opposite_b = turned(from_right[1024:], -1)
    acc = in_projection(*common, [from_left, from_right], [3, 1], acc=acc, cost=2)
    acc, raw = in_projection(*common, [opposite_a, opposite_b], [2], acc=acc, halves=True)

    normed = mixer(acc, raw, chan, heads)

    common = (me, out_list, out_n, w_out, mask, normed)
    (far,) = out_projection(*common, [2], 1)
    far = far.astype(BF)
    far_left = turned(far[:1024], 1)
    far_right = turned(far[1024:], -1)
    right, left = out_projection(*common, [1, 3], 2)
    right = jnp.concatenate([right[:1024] + far_left.astype(F32), right[1024:]], axis=0).astype(BF)
    left = jnp.concatenate([left[:1024], left[1024:] + far_right.astype(F32)], axis=0).astype(BF)
    near_left = turned(right, 1)
    near_right = turned(left, -1)
    (own,) = out_projection(*common, [0], 2)
    return (own + near_left.astype(F32) + near_right.astype(F32)).astype(BF).T


def solution(mesh):
    return jax.shard_map(
        per_device,
        mesh=mesh,
        in_specs=(
            P("seq", "head"),
            P("head", None),
            P("head"),
            P("head"),
            P("head"),
            P("head", None),
            P("head"),
            P("head"),
            P(None, "head"),
            P("head"),
            P("head"),
            P("head"),
            P("head", None),
            P("head"),
            P("head"),
            P("head"),
        ),
        out_specs=P("seq", "head"),
        check_vma=False,
    )
```

```python
import functools

import jax
import jax.numpy as jnp
from jax import lax
from jax.experimental import pallas as pl
from jax.experimental.pallas import tpu as pltpu
from jax.sharding import PartitionSpec as P

MESH = pl.DeviceIdType.MESH
BF = jnp.bfloat16
F32 = jnp.float32
BLOCK = 64
TOK = 128
UNROLL = 8
EPS = 1e-05
VMEM = pl.BlockSpec(memory_space=pltpu.VMEM)
SMEM = pl.BlockSpec(memory_space=pltpu.SMEM)


def sds(shape, dtype):
    return jax.ShapeDtypeStruct(shape, dtype)


def dot(a, b, ca=1, cb=0, precision=None):
    return lax.dot_general(
        a, b, (((ca,), (cb,)), ((), ())), preferred_element_type=F32, precision=precision
    )


def block_order(size):
    place = lax.broadcasted_iota(jnp.int32, (size, size), 0)
    feature = lax.broadcasted_iota(jnp.int32, (size, size), 1)
    source = (place & ~63) + 2 * (place & 31) + ((place >> 5) & 1)
    return jnp.where(feature == source, 1.0, 0.0).astype(BF)


def turn_kernel(x_ref, o_ref):
    order = block_order(128)
    for i in range(x_ref.shape[1] // 128):
        rows = pl.ds(128 * i, 128)
        o_ref[rows, :] = dot(order, x_ref[:, rows], 1, 1).astype(BF)


def turn(tokens):
    return pl.pallas_call(
        turn_kernel,
        out_shape=sds((tokens.shape[1], TOK), BF),
        in_specs=[VMEM],
        out_specs=VMEM,
    )(tokens)


def to_tiles(src, dst, unroll=1):
    lane = lax.broadcasted_iota(jnp.int32, (64, 128), 1)
    low = lane < 64

    def sixteen(g, carry):
        v = src[pl.ds(pl.multiple_of(g * 16, 16), 16), :].astype(F32)
        for s0 in (0, 8):
            t = jnp.swapaxes(jnp.stack([v[s0 : s0 + 8, 128 * j : 128 * j + 128] for j in range(32)], axis=0), 0, 1)
            for i in (0, 4):
                m = t[i : i + 4].reshape(128, 128).astype(BF).T.astype(F32)
                even, odd = m[:64], m[64:]
                k = g * 8 + (s0 + i) // 2
                dst[k] = jnp.where(low, even, pltpu.roll(odd, 64, 1)).astype(BF)
                dst[k + 1] = jnp.where(low, pltpu.roll(even, 64, 1), odd).astype(BF)
        return carry

    lax.fori_loop(0, src.shape[0] // 16, sixteen, 0, unroll=unroll)


def to_list(quarter, value, count, length, list_ref, n_ref):
    slots = quarter.shape[1]
    lists = list_ref.shape[0]
    live = lax.broadcasted_iota(jnp.int32, (1, slots), 1) < count
    one_of = lambda n, v: lax.broadcasted_iota(jnp.int32, (n, slots), 0) == v
    member = jnp.where(one_of(8, quarter) & live, 1.0, 0.0)
    before = jnp.where(
        lax.broadcasted_iota(jnp.int32, (slots, slots), 0) < lax.broadcasted_iota(jnp.int32, (slots, slots), 1), 1.0, 0.0
    ).astype(BF)
    order = dot(member.astype(BF), before)
    position = quarter * length + jnp.sum(member * order, axis=0, keepdims=True).astype(jnp.int32)
    row = jnp.where(one_of(lists, position >> 7) & live, 1.0, 0.0)
    lane = jnp.where(one_of(128, position & 127), 1.0, 0.0).astype(BF)
    filled = dot(row.astype(BF), lane, 1, 1)
    total = jnp.zeros((lists, 128), jnp.int32)
    for shift in (0, 8, 16):
        byte = ((value >> shift) & 255).astype(F32)
        total = total + (dot((row * byte).astype(BF), lane, 1, 1).astype(jnp.int32) << shift)
    list_ref[...] = jnp.where(filled > 0.5, total, 2 << 12)
    n_ref[...] = jnp.broadcast_to(jnp.sum(member, axis=1, keepdims=True), (8, 128)).astype(jnp.int32)


def prepare_kernel(
    in_count, out_count, in_rows, in_cols, out_rows, out_cols, dt_ref, in_blocks, out_blocks,
    in_list, in_n, w_in, w_out, dt_out, meta, in_held, out_held, sems,
):
    core = lax.axis_index("seq") % 2
    chunk = in_held.shape[0] // 4
    copies = []
    for i in range(4):
        rows = pl.ds(i * chunk, chunk)
        copies.append(pltpu.make_async_copy(in_blocks.at[rows], in_held.at[rows], sems.at[i]))
    share = out_held.shape[0]
    rows = pl.ds(pl.multiple_of(core * share, share), share)
    copies.append(pltpu.make_async_copy(out_blocks.at[rows], out_held, sems.at[4]))
    for c in copies:
        c.start()
    slots = in_rows.shape[0]
    k = lax.broadcasted_iota(jnp.int32, (1, slots), 1)
    r = in_rows[...].reshape(1, slots)
    value = ((k >> 1) << 14) + ((k & 1) << 12) + ((r & 31) << 6) + in_cols[...].reshape(1, slots)
    to_list(r >> 5, value, in_count[0], slots + UNROLL, in_list, in_n)
    slots = out_rows.shape[0]
    meta[0:1, :] = out_rows[...].reshape(1, slots)
    meta[1:2, :] = out_cols[...].reshape(1, slots)
    meta[2:8, :] = jnp.broadcast_to(out_count[0], (6, slots))
    order = block_order(128)
    for i in range(dt_ref.shape[1] // 128):
        rows = pl.ds(128 * i, 128)
        dt_out[:, rows] = dot(dt_ref[:, rows], order, 1, 1).astype(BF)
    for i in range(4):
        copies[i].wait()
        to_tiles(in_held.at[pl.ds(i * chunk, chunk)], w_in.at[pl.ds(i * chunk // 2, chunk // 2)], 2)
    copies[4].wait()
    to_tiles(out_held, w_out, 2)


def prepare(in_blocks, in_rows, in_cols, in_count, out_blocks, out_rows, out_cols, out_count, dt_weight):
    a, b = in_rows.shape[0], out_rows.shape[0]
    anywhere = pl.BlockSpec(memory_space=pl.ANY)
    return pl.pallas_call(
        prepare_kernel,
        out_shape=[
            sds((16, 128), jnp.int32),
            sds((8, 128), jnp.int32),
            sds((a // 2, BLOCK, 2 * BLOCK), BF),
            sds((b // 4, BLOCK, 2 * BLOCK), BF),
            sds(dt_weight.shape, BF),
            sds((8, 128), jnp.int32),
        ],
        in_specs=[SMEM] * 2 + [VMEM] * 5 + [anywhere] * 2,
        out_specs=[VMEM] * 6,
        scratch_shapes=[
            pltpu.VMEM(in_blocks.shape, BF),
            pltpu.VMEM((b // 2, out_blocks.shape[1]), BF),
            pltpu.SemaphoreType.DMA((5,)),
        ],
        compiler_params=pltpu.CompilerParams(vmem_limit_bytes=40 * 1024 * 1024),
        cost_estimate=pl.CostEstimate(flops=1000000000, bytes_accessed=12000000, transcendentals=0),
    )(in_count, out_count, in_rows, in_cols, out_rows, out_cols, dt_weight, in_blocks, out_blocks)


def fill_mask(mask):
    half = (lax.broadcasted_iota(jnp.int32, (BLOCK, 2 * BLOCK), 1) >> 5) & 1
    for k in range(3):
        mask[k] = jnp.where(half == k, 1.0, 0.0).astype(BF)


def accumulate(x_ref, w_ref, mask_ref, list_ref, base, count, acc_ref):
    def turn(i, carry):
        parts = []
        for u in range(UNROLL):
            at = base + i * UNROLL + u
            e = list_ref[at >> 7, at & 127]
            r = pl.multiple_of(((e >> 6) & 63) * BLOCK, BLOCK)
            c = pl.multiple_of((e & 63) * BLOCK, BLOCK)
            w = w_ref[e >> 14] * mask_ref[(e >> 12) & 3]
            even = x_ref[pl.ds(r, BLOCK // 2), :]
            odd = x_ref[pl.ds(r + BLOCK // 2, BLOCK // 2), :]
            parts.append((c, dot(w, jnp.concatenate([even, even, odd, odd], axis=0))))
        for c, product in parts:
            acc_ref[pl.ds(c, BLOCK), :] += product
        return carry

    lax.fori_loop(0, (count + UNROLL - 1) // UNROLL, turn, 0)


def in_kernel(offsets, halves, first, list_ref, n_ref, w_ref, dt_ref, *rest):
    x_refs = rest[: len(offsets) * (2 if halves else 1)]
    rest = rest[len(x_refs) :]
    mask = rest[-1]
    fill_mask(mask)
    if first:
        acc_ref, raw_ref = rest[:2]
        acc_ref[...] = jnp.zeros_like(acc_ref)
        raw_ref[...] = jnp.zeros_like(raw_ref)
    else:
        acc_in, raw_in, acc_ref, raw_ref = rest[:4]
        acc_ref[...] = acc_in[...]
        raw_ref[...] = raw_in[...]
    in_len = 2 * w_ref.shape[0] + UNROLL
    if halves:
        joined = rest[-2]
        joined[pl.ds(0, 1024), :] = x_refs[0][...]
        joined[pl.ds(1024, 1024), :] = x_refs[1][...]
        x_refs = [joined]
    for x_ref, offset in zip(x_refs, offsets):
        q = (lax.axis_index("head") + offset) & 3
        columns = pl.ds(pl.multiple_of(q * 2048, 2048), 2048)
        raw_ref[...] += dot(dt_ref[:, columns], x_ref[...])
        accumulate(x_ref, w_ref, mask, list_ref, q * in_len, n_ref[q, 0], acc_ref)


def in_projection(in_list, in_n, w, dt_weight, xs, offsets, acc=None, halves=False, cost=1):
    first = acc is None
    width = 2304
    previous = () if first else acc
    mask = pltpu.VMEM((3, BLOCK, 2 * BLOCK), BF)
    return pl.pallas_call(
        functools.partial(in_kernel, offsets, halves, first),
        out_shape=[sds((width, TOK), F32), sds((16, TOK), F32)],
        in_specs=[SMEM] * 2 + [VMEM] * (2 + len(xs) + len(previous)),
        out_specs=[VMEM] * 2,
        scratch_shapes=[pltpu.VMEM((2048, TOK), BF), mask] if halves else [mask],
        compiler_params=pltpu.CompilerParams(vmem_limit_bytes=32 * 1024 * 1024),
        cost_estimate=pl.CostEstimate(flops=cost * 1000000000, bytes_accessed=cost * 8000000, transcendentals=0),
    )(in_list, in_n, w, dt_weight, *xs, *previous)


def out_kernel(list_ref, n_ref, w_ref, x_ref, out_ref, acc, mask):
    fill_mask(mask)
    acc[...] = jnp.zeros_like(acc)
    accumulate(x_ref, w_ref, mask, list_ref, 0, n_ref[0, 0], acc)
    for i in range(acc.shape[0] // 128):
        rows = pl.ds(128 * i, 128)
        out_ref[:, rows] = acc[rows, :].T.astype(BF)


def out_projection(out_list, out_n, w, normed):
    return pl.pallas_call(
        out_kernel,
        out_shape=sds((TOK, 2048), BF),
        in_specs=[SMEM] * 2 + [VMEM] * 2,
        out_specs=VMEM,
        scratch_shapes=[pltpu.VMEM((2048, TOK), F32), pltpu.VMEM((3, BLOCK, 2 * BLOCK), BF)],
        compiler_params=pltpu.CompilerParams(vmem_limit_bytes=32 * 1024 * 1024),
        cost_estimate=pl.CostEstimate(flops=1000000000, bytes_accessed=8000000, transcendentals=0),
    )(out_list, out_n, w, normed)


def list_for(metas, mine, list_ref, n_ref):
    before = jnp.where(
        lax.broadcasted_iota(jnp.int32, (128, 128), 0) < lax.broadcasted_iota(jnp.int32, (128, 128), 1), 1.0, 0.0
    ).astype(BF)
    k = lax.broadcasted_iota(jnp.int32, (1, 128), 1)
    lists = list_ref.shape[0]
    rows_of = lax.broadcasted_iota(jnp.int32, (lists, 128), 0)
    lanes_of = lax.broadcasted_iota(jnp.int32, (128, 128), 0)
    start = jnp.zeros((1, 1), jnp.int32)
    filled = jnp.zeros((lists, 128), F32)
    total = jnp.zeros((lists, 128), jnp.int32)
    for g in range(4):
        rows, cols, count = metas[g, 0:1, :], metas[g, 1:2, :], metas[g, 2:3, :]
        live = (k < count) & ((cols >> 5) == mine)
        member = jnp.where(live, 1.0, 0.0)
        order = dot(jnp.broadcast_to(member, (16, 128)).astype(BF), before)[0:1, :]
        position = order.astype(jnp.int32) + start
        value = ((g * 64 + (k >> 1)) << 14) + ((k & 1) << 12) + ((g * 16 + rows) << 6) + (cols & 31)
        row = jnp.where((rows_of == (position >> 7)) & live, 1.0, 0.0)
        lane = jnp.where(lanes_of == (position & 127), 1.0, 0.0).astype(BF)
        filled = filled + dot(row.astype(BF), lane, 1, 1)
        for shift in (0, 8, 16):
            byte = ((value >> shift) & 255).astype(F32)
            total = total + (dot((row * byte).astype(BF), lane, 1, 1).astype(jnp.int32) << shift)
        start = start + jnp.sum(member, axis=1, keepdims=True).astype(jnp.int32)
    list_ref[...] = jnp.where(filled > 0.5, total, 2 << 12)
    n_ref[...] = jnp.broadcast_to(start, (8, 128))


def silu(v):
    return v / (1.0 + jnp.exp(-v))


def pack_log(value):
    high = value.astype(BF)
    low = (value - high.astype(F32)).astype(BF)
    return high, low


def mixer_kernel(
    dt_bias,
    a_log,
    skip_gain,
    acc_ref,
    raw_ref,
    conv_weight,
    conv_bias,
    norm_gain,
    w_ref,
    meta_ref,
    w_all,
    normed_all,
    list_ref,
    n_ref,
    chan_ref,
    metas,
    mixed,
    x_ref,
    inner,
    gate_ref,
    rim_out,
    rim_in,
    own_state,
    send0,
    recv0,
    send1,
    recv1,
    logs1,
    send2,
    recv2,
    send3,
    recv3,
    recv4,
    prior,
    rim_sems,
    sems0,
    ssem1,
    rsem1,
    sems2,
    ssem3,
    rsem3,
    sems4,
    meta_sems,
    w_near,
    w_far,
    w_mate,
    w_own,
    n_near,
    n_far,
):
    s = lax.axis_index("seq")
    g = lax.axis_index("head")
    core = s % 2
    y = (s // 2) % 4
    z = s // 8

    def at_y(v):
        return z * 8 + ((y + v) % 4) * 2 + core

    def at_z(v):
        return ((z + v) % 8) * 8 + s % 8

    mate = s + 1 - 2 * core
    after = (s + 1) % 64
    before = (s + 63) % 64
    barrier = pltpu.get_barrier_semaphore()
    partners = [after, before, mate, at_y(1), at_y(2), at_y(3)] + [at_z(v) for v in (1, 2, 4, 6, 7)]
    for partner in partners:
        pl.semaphore_signal(barrier, inc=1, device_id=(partner, g), device_id_type=MESH)
    for v in (1, 2, 3):
        pl.semaphore_signal(barrier, inc=1, device_id=(s, (g + v) % 4), device_id_type=MESH)

    def copy(src, dst, send_sem, recv_sem, to, group=g):
        return pltpu.make_async_remote_copy(
            src_ref=src,
            dst_ref=dst,
            send_sem=send_sem,
            recv_sem=recv_sem,
            device_id=(to, group),
            device_id_type=MESH,
        )

    right, left = (g + 1) % 4, (g + 3) % 4
    far = (g + 2) % 4

    class Ring:
        def __init__(self, near, beyond, view):
            self.near = [
                [copy(view(g, i), view(g, i), near.at[0, w, i], near.at[1, w, i], s, to) for i in range(4)]
                for w, to in ((0, right), (1, left))
            ]
            self.far = [
                copy(view(left, i), view(left, i), beyond.at[0, i], beyond.at[1, i], s, right) for i in (0, 1)
            ] + [copy(view(right, i), view(right, i), beyond.at[0, i], beyond.at[1, i], s, left) for i in (2, 3)]

        def start(self, i):
            self.near[0][i].start()
            self.near[1][3 - i].start()

        def forward(self):
            for i in (0, 1):
                self.near[0][i].wait_recv()
                self.far[i].start()
                self.near[1][3 - i].wait_recv()
                self.far[3 - i].start()

        def arrived(self):
            for i in (2, 3):
                self.near[0][i].wait_recv()
                self.near[1][3 - i].wait_recv()

        def finish(self):
            for c in self.far:
                c.wait_recv()

        def sent(self):
            for c in self.near[0] + self.near[1] + self.far:
                c.wait_send()

    own_mixed = acc_ref[pl.ds(1024, 1280), :].astype(BF)
    mixed[...] = own_mixed.astype(F32)
    row16 = lax.broadcasted_iota(jnp.int32, (16, TOK), 0)
    lane16 = lax.broadcasted_iota(jnp.int32, (16, TOK), 1)
    pick = jnp.where((lane16 == row16 + 125) & (row16 < 3), 1.0, 0.0).astype(BF)
    rim_out[...] = dot(pick, own_mixed, 1, 1).astype(BF)
    share = w_ref.shape[0]
    own_copy = pltpu.make_async_copy(w_ref, w_all.at[g, core], w_own)
    own_copy.start()
    metas[g] = meta_ref[...]
    own_copy.wait()
    pl.semaphore_wait(barrier, len(partners) + 3)
    rim_copy = copy(rim_out, rim_in, rim_sems.at[0], rim_sems.at[1], after)
    rim_copy.start()
    meta_copies = [
        copy(meta_ref, metas.at[g], meta_sems.at[0, v - 1], meta_sems.at[1, v - 1], s, (g + v) % 4) for v in (1, 2, 3)
    ]
    for c in meta_copies:
        c.start()
    w_ring = Ring(w_near, w_far, lambda k, i: w_all.at[k, core, pl.ds(i * share // 4, share // 4)])
    for i in range(4):
        w_ring.start(i)

    def to_mate(k):
        return copy(w_all.at[k, core], w_all.at[k, core], w_mate.at[0, k], w_mate.at[1, k], mate)

    for part in range(10):
        lanes = pl.ds(part * 128, 128)
        gain = norm_gain[lanes].reshape(1, 128) if part < 8 else jnp.zeros((1, 128), F32)
        stacked = [conv_weight[:, lanes], conv_bias[lanes].reshape(1, 128), gain, jnp.zeros((122, 128), F32)]
        chan_ref[lanes, :] = jnp.concatenate(stacked, axis=0).T

    lane = lax.broadcasted_iota(jnp.int32, (TOK, TOK), 1)
    row = lax.broadcasted_iota(jnp.int32, (TOK, TOK), 0)
    bias = jnp.zeros((16, TOK), F32)
    log_rate = jnp.zeros((16, TOK), F32)
    for h in range(16):
        bias = jnp.where(row16 == h, dt_bias[h], bias)
        log_rate = jnp.where(row16 == h, a_log[h], log_rate)
    v = raw_ref[...] + bias
    step = jnp.maximum(v, 0.0) + jnp.log1p(jnp.exp(-jnp.abs(v)))
    rate = -jnp.exp(log_rate)
    pace = step * rate
    causal = row <= lane
    running = dot(pace, jnp.where(causal, 1.0, 0.0), precision=lax.Precision.HIGHEST)
    total = dot(pace, jnp.ones((TOK, TOK), F32), precision=lax.Precision.HIGHEST)
    tail = jnp.exp(total - running) * step
    lead = jnp.exp(running)
    columns = jnp.concatenate([running, step, jnp.zeros((96, TOK), F32)], axis=0).T
    gate_ref[...] = silu(acc_ref[pl.ds(0, 1024), :].astype(BF).astype(F32))

    rim_copy.wait_recv()
    keep = jnp.where(s > 0, 1.0, 0.0)
    place = jnp.where((lane16 == row16 + 125) & (row16 < 3), keep, 0.0).astype(BF)
    b_t = None
    c_t = None
    for part in range(10):
        rows = pl.ds(part * 128, 128)
        own = mixed[rows, :]
        rim = dot(rim_in[:, rows], place, 0, 0)
        total_v = jnp.broadcast_to(chan_ref[rows, 4:5], (128, TOK))
        for tap in range(4):
            shift = 3 - tap
            if shift:
                moved = pltpu.roll(jnp.where(lane >= TOK - shift, rim, own), shift, 1)
            else:
                moved = own
            total_v = total_v + chan_ref[rows, tap : tap + 1] * moved
        active = silu(total_v).astype(BF)
        if part < 8:
            x_ref[rows, :] = active
            for k in range(2):
                h = part * 2 + k
                piece = active[k * 64 : k * 64 + 64, :].astype(F32)
                send0[pl.ds(h * 64, 64), :] = (piece * tail[h : h + 1, :]).astype(BF)
        elif part == 8:
            b_t = active
        else:
            c_t = active
    own_state[...] = dot(send0[pl.ds(0, 1024), :], b_t, 1, 1)

    send0[pl.ds(0, 1024), :] = own_state[...].astype(BF)
    high, low = pack_log(total)
    send0[pl.ds(1024, 16), :] = high
    send0[pl.ds(1040, 16), :] = low
    copy0 = copy(send0, recv0, sems0.at[0], sems0.at[1], mate)
    copy0.start()
    own_mate = to_mate(g)
    own_mate.start()

    scores = dot(b_t, c_t, 0, 0)

    def inner_heads(first, last):
        for h in range(first, last):
            gap = running[h : h + 1, :] - columns[:, h : h + 1]
            factor = jnp.exp(jnp.where(causal, gap, -jnp.inf))
            weights = (scores * factor * columns[:, 16 + h : 17 + h]).astype(BF)
            rows = pl.ds(h * 64, 64)
            xh = x_ref[rows, :]
            inner[rows, :] = dot(xh, weights) + skip_gain[h] * xh.astype(F32)

    inner_heads(0, 4)
    copy0.wait_recv()
    mate_log = recv0[pl.ds(1024, 16), :].astype(F32) + recv0[pl.ds(1040, 16), :].astype(F32)
    is_first = core == 0
    own_by = jnp.where(is_first, jnp.exp(mate_log), 1.0)
    mate_by = jnp.where(is_first, 1.0, jnp.exp(total))
    chip_log = total + mate_log
    high, low = pack_log(chip_log)
    logs1[4] = own_by
    logs1[5] = mate_by
    for j in range(4):
        for k in range(2):
            h = core * 8 + j * 2 + k
            rows = pl.ds(pl.multiple_of(h * 64, 64), 64)
            chip_state = logs1[4, pl.ds(h, 1), :] * own_state[rows, :] + logs1[5, pl.ds(h, 1), :] * recv0[
                rows, :
            ].astype(F32)
            send1[j, pl.ds(k * 64, 64), :] = chip_state.astype(BF)
        send1[j, pl.ds(128, 16), :] = high
        send1[j, pl.ds(144, 16), :] = low
    copies1 = []
    for v in range(1, 4):
        to = (y + v) % 4
        c = copy(send1.at[to], recv1.at[y], ssem1.at[v - 1], rsem1.at[v - 1], at_y(v))
        c.start()
        copies1.append(c)
    recv1[y] = send1[y]
    inner_heads(4, 6)
    for c in copies1:
        c.wait_recv()
    rows_log = []
    states = []
    first_head = core * 8 + y * 2
    for j in range(4):
        logs1[j] = recv1[j, pl.ds(128, 16), :].astype(F32) + recv1[j, pl.ds(144, 16), :].astype(F32)
        pair = [logs1[j, pl.ds(first_head + k, 1), :] for k in range(2)]
        rows_log.append(jnp.concatenate([jnp.broadcast_to(p, (64, TOK)) for p in pair], axis=0))
        states.append(recv1[j, pl.ds(0, 128), :].astype(F32))
    window = states[0]
    window_log = rows_log[0]
    for j in range(1, 4):
        window = jnp.exp(rows_log[j]) * window + states[j]
        window_log = window_log + rows_log[j]

    entering = jnp.zeros((128, TOK), F32)
    entering_log = jnp.zeros((128, TOK), F32)
    copies2 = []
    for i, distance in enumerate((1, 2, 4)):
        high, low = pack_log(window_log)
        send2[i, pl.ds(0, 128), :] = window.astype(BF)
        for k in range(2):
            send2[i, pl.ds(128 + 32 * k, 16), :] = high[64 * k : 64 * k + 16, :]
            send2[i, pl.ds(144 + 32 * k, 16), :] = low[64 * k : 64 * k + 16, :]
        c = copy(send2.at[i], recv2.at[i], sems2.at[0, i], sems2.at[1, i], at_z(distance))
        c.start()
        copies2.append(c)
        inner_heads(6 + 3 * i, 9 + 3 * i)
        c.wait_recv()
        if i == 1:
            w_ring.forward()
            w_ring.arrived()
            mates = [to_mate(left), to_mate(right)]
            for m in mates:
                m.start()
        valid = z >= distance
        came = jnp.where(valid, recv2[i, pl.ds(0, 128), :].astype(F32), 0.0)
        came_log = []
        for k in range(2):
            part = recv2[i, pl.ds(128 + 32 * k, 16), :].astype(F32) + recv2[
                i, pl.ds(144 + 32 * k, 16), :
            ].astype(F32)
            came_log += [part] * 4
        came_log = jnp.where(valid, jnp.concatenate(came_log, axis=0), 0.0)
        entering = jnp.exp(entering_log) * came + entering
        entering_log = entering_log + came_log
        if distance < 4:
            window = jnp.exp(window_log) * came + window
            window_log = window_log + came_log

    for j in range(4):
        send3[j] = entering.astype(BF)
        if j < 3:
            entering = jnp.exp(rows_log[j]) * entering + states[j]
    copies3 = []
    for v in range(1, 4):
        to = (y + v) % 4
        c = copy(send3.at[to], recv3.at[y], ssem3.at[v - 1], rsem3.at[v - 1], at_y(v))
        c.start()
        copies3.append(c)
    recv3[y] = send3[y]
    inner_heads(15, 16)
    for c in meta_copies:
        c.wait_recv()
    list_for(metas, g, list_ref, n_ref)
    w_ring.finish()
    mates.append(to_mate(far))
    mates[-1].start()
    for c in copies3:
        c.wait_recv()
    copy4 = copy(recv3, recv4, sems4.at[0], sems4.at[1], mate)
    copy4.start()
    logs1[4] = jnp.where(is_first, 1.0, jnp.exp(mate_log))
    with_state = jnp.where(is_first, 0.0, 1.0)

    def to_prior(half, source):
        for j in range(4):
            for k in range(2):
                h = half * 8 + j * 2 + k
                rows = pl.ds(pl.multiple_of(h * 64, 64), 64)
                value = source[j, pl.ds(k * 64, 64), :].astype(F32)
                value = logs1[4, pl.ds(h, 1), :] * value + with_state * recv0[rows, :].astype(F32)
                prior[rows, :] = value.astype(BF)

    to_prior(core, recv3)
    copy4.wait_recv()
    to_prior(1 - core, recv4)

    squares = jnp.zeros((8, TOK), F32)
    for h in range(16):
        rows = pl.ds(h * 64, 64)
        carried = dot(prior[rows, :], c_t) * lead[h : h + 1, :]
        gated = (inner[rows, :] + carried) * gate_ref[rows, :]
        inner[rows, :] = gated
        squares = squares + jnp.sum((gated * gated).reshape(8, 8, TOK), axis=0)
    mean = jnp.sum(squares, axis=0, keepdims=True) * (1.0 / 1024.0)
    scale = lax.rsqrt(mean + EPS)
    order = block_order(64)
    ring = Ring(n_near, n_far, lambda k, i: normed_all.at[k, pl.ds(i * 256, 256)])
    for part in (0, 3, 1, 2):
        for h in range(4 * part, 4 * part + 4):
            rows = pl.ds(h * 64, 64)
            normed = (inner[rows, :] * scale * chan_ref[rows, 5:6]).astype(BF)
            normed_all[g, rows, :] = dot(order, normed).astype(BF)
        if part == 3:
            ring.start(0)
        if part == 2:
            for i in range(1, 4):
                ring.start(i)
    ring.forward()
    rim_copy.wait_send()
    copy0.wait_send()
    copy4.wait_send()
    for c in copies1 + copies2 + copies3 + meta_copies:
        c.wait_send()
    w_ring.sent()
    for c in [own_mate] + mates:
        c.wait()
    ring.arrived()
    ring.finish()
    ring.sent()


def mixer(dt_bias, a_log, skip_gain, acc, raw, conv_weight, conv_bias, norm_gain, w_half, meta):
    dma = pltpu.SemaphoreType.DMA
    return pl.pallas_call(
        mixer_kernel,
        out_shape=[
            sds((4, 2) + w_half.shape, BF),
            sds((4, 1024, TOK), BF),
            sds((8, 128), jnp.int32),
            sds((8, 128), jnp.int32),
        ],
        in_specs=[SMEM] * 3 + [VMEM] * 7,
        out_specs=[VMEM] * 4,
        scratch_shapes=[
            pltpu.VMEM((1280, TOK), F32),
            pltpu.VMEM((4, 8, 128), jnp.int32),
            pltpu.VMEM((1280, TOK), F32),
            pltpu.VMEM((1024, TOK), BF),
            pltpu.VMEM((1024, TOK), F32),
            pltpu.VMEM((1024, TOK), F32),
            pltpu.VMEM((16, 1280), BF),
            pltpu.VMEM((16, 1280), BF),
            pltpu.VMEM((1024, TOK), F32),
            pltpu.VMEM((1056, TOK), BF),
            pltpu.VMEM((1056, TOK), BF),
            pltpu.VMEM((4, 160, TOK), BF),
            pltpu.VMEM((4, 160, TOK), BF),
            pltpu.VMEM((6, 16, TOK), F32),
            pltpu.VMEM((3, 192, TOK), BF),
            pltpu.VMEM((3, 192, TOK), BF),
            pltpu.VMEM((4, 128, TOK), BF),
            pltpu.VMEM((4, 128, TOK), BF),
            pltpu.VMEM((4, 128, TOK), BF),
            pltpu.VMEM((1024, TOK), BF),
            dma((2,)),
            dma((2,)),
            dma((3,)),
            dma((3,)),
            dma((2, 3)),
            dma((3,)),
            dma((3,)),
            dma((2,)),
            dma((2, 3)),
            dma((2, 2, 4)),
            dma((2, 4)),
            dma((2, 4)),
            dma,
            dma((2, 2, 4)),
            dma((2, 4)),
        ],
        compiler_params=pltpu.CompilerParams(
            collective_id=0, has_side_effects=True, vmem_limit_bytes=32 * 1024 * 1024
        ),
        cost_estimate=pl.CostEstimate(flops=1000000000, bytes_accessed=8000000, transcendentals=0),
    )(dt_bias, a_log, skip_gain, acc, raw, conv_weight, conv_bias, norm_gain, w_half, meta)


def turned(value, steps):
    count = lax.axis_size("head")
    return lax.ppermute(value, "head", [(i, (i + steps) % count) for i in range(count)])


def per_device(
    tokens,
    in_blocks,
    in_rows,
    in_cols,
    in_count,
    dt_weight,
    dt_bias,
    a_log,
    conv_weight,
    conv_bias,
    skip_gain,
    norm_gain,
    out_blocks,
    out_rows,
    out_cols,
    out_count,
):
    x = turn(tokens)
    from_left = turned(x, 1)
    from_right = turned(x, -1)
    in_list, in_n, w_in, w_half, dt_weight, meta = prepare(
        in_blocks, in_rows, in_cols, in_count, out_blocks, out_rows, out_cols, out_count, dt_weight
    )
    common = (in_list, in_n, w_in, dt_weight)
    acc = in_projection(*common, [x], [0], cost=2)
    opposite_a = turned(from_left[:1024], 1)
    opposite_b = turned(from_right[1024:], -1)
    acc = in_projection(*common, [from_left, from_right], [3, 1], acc=acc, cost=2)
    acc, raw = in_projection(*common, [opposite_a, opposite_b], [2], acc=acc, halves=True)
    w_all, normed, out_list, out_n = mixer(
        dt_bias, a_log, skip_gain, acc, raw, conv_weight, conv_bias, norm_gain, w_half, meta
    )
    return out_projection(out_list, out_n, w_all.reshape(-1, BLOCK, 2 * BLOCK), normed.reshape(-1, TOK))


def solution(mesh):
    return jax.shard_map(
        per_device,
        mesh=mesh,
        in_specs=(
            P("seq", "head"),
            P("head", None),
            P("head"),
            P("head"),
            P("head"),
            P("head", None),
            P("head"),
            P("head"),
            P(None, "head"),
            P("head"),
            P("head"),
            P("head"),
            P("head", None),
            P("head"),
            P("head"),
            P("head"),
        ),
        out_specs=P("seq", "head"),
        check_vma=False,
    )
```

```python
import functools

import jax
import jax.numpy as jnp
from jax import lax
from jax.experimental import pallas as pl
from jax.experimental.pallas import tpu as pltpu
from jax.sharding import PartitionSpec as P

MESH = pl.DeviceIdType.MESH
BF = jnp.bfloat16
F32 = jnp.float32
BLOCK = 64
TOK = 128
UNROLL = 8
EPS = 1e-05
VMEM = pl.BlockSpec(memory_space=pltpu.VMEM)
SMEM = pl.BlockSpec(memory_space=pltpu.SMEM)


def sds(shape, dtype):
    return jax.ShapeDtypeStruct(shape, dtype)


def dot(a, b, ca=1, cb=0, precision=None):
    return lax.dot_general(
        a, b, (((ca,), (cb,)), ((), ())), preferred_element_type=F32, precision=precision
    )


def block_order(size):
    place = lax.broadcasted_iota(jnp.int32, (size, size), 0)
    feature = lax.broadcasted_iota(jnp.int32, (size, size), 1)
    source = (place & ~63) + 2 * (place & 31) + ((place >> 5) & 1)
    return jnp.where(feature == source, 1.0, 0.0).astype(BF)


def turn(x, turned_ref):
    order = block_order(128)
    for i in range(x.shape[1] // 128):
        rows = pl.ds(128 * i, 128)
        turned_ref[rows, :] = dot(order, x[:, 128 * i : 128 * i + 128], 1, 1).astype(BF)


def to_tiles(src, dst, unroll=1):
    lane = lax.broadcasted_iota(jnp.int32, (64, 128), 1)
    low = lane < 64

    def sixteen(g, carry):
        v = src[pl.ds(pl.multiple_of(g * 16, 16), 16), :].astype(F32)
        for s0 in (0, 8):
            t = jnp.swapaxes(jnp.stack([v[s0 : s0 + 8, 128 * j : 128 * j + 128] for j in range(32)], axis=0), 0, 1)
            for i in (0, 4):
                m = t[i : i + 4].reshape(128, 128).astype(BF).T.astype(F32)
                even, odd = m[:64], m[64:]
                k = g * 8 + (s0 + i) // 2
                dst[k] = jnp.where(low, even, pltpu.roll(odd, 64, 1)).astype(BF)
                dst[k + 1] = jnp.where(low, pltpu.roll(even, 64, 1), odd).astype(BF)
        return carry

    lax.fori_loop(0, src.shape[0] // 16, sixteen, 0, unroll=unroll)


def to_list(quarter, value, count, length, list_ref, n_ref):
    slots = quarter.shape[1]
    lists = list_ref.shape[0]
    live = lax.broadcasted_iota(jnp.int32, (1, slots), 1) < count
    one_of = lambda n, v: lax.broadcasted_iota(jnp.int32, (n, slots), 0) == v
    member = jnp.where(one_of(8, quarter) & live, 1.0, 0.0)
    before = jnp.where(
        lax.broadcasted_iota(jnp.int32, (slots, slots), 0) < lax.broadcasted_iota(jnp.int32, (slots, slots), 1), 1.0, 0.0
    ).astype(BF)
    order = dot(member.astype(BF), before)
    position = quarter * length + jnp.sum(member * order, axis=0, keepdims=True).astype(jnp.int32)
    row = jnp.where(one_of(lists, position >> 7) & live, 1.0, 0.0)
    lane = jnp.where(one_of(128, position & 127), 1.0, 0.0).astype(BF)
    filled = dot(row.astype(BF), lane, 1, 1)
    total = jnp.zeros((lists, 128), jnp.int32)
    for shift in (0, 8, 16):
        byte = ((value >> shift) & 255).astype(F32)
        total = total + (dot((row * byte).astype(BF), lane, 1, 1).astype(jnp.int32) << shift)
    list_ref[...] = jnp.where(filled > 0.5, total, 2 << 12)
    n_ref[...] = jnp.broadcast_to(jnp.sum(member, axis=1, keepdims=True), (8, 128)).astype(jnp.int32)


def prepare_kernel(
    in_count, out_count, in_rows, in_cols, out_rows, out_cols, in_blocks, out_blocks,
    in_list, in_n, w_in, w_out, meta, in_held, out_held, sems,
):
    core = lax.axis_index("seq") % 2
    chunk = in_held.shape[0] // 4
    copies = []
    for i in range(4):
        rows = pl.ds(i * chunk, chunk)
        copies.append(pltpu.make_async_copy(in_blocks.at[rows], in_held.at[rows], sems.at[i]))
    share = out_held.shape[0]
    rows = pl.ds(pl.multiple_of(core * share, share), share)
    copies.append(pltpu.make_async_copy(out_blocks.at[rows], out_held, sems.at[4]))
    for c in copies:
        c.start()
    slots = in_rows.shape[0]
    k = lax.broadcasted_iota(jnp.int32, (1, slots), 1)
    r = in_rows[...].reshape(1, slots)
    value = ((k >> 1) << 14) + ((k & 1) << 12) + ((r & 31) << 6) + in_cols[...].reshape(1, slots)
    to_list(r >> 5, value, in_count[0], slots + UNROLL, in_list, in_n)
    slots = out_rows.shape[0]
    meta[0:1, :] = out_rows[...].reshape(1, slots)
    meta[1:2, :] = out_cols[...].reshape(1, slots)
    meta[2:8, :] = jnp.broadcast_to(out_count[0], (6, slots))
    for i in range(4):
        copies[i].wait()
        to_tiles(in_held.at[pl.ds(i * chunk, chunk)], w_in.at[pl.ds(i * chunk // 2, chunk // 2)], 2)
    copies[4].wait()
    to_tiles(out_held, w_out, 2)


def prepare(in_blocks, in_rows, in_cols, in_count, out_blocks, out_rows, out_cols, out_count):
    a, b = in_rows.shape[0], out_rows.shape[0]
    anywhere = pl.BlockSpec(memory_space=pl.ANY)
    return pl.pallas_call(
        prepare_kernel,
        out_shape=[
            sds((16, 128), jnp.int32),
            sds((8, 128), jnp.int32),
            sds((a // 2, BLOCK, 2 * BLOCK), BF),
            sds((b // 4, BLOCK, 2 * BLOCK), BF),
            sds((8, 128), jnp.int32),
        ],
        in_specs=[SMEM] * 2 + [VMEM] * 4 + [anywhere] * 2,
        out_specs=[VMEM] * 5,
        scratch_shapes=[
            pltpu.VMEM(in_blocks.shape, BF),
            pltpu.VMEM((b // 2, out_blocks.shape[1]), BF),
            pltpu.SemaphoreType.DMA((5,)),
        ],
        compiler_params=pltpu.CompilerParams(vmem_limit_bytes=58 * 1024 * 1024),
        cost_estimate=pl.CostEstimate(flops=1000000000, bytes_accessed=12000000, transcendentals=0),
    )(in_count, out_count, in_rows, in_cols, out_rows, out_cols, in_blocks, out_blocks)


def fill_mask(mask):
    half = (lax.broadcasted_iota(jnp.int32, (BLOCK, 2 * BLOCK), 1) >> 5) & 1
    for k in range(3):
        mask[k] = jnp.where(half == k, 1.0, 0.0).astype(BF)


def accumulate(x_ref, w_ref, mask_ref, list_ref, base, count, acc_ref):
    def turn(i, carry):
        parts = []
        for u in range(UNROLL):
            at = base + i * UNROLL + u
            e = list_ref[at >> 7, at & 127]
            r = pl.multiple_of(((e >> 6) & 63) * BLOCK, BLOCK)
            c = pl.multiple_of((e & 63) * BLOCK, BLOCK)
            w = w_ref[e >> 14] * mask_ref[(e >> 12) & 3]
            even = x_ref[pl.ds(r, BLOCK // 2), :]
            odd = x_ref[pl.ds(r + BLOCK // 2, BLOCK // 2), :]
            parts.append((c, dot(w, jnp.concatenate([even, even, odd, odd], axis=0))))
        for c, product in parts:
            acc_ref[pl.ds(c, BLOCK), :] += product
        return carry

    lax.fori_loop(0, (count + UNROLL - 1) // UNROLL, turn, 0)


def in_kernel(offsets, halves, first, list_ref, n_ref, w_ref, dt_ref, *rest):
    x_refs = rest[: len(offsets) * (2 if halves else 1)]
    rest = rest[len(x_refs) :]
    mask = rest[-1]
    fill_mask(mask)
    if first:
        acc_ref, raw_ref = rest[:2]
        acc_ref[...] = jnp.zeros_like(acc_ref)
        raw_ref[...] = jnp.zeros_like(raw_ref)
    else:
        acc_in, raw_in, acc_ref, raw_ref = rest[:4]
        acc_ref[...] = acc_in[...]
        raw_ref[...] = raw_in[...]
    in_len = 2 * w_ref.shape[0] + UNROLL
    xt = rest[-2]
    xs = [x_ref[...] for x_ref in x_refs]
    if halves:
        xs = [jnp.concatenate(xs, axis=0)]
    for x, offset in zip(xs, offsets):
        turn(x, xt)
        q = (lax.axis_index("head") + offset) % 4
        columns = pl.ds(pl.multiple_of(q * 2048, 2048), 2048)
        raw_ref[...] += dot(dt_ref[:, columns], x, 1, 1)
        accumulate(xt, w_ref, mask, list_ref, q * in_len, n_ref[q, 0], acc_ref)


def in_projection(in_list, in_n, w, dt_weight, xs, offsets, acc=None, halves=False, cost=1):
    first = acc is None
    width = 2304
    previous = () if first else acc
    mask = pltpu.VMEM((3, BLOCK, 2 * BLOCK), BF)
    return pl.pallas_call(
        functools.partial(in_kernel, offsets, halves, first),
        out_shape=[sds((width, TOK), F32), sds((16, TOK), F32)],
        in_specs=[SMEM] * 2 + [VMEM] * (2 + len(xs) + len(previous)),
        out_specs=[VMEM] * 2,
        scratch_shapes=[pltpu.VMEM((2048, TOK), BF), mask],
        compiler_params=pltpu.CompilerParams(vmem_limit_bytes=32 * 1024 * 1024),
        cost_estimate=pl.CostEstimate(flops=cost * 1000000000, bytes_accessed=cost * 8000000, transcendentals=0),
    )(in_list, in_n, w, dt_weight, *xs, *previous)


def out_kernel(list_ref, n_ref, w_ref, x_ref, out_ref, acc, mask):
    fill_mask(mask)
    acc[...] = jnp.zeros_like(acc)
    accumulate(x_ref, w_ref, mask, list_ref, 0, n_ref[0, 0], acc)
    for i in range(acc.shape[0] // 128):
        rows = pl.ds(128 * i, 128)
        out_ref[:, rows] = acc[rows, :].T.astype(BF)


def out_projection(out_list, out_n, w, normed):
    return pl.pallas_call(
        out_kernel,
        out_shape=sds((TOK, 2048), BF),
        in_specs=[SMEM] * 2 + [VMEM] * 2,
        out_specs=VMEM,
        scratch_shapes=[pltpu.VMEM((2048, TOK), F32), pltpu.VMEM((3, BLOCK, 2 * BLOCK), BF)],
        compiler_params=pltpu.CompilerParams(vmem_limit_bytes=32 * 1024 * 1024),
        cost_estimate=pl.CostEstimate(flops=1000000000, bytes_accessed=8000000, transcendentals=0),
    )(out_list, out_n, w, normed)


def list_for(metas, mine, list_ref, n_ref):
    before = jnp.where(
        lax.broadcasted_iota(jnp.int32, (128, 128), 0) < lax.broadcasted_iota(jnp.int32, (128, 128), 1), 1.0, 0.0
    ).astype(BF)
    k = lax.broadcasted_iota(jnp.int32, (1, 128), 1)
    lists = list_ref.shape[0]
    rows_of = lax.broadcasted_iota(jnp.int32, (lists, 128), 0)
    lanes_of = lax.broadcasted_iota(jnp.int32, (128, 128), 0)
    start = jnp.zeros((1, 1), jnp.int32)
    filled = jnp.zeros((lists, 128), F32)
    total = jnp.zeros((lists, 128), jnp.int32)
    for g in range(4):
        rows, cols, count = metas[g, 0:1, :], metas[g, 1:2, :], metas[g, 2:3, :]
        live = (k < count) & ((cols >> 5) == mine)
        member = jnp.where(live, 1.0, 0.0)
        order = dot(jnp.broadcast_to(member, (16, 128)).astype(BF), before)[0:1, :]
        position = order.astype(jnp.int32) + start
        value = ((g * 64 + (k >> 1)) << 14) + ((k & 1) << 12) + ((g * 16 + rows) << 6) + (cols & 31)
        row = jnp.where((rows_of == (position >> 7)) & live, 1.0, 0.0)
        lane = jnp.where(lanes_of == (position & 127), 1.0, 0.0).astype(BF)
        filled = filled + dot(row.astype(BF), lane, 1, 1)
        for shift in (0, 8, 16):
            byte = ((value >> shift) & 255).astype(F32)
            total = total + (dot((row * byte).astype(BF), lane, 1, 1).astype(jnp.int32) << shift)
        start = start + jnp.sum(member, axis=1, keepdims=True).astype(jnp.int32)
    list_ref[...] = jnp.where(filled > 0.5, total, 2 << 12)
    n_ref[...] = jnp.broadcast_to(start, (8, 128))


def silu(v):
    return v / (1.0 + jnp.exp(-v))


def mixer_kernel(
    dt_bias,
    a_log,
    skip_gain,
    acc_ref,
    raw_ref,
    conv_weight,
    conv_bias,
    norm_gain,
    w_ref,
    meta_ref,
    w_all,
    normed_all,
    list_ref,
    n_ref,
    chan_ref,
    metas,
    mixed,
    x_ref,
    inner,
    gate_ref,
    rim_out,
    rim_in,
    own_state,
    send0,
    recv0,
    send1,
    recv1,
    send3,
    recv3,
    recv4,
    prior,
    own_log,
    mate_log,
    chip_log,
    logs,
    factors,
    rim_sems,
    sems0,
    log_sems,
    all_sems,
    sems4,
    meta_sems,
    w_near,
    w_far,
    w_mate,
    w_own,
    n_near,
    n_far,
):
    s = lax.axis_index("seq")
    g = lax.axis_index("head")
    core = s % 2
    chip = s // 2
    mate = s + 1 - 2 * core
    after = (s + 1) % 64
    before = (s + 63) % 64
    barrier = pltpu.get_barrier_semaphore()

    def greet(i, carry):
        pl.semaphore_signal(barrier, inc=1, device_id=((s + 2 * i) % 64, g), device_id_type=MESH)
        return carry

    lax.fori_loop(1, 32, greet, 0)
    for partner in (after, before, mate):
        pl.semaphore_signal(barrier, inc=1, device_id=(partner, g), device_id_type=MESH)
    for v in (1, 2, 3):
        pl.semaphore_signal(barrier, inc=1, device_id=(s, (g + v) % 4), device_id_type=MESH)

    def copy(src, dst, send_sem, recv_sem, to, group=g):
        return pltpu.make_async_remote_copy(
            src_ref=src,
            dst_ref=dst,
            send_sem=send_sem,
            recv_sem=recv_sem,
            device_id=(to, group),
            device_id_type=MESH,
        )

    def to_chips(source, target, k):
        def one(i, carry):
            copy(source(i), target.at[i - 1], all_sems.at[0, k], all_sems.at[1, k], (s + 2 * i) % 64).start()
            return carry

        lax.fori_loop(1, 32, one, 0)

    def from_chips(target, k):
        return copy(target.at[pl.ds(0, 31)], target.at[pl.ds(0, 31)], all_sems.at[0, k], all_sems.at[1, k], mate)

    def place_of(j):
        return (chip + 31 - j) % 32

    right, left = (g + 1) % 4, (g + 3) % 4
    far = (g + 2) % 4

    class Ring:
        def __init__(self, near, beyond, view):
            self.near = [
                [copy(view(g, i), view(g, i), near.at[0, w, i], near.at[1, w, i], s, to) for i in range(4)]
                for w, to in ((0, right), (1, left))
            ]
            self.far = [
                copy(view(left, i), view(left, i), beyond.at[0, i], beyond.at[1, i], s, right) for i in (0, 1)
            ] + [copy(view(right, i), view(right, i), beyond.at[0, i], beyond.at[1, i], s, left) for i in (2, 3)]

        def start(self, i):
            self.near[0][i].start()
            self.near[1][3 - i].start()

        def forward(self):
            for i in (0, 1):
                self.near[0][i].wait_recv()
                self.far[i].start()
                self.near[1][3 - i].wait_recv()
                self.far[3 - i].start()

        def arrived(self):
            for i in (2, 3):
                self.near[0][i].wait_recv()
                self.near[1][3 - i].wait_recv()

        def finish(self):
            for c in self.far:
                c.wait_recv()

        def sent(self):
            for c in self.near[0] + self.near[1] + self.far:
                c.wait_send()

    own_mixed = acc_ref[pl.ds(1024, 1280), :].astype(BF)
    mixed[...] = own_mixed.astype(F32)
    row16 = lax.broadcasted_iota(jnp.int32, (16, TOK), 0)
    lane16 = lax.broadcasted_iota(jnp.int32, (16, TOK), 1)
    pick = jnp.where((lane16 == row16 + 125) & (row16 < 3), 1.0, 0.0).astype(BF)
    rim_out[...] = dot(pick, own_mixed, 1, 1).astype(BF)
    share = w_ref.shape[0]
    own_copy = pltpu.make_async_copy(w_ref, w_all.at[g, core], w_own)
    own_copy.start()
    metas[g] = meta_ref[...]
    own_copy.wait()
    pl.semaphore_wait(barrier, 37)
    rim_copy = copy(rim_out, rim_in, rim_sems.at[0], rim_sems.at[1], after)
    rim_copy.start()
    meta_copies = [
        copy(meta_ref, metas.at[g], meta_sems.at[0, v - 1], meta_sems.at[1, v - 1], s, (g + v) % 4) for v in (1, 2, 3)
    ]
    for c in meta_copies:
        c.start()
    w_ring = Ring(w_near, w_far, lambda k, i: w_all.at[k, core, pl.ds(i * share // 4, share // 4)])
    for i in range(4):
        w_ring.start(i)

    def to_mate(k):
        return copy(w_all.at[k, core], w_all.at[k, core], w_mate.at[0, k], w_mate.at[1, k], mate)

    lane = lax.broadcasted_iota(jnp.int32, (TOK, TOK), 1)
    row = lax.broadcasted_iota(jnp.int32, (TOK, TOK), 0)
    bias = jnp.zeros((16, TOK), F32)
    log_rate = jnp.zeros((16, TOK), F32)
    for h in range(16):
        bias = jnp.where(row16 == h, dt_bias[h], bias)
        log_rate = jnp.where(row16 == h, a_log[h], log_rate)
    v = raw_ref[...] + bias
    step = jnp.maximum(v, 0.0) + jnp.log1p(jnp.exp(-jnp.abs(v)))
    rate = -jnp.exp(log_rate)
    pace = step * rate
    causal = row <= lane
    running = dot(pace, jnp.where(causal, 1.0, 0.0), precision=lax.Precision.HIGHEST)
    total = dot(pace, jnp.ones((TOK, TOK), F32), precision=lax.Precision.HIGHEST)
    own_log[...] = total
    log_copy = copy(own_log, mate_log, log_sems.at[0], log_sems.at[1], mate)
    log_copy.start()
    for part in range(10):
        lanes = pl.ds(part * 128, 128)
        gain = norm_gain[lanes].reshape(1, 128) if part < 8 else jnp.zeros((1, 128), F32)
        stacked = [conv_weight[:, lanes], conv_bias[lanes].reshape(1, 128), gain, jnp.zeros((122, 128), F32)]
        chan_ref[lanes, :] = jnp.concatenate(stacked, axis=0).T
    tail = jnp.exp(total - running) * step
    lead = jnp.exp(running)
    columns = jnp.concatenate([running, step, jnp.zeros((96, TOK), F32)], axis=0).T
    gate_ref[...] = silu(acc_ref[pl.ds(0, 1024), :].astype(BF).astype(F32))
    log_copy.wait_recv()
    half = pl.ds(pl.multiple_of(core * 8, 8), 8)
    chip_log[...] = own_log[half, :] + mate_log[half, :]
    logs[31] = chip_log[...]
    to_chips(lambda i: chip_log, logs, 0)

    rim_copy.wait_recv()
    keep = jnp.where(s > 0, 1.0, 0.0)
    place = jnp.where((lane16 == row16 + 125) & (row16 < 3), keep, 0.0).astype(BF)
    b_t = None
    c_t = None
    for part in range(10):
        rows = pl.ds(part * 128, 128)
        own = mixed[rows, :]
        rim = dot(rim_in[:, rows], place, 0, 0)
        total_v = jnp.broadcast_to(chan_ref[rows, 4:5], (128, TOK))
        for tap in range(4):
            shift = 3 - tap
            if shift:
                moved = pltpu.roll(jnp.where(lane >= TOK - shift, rim, own), shift, 1)
            else:
                moved = own
            total_v = total_v + chan_ref[rows, tap : tap + 1] * moved
        active = silu(total_v).astype(BF)
        if part < 8:
            x_ref[rows, :] = active
            for k in range(2):
                h = part * 2 + k
                piece = active[k * 64 : k * 64 + 64, :].astype(F32)
                send0[pl.ds(h * 64, 64), :] = (piece * tail[h : h + 1, :]).astype(BF)
        elif part == 8:
            b_t = active
        else:
            c_t = active
    own_state[...] = dot(send0[pl.ds(0, 1024), :], b_t, 1, 1)

    send0[pl.ds(0, 1024), :] = own_state[...].astype(BF)
    copy0 = copy(send0, recv0, sems0.at[0], sems0.at[1], mate)
    copy0.start()
    own_mate = to_mate(g)
    own_mate.start()

    scores = dot(b_t, c_t, 0, 0)

    def inner_heads(first, last):
        for h in range(first, last):
            gap = running[h : h + 1, :] - columns[:, h : h + 1]
            factor = jnp.exp(jnp.where(causal, gap, -jnp.inf))
            weights = (scores * factor * columns[:, 16 + h : 17 + h]).astype(BF)
            rows = pl.ds(h * 64, 64)
            xh = x_ref[rows, :]
            inner[rows, :] = dot(xh, weights) + skip_gain[h] * xh.astype(F32)

    inner_heads(0, 4)
    is_first = core == 0
    factors[0] = jnp.where(is_first, jnp.exp(mate_log[...]), 1.0)
    factors[1] = jnp.where(is_first, 1.0, jnp.exp(total))
    factors[2] = jnp.where(is_first, 1.0, jnp.exp(mate_log[...]))
    copy0.wait_recv()
    for j in range(8):
        h = core * 8 + j
        rows = pl.ds(pl.multiple_of(h * 64, 64), 64)
        both = factors[0, pl.ds(h, 1), :] * own_state[rows, :] + factors[1, pl.ds(h, 1), :] * recv0[rows, :].astype(F32)
        for k in range(4):
            send1[4 * j + k] = both[16 * k : 16 * k + 16, :].astype(BF)
    to_chips(lambda i: send1.at[(chip + i) % 32], recv1, 1)
    recv1[31] = send1[chip]
    inner_heads(4, 11)
    from_chips(logs, 0).wait_recv()
    from_chips(recv1, 1).wait_recv()
    entering = jnp.zeros((16, TOK), F32)
    for j in range(32):
        send3[j] = entering.astype(BF)
        if j < 31:
            place = place_of(j)
            decay = jnp.exp(logs[place, pl.ds(chip // 4, 1), :])
            entering = decay * entering + recv1[place].astype(F32)
    to_chips(lambda i: send3.at[(chip + i) % 32], recv3, 2)
    recv3[31] = send3[chip]
    w_ring.forward()
    w_ring.arrived()
    mates = [to_mate(left), to_mate(right)]
    for m in mates:
        m.start()
    inner_heads(11, 16)
    for c in meta_copies:
        c.wait_recv()
    list_for(metas, g, list_ref, n_ref)
    from_chips(recv3, 2).wait_recv()
    copy4 = copy(recv3, recv4, sems4.at[0], sems4.at[1], mate)
    copy4.start()
    with_state = jnp.where(is_first, 0.0, 1.0)

    def to_prior(half, source):
        for j in range(8):
            h = half * 8 + j
            rows = pl.ds(pl.multiple_of(h * 64, 64), 64)
            parts = [source[place_of(4 * j + k)].astype(F32) for k in range(4)]
            value = factors[2, pl.ds(h, 1), :] * jnp.concatenate(parts, axis=0)
            prior[rows, :] = (value + with_state * recv0[rows, :].astype(F32)).astype(BF)

    to_prior(core, recv3)
    w_ring.finish()
    mates.append(to_mate(far))
    mates[-1].start()
    copy4.wait_recv()
    to_prior(1 - core, recv4)

    squares = jnp.zeros((8, TOK), F32)
    for h in range(16):
        rows = pl.ds(h * 64, 64)
        carried = dot(prior[rows, :], c_t) * lead[h : h + 1, :]
        gated = (inner[rows, :] + carried) * gate_ref[rows, :]
        inner[rows, :] = gated
        squares = squares + jnp.sum((gated * gated).reshape(8, 8, TOK), axis=0)
    mean = jnp.sum(squares, axis=0, keepdims=True) * (1.0 / 1024.0)
    scale = lax.rsqrt(mean + EPS)
    order = block_order(64)
    ring = Ring(n_near, n_far, lambda k, i: normed_all.at[k, pl.ds(i * 256, 256)])
    for part in (0, 3, 1, 2):
        for h in range(4 * part, 4 * part + 4):
            rows = pl.ds(h * 64, 64)
            normed = (inner[rows, :] * scale * chan_ref[rows, 5:6]).astype(BF)
            normed_all[g, rows, :] = dot(order, normed).astype(BF)
        if part == 3:
            ring.start(0)
        if part == 2:
            for i in range(1, 4):
                ring.start(i)
    ring.forward()
    rim_copy.wait_send()
    copy0.wait_send()
    copy4.wait_send()
    log_copy.wait_send()
    from_chips(logs, 0).wait_send()
    from_chips(recv1, 1).wait_send()
    from_chips(recv3, 2).wait_send()
    for c in meta_copies:
        c.wait_send()
    w_ring.sent()
    for c in [own_mate] + mates:
        c.wait()
    ring.arrived()
    ring.finish()
    ring.sent()


def mixer(dt_bias, a_log, skip_gain, acc, raw, conv_weight, conv_bias, norm_gain, w_half, meta):
    dma = pltpu.SemaphoreType.DMA
    return pl.pallas_call(
        mixer_kernel,
        out_shape=[
            sds((4, 2) + w_half.shape, BF),
            sds((4, 1024, TOK), BF),
            sds((8, 128), jnp.int32),
            sds((8, 128), jnp.int32),
        ],
        in_specs=[SMEM] * 3 + [VMEM] * 7,
        out_specs=[VMEM] * 4,
        scratch_shapes=[
            pltpu.VMEM((1280, TOK), F32),
            pltpu.VMEM((4, 8, 128), jnp.int32),
            pltpu.VMEM((1280, TOK), F32),
            pltpu.VMEM((1024, TOK), BF),
            pltpu.VMEM((1024, TOK), F32),
            pltpu.VMEM((1024, TOK), F32),
            pltpu.VMEM((16, 1280), BF),
            pltpu.VMEM((16, 1280), BF),
            pltpu.VMEM((1024, TOK), F32),
            pltpu.VMEM((1024, TOK), BF),
            pltpu.VMEM((1024, TOK), BF),
            pltpu.VMEM((32, 16, TOK), BF),
            pltpu.VMEM((32, 16, TOK), BF),
            pltpu.VMEM((32, 16, TOK), BF),
            pltpu.VMEM((32, 16, TOK), BF),
            pltpu.VMEM((32, 16, TOK), BF),
            pltpu.VMEM((1024, TOK), BF),
            pltpu.VMEM((16, TOK), F32),
            pltpu.VMEM((16, TOK), F32),
            pltpu.VMEM((8, TOK), F32),
            pltpu.VMEM((32, 8, TOK), F32),
            pltpu.VMEM((3, 16, TOK), F32),
            dma((2,)),
            dma((2,)),
            dma((2,)),
            dma((2, 3)),
            dma((2,)),
            dma((2, 3)),
            dma((2, 2, 4)),
            dma((2, 4)),
            dma((2, 4)),
            dma,
            dma((2, 2, 4)),
            dma((2, 4)),
        ],
        compiler_params=pltpu.CompilerParams(
            collective_id=0, has_side_effects=True, vmem_limit_bytes=32 * 1024 * 1024
        ),
        cost_estimate=pl.CostEstimate(flops=1000000000, bytes_accessed=8000000, transcendentals=0),
    )(dt_bias, a_log, skip_gain, acc, raw, conv_weight, conv_bias, norm_gain, w_half, meta)


def turned(value, steps):
    count = lax.axis_size("head")
    return lax.ppermute(value, "head", [(i, (i + steps) % count) for i in range(count)])


def per_device(
    tokens,
    in_blocks,
    in_rows,
    in_cols,
    in_count,
    dt_weight,
    dt_bias,
    a_log,
    conv_weight,
    conv_bias,
    skip_gain,
    norm_gain,
    out_blocks,
    out_rows,
    out_cols,
    out_count,
):
    from_left = turned(tokens, 1)
    from_right = turned(tokens, -1)
    in_list, in_n, w_in, w_half, meta = prepare(
        in_blocks, in_rows, in_cols, in_count, out_blocks, out_rows, out_cols, out_count
    )
    common = (in_list, in_n, w_in, dt_weight)
    acc = in_projection(*common, [tokens], [0], cost=2)
    half = tokens.shape[0] // 2
    opposite_a = turned(from_left[:half], 1)
    opposite_b = turned(from_right[half:], -1)
    acc = in_projection(*common, [from_left, from_right], [3, 1], acc=acc, cost=2)
    acc, raw = in_projection(*common, [opposite_a, opposite_b], [2], acc=acc, halves=True)
    w_all, normed, out_list, out_n = mixer(
        dt_bias, a_log, skip_gain, acc, raw, conv_weight, conv_bias, norm_gain, w_half, meta
    )
    return out_projection(out_list, out_n, w_all.reshape(-1, BLOCK, 2 * BLOCK), normed.reshape(-1, TOK))


def solution(mesh):
    return jax.shard_map(
        per_device,
        mesh=mesh,
        in_specs=(
            P("seq", "head"),
            P("head", None),
            P("head"),
            P("head"),
            P("head"),
            P("head", None),
            P("head"),
            P("head"),
            P(None, "head"),
            P("head"),
            P("head"),
            P("head"),
            P("head", None),
            P("head"),
            P("head"),
            P("head"),
        ),
        out_specs=P("seq", "head"),
        check_vma=False,
    )
```

```python
import functools

import jax
import jax.numpy as jnp
from jax import lax
from jax.experimental import pallas as pl
from jax.experimental.pallas import tpu as pltpu
from jax.sharding import PartitionSpec as P

MESH = pl.DeviceIdType.MESH
BF = jnp.bfloat16
F32 = jnp.float32
BLOCK = 64
TOK = 128
UNROLL = 16
EPS = 1e-05
VMEM = pl.BlockSpec(memory_space=pltpu.VMEM)
SMEM = pl.BlockSpec(memory_space=pltpu.SMEM)
HBM = pl.BlockSpec(memory_space=pltpu.HBM)


def sds(shape, dtype):
    return jax.ShapeDtypeStruct(shape, dtype)


def dot(a, b, ca=1, cb=0, precision=None):
    return lax.dot_general(
        a, b, (((ca,), (cb,)), ((), ())), preferred_element_type=F32, precision=precision
    )


def block_order(size):
    place = lax.broadcasted_iota(jnp.int32, (size, size), 0)
    feature = lax.broadcasted_iota(jnp.int32, (size, size), 1)
    source = (place & ~63) + 2 * (place & 31) + ((place >> 5) & 1)
    return jnp.where(feature == source, 1.0, 0.0).astype(BF)


def turn(x, turned_ref):
    order = block_order(128)
    for i in range(x.shape[1] // 128):
        rows = pl.ds(128 * i, 128)
        turned_ref[rows, :] = dot(order, x[:, 128 * i : 128 * i + 128], 1, 1).astype(BF)


def to_tiles(src, dst, unroll=1):
    lane = lax.broadcasted_iota(jnp.int32, (64, 128), 1)
    low = lane < 64

    def sixteen(g, carry):
        v = src[pl.ds(pl.multiple_of(g * 16, 16), 16), :].astype(F32)
        for s0 in (0, 8):
            t = jnp.swapaxes(jnp.stack([v[s0 : s0 + 8, 128 * j : 128 * j + 128] for j in range(32)], axis=0), 0, 1)
            for i in (0, 4):
                m = t[i : i + 4].reshape(128, 128).astype(BF).T.astype(F32)
                even, odd = m[:64], m[64:]
                k = g * 8 + (s0 + i) // 2
                dst[k] = jnp.where(low, even, pltpu.roll(odd, 64, 1)).astype(BF)
                dst[k + 1] = jnp.where(low, pltpu.roll(even, 64, 1), odd).astype(BF)
        return carry

    lax.fori_loop(0, src.shape[0] // 16, sixteen, 0, unroll=unroll)


def to_list(quarter, value, count, length, list_ref, n_ref):
    slots = quarter.shape[1]
    lists = list_ref.shape[0]
    live = lax.broadcasted_iota(jnp.int32, (1, slots), 1) < count
    one_of = lambda n, v: lax.broadcasted_iota(jnp.int32, (n, slots), 0) == v
    member = jnp.where(one_of(8, quarter) & live, 1.0, 0.0)
    before = jnp.where(
        lax.broadcasted_iota(jnp.int32, (slots, slots), 0) < lax.broadcasted_iota(jnp.int32, (slots, slots), 1), 1.0, 0.0
    ).astype(BF)
    order = dot(member.astype(BF), before)
    position = quarter * length + jnp.sum(member * order, axis=0, keepdims=True).astype(jnp.int32)
    row = jnp.where(one_of(lists, position >> 7) & live, 1.0, 0.0)
    lane = jnp.where(one_of(128, position & 127), 1.0, 0.0).astype(BF)
    filled = dot(row.astype(BF), lane, 1, 1)
    total = jnp.zeros((lists, 128), jnp.int32)
    for shift in (0, 8, 16):
        byte = ((value >> shift) & 255).astype(F32)
        total = total + (dot((row * byte).astype(BF), lane, 1, 1).astype(jnp.int32) << shift)
    list_ref[...] = jnp.where(filled > 0.5, total, 2 << 12)
    n_ref[...] = jnp.broadcast_to(jnp.sum(member, axis=1, keepdims=True), (8, 128)).astype(jnp.int32)


def fill_mask(mask):
    half = (lax.broadcasted_iota(jnp.int32, (BLOCK, 2 * BLOCK), 1) >> 5) & 1
    for k in range(3):
        mask[k] = jnp.where(half == k, 1.0, 0.0).astype(BF)


def accumulate(x_ref, w_ref, mask_ref, list_ref, base, count, acc_ref):
    def turn(i, carry):
        parts = []
        for u in range(UNROLL):
            at = base + i * UNROLL + u
            e = list_ref[at >> 7, at & 127]
            r = pl.multiple_of(((e >> 6) & 63) * BLOCK, BLOCK)
            c = pl.multiple_of((e & 63) * BLOCK, BLOCK)
            w = w_ref[e >> 14] * mask_ref[(e >> 12) & 3]
            even = x_ref[pl.ds(r, BLOCK // 2), :]
            odd = x_ref[pl.ds(r + BLOCK // 2, BLOCK // 2), :]
            parts.append((c, dot(w, jnp.concatenate([even, even, odd, odd], axis=0))))
        for c, product in parts:
            acc_ref[pl.ds(c, BLOCK), :] += product
        return carry

    lax.fori_loop(0, (count + UNROLL - 1) // UNROLL, turn, 0)


def first_kernel(
    in_count, out_count, in_rows, in_cols, out_rows, out_cols, in_blocks, out_blocks, tokens, dt_weight,
    in_list, in_n, w_in, w_out, meta, acc_ref, raw_ref,
    in_held, out_held, x_held, dt_held, xt, mask, rows_in, cols_in, rows_out, cols_out, list_held, n_held, sems,
):
    core = lax.axis_index("seq") % 2
    q = lax.axis_index("head")
    chunk = in_held.shape[0] // 4
    share = out_held.shape[0]
    pairs = [
        (in_rows, rows_in),
        (in_cols, cols_in),
        (out_rows, rows_out),
        (out_cols, cols_out),
    ]
    pairs += [(in_blocks.at[pl.ds(i * chunk, chunk)], in_held.at[pl.ds(i * chunk, chunk)]) for i in range(4)]
    columns = pl.ds(pl.multiple_of(q * 2048, 2048), 2048)
    pairs += [
        (tokens, x_held),
        (dt_weight.at[:, columns], dt_held),
        (out_blocks.at[pl.ds(pl.multiple_of(core * share, share), share)], out_held),
    ]
    copies = [pltpu.make_async_copy(a, b, sems.at[i]) for i, (a, b) in enumerate(pairs)]
    for c in copies:
        c.start()
    fill_mask(mask)
    acc_ref[...] = jnp.zeros_like(acc_ref)
    for c in copies[:4]:
        c.wait()
    slots = in_rows.shape[0]
    k = lax.broadcasted_iota(jnp.int32, (1, slots), 1)
    r = rows_in[...].reshape(1, slots)
    value = ((k >> 1) << 14) + ((k & 1) << 12) + ((r & 31) << 6) + cols_in[...].reshape(1, slots)
    to_list(r >> 5, value, in_count[0], slots + UNROLL, in_list, in_n)
    to_smem = [
        pltpu.make_async_copy(in_list, list_held, sems.at[13]),
        pltpu.make_async_copy(in_n, n_held, sems.at[14]),
    ]
    for c in to_smem:
        c.start()
    slots = out_rows.shape[0]
    meta[0:1, :] = rows_out[...].reshape(1, slots)
    meta[1:2, :] = cols_out[...].reshape(1, slots)
    meta[2:8, :] = jnp.broadcast_to(out_count[0], (6, slots))
    for i in range(4):
        copies[4 + i].wait()
        to_tiles(in_held.at[pl.ds(i * chunk, chunk)], w_in.at[pl.ds(i * chunk // 2, chunk // 2)], 2)
    for c in copies[8:] + to_smem:
        c.wait()
    x = x_held[...]
    turn(x, xt)
    raw_ref[...] = dot(dt_held[...], x, 1, 1)
    in_len = 2 * w_in.shape[0] + UNROLL
    accumulate(xt, w_in, mask, list_held, q * in_len, n_held[q, 0], acc_ref)
    to_tiles(out_held, w_out, 2)


def first_projection(in_blocks, in_rows, in_cols, in_count, out_blocks, out_rows, out_cols, out_count, tokens, dt_weight):
    a, b = in_rows.shape[0], out_rows.shape[0]
    operands = (in_rows, in_cols, out_rows, out_cols, in_blocks, out_blocks, tokens, dt_weight)
    return pl.pallas_call(
        first_kernel,
        out_shape=[
            sds((16, 128), jnp.int32),
            sds((8, 128), jnp.int32),
            sds((a // 2, BLOCK, 2 * BLOCK), BF),
            sds((b // 4, BLOCK, 2 * BLOCK), BF),
            sds((8, 128), jnp.int32),
            sds((2304, TOK), F32),
            sds((16, TOK), F32),
        ],
        in_specs=[SMEM] * 2 + [HBM] * 8,
        out_specs=[VMEM] * 7,
        scratch_shapes=[
            pltpu.VMEM(in_blocks.shape, BF),
            pltpu.VMEM((b // 2, out_blocks.shape[1]), BF),
            pltpu.VMEM(tokens.shape, BF),
            pltpu.VMEM((16, 2048), BF),
            pltpu.VMEM((2048, TOK), BF),
            pltpu.VMEM((3, BLOCK, 2 * BLOCK), BF),
            pltpu.VMEM((a,), jnp.int32),
            pltpu.VMEM((a,), jnp.int32),
            pltpu.VMEM((b,), jnp.int32),
            pltpu.VMEM((b,), jnp.int32),
            pltpu.SMEM((16, 128), jnp.int32),
            pltpu.SMEM((8, 128), jnp.int32),
            pltpu.SemaphoreType.DMA((15,)),
        ],
        compiler_params=pltpu.CompilerParams(vmem_limit_bytes=40 * 1024 * 1024),
        cost_estimate=pl.CostEstimate(flops=8000000000, bytes_accessed=12000000, transcendentals=0),
    )(in_count, out_count, *[pltpu.with_memory_space_constraint(v, pltpu.HBM) for v in operands])


def in_kernel(offsets, halves, list_ref, n_ref, w_ref, dt_ref, *rest):
    x_refs = rest[: len(offsets) * (2 if halves else 1)]
    acc_in, raw_in, acc_ref, raw_ref, xt, mask = rest[len(x_refs) :]
    fill_mask(mask)
    acc_ref[...] = acc_in[...]
    raw_ref[...] = raw_in[...]
    in_len = 2 * w_ref.shape[0] + UNROLL
    xs = [x_ref[...] for x_ref in x_refs]
    if halves:
        xs = [jnp.concatenate(xs, axis=0)]
    for x, offset in zip(xs, offsets):
        turn(x, xt)
        q = (lax.axis_index("head") + offset) % 4
        columns = pl.ds(pl.multiple_of(q * 2048, 2048), 2048)
        raw_ref[...] += dot(dt_ref[:, columns], x, 1, 1)
        accumulate(xt, w_ref, mask, list_ref, q * in_len, n_ref[q, 0], acc_ref)


def in_projection(in_list, in_n, w, dt_weight, xs, offsets, acc, halves=False, cost=1):
    return pl.pallas_call(
        functools.partial(in_kernel, offsets, halves),
        out_shape=[sds((2304, TOK), F32), sds((16, TOK), F32)],
        in_specs=[SMEM] * 2 + [VMEM] * (4 + len(xs)),
        out_specs=[VMEM] * 2,
        scratch_shapes=[pltpu.VMEM((2048, TOK), BF), pltpu.VMEM((3, BLOCK, 2 * BLOCK), BF)],
        compiler_params=pltpu.CompilerParams(vmem_limit_bytes=32 * 1024 * 1024),
        cost_estimate=pl.CostEstimate(flops=cost * 1000000000, bytes_accessed=cost * 8000000, transcendentals=0),
    )(in_list, in_n, w, dt_weight, *xs, *acc)


def out_kernel(list_ref, n_ref, w_ref, x_ref, out_ref, acc, mask):
    fill_mask(mask)
    acc[...] = jnp.zeros_like(acc)
    accumulate(x_ref, w_ref, mask, list_ref, 0, n_ref[0, 0], acc)
    for i in range(acc.shape[0] // 128):
        rows = pl.ds(128 * i, 128)
        out_ref[:, rows] = acc[rows, :].T.astype(BF)


def out_projection(out_list, out_n, w, normed):
    return pl.pallas_call(
        out_kernel,
        out_shape=sds((TOK, 2048), BF),
        in_specs=[SMEM] * 2 + [VMEM] * 2,
        out_specs=VMEM,
        scratch_shapes=[pltpu.VMEM((2048, TOK), F32), pltpu.VMEM((3, BLOCK, 2 * BLOCK), BF)],
        compiler_params=pltpu.CompilerParams(vmem_limit_bytes=32 * 1024 * 1024),
        cost_estimate=pl.CostEstimate(flops=1000000000, bytes_accessed=8000000, transcendentals=0),
    )(out_list, out_n, w, normed)


def list_for(metas, mine, list_ref, n_ref):
    before = jnp.where(
        lax.broadcasted_iota(jnp.int32, (128, 128), 0) < lax.broadcasted_iota(jnp.int32, (128, 128), 1), 1.0, 0.0
    ).astype(BF)
    k = lax.broadcasted_iota(jnp.int32, (1, 128), 1)
    lists = list_ref.shape[0]
    rows_of = lax.broadcasted_iota(jnp.int32, (lists, 128), 0)
    lanes_of = lax.broadcasted_iota(jnp.int32, (128, 128), 0)
    start = jnp.zeros((1, 1), jnp.int32)
    filled = jnp.zeros((lists, 128), F32)
    total = jnp.zeros((lists, 128), jnp.int32)
    for g in range(4):
        rows, cols, count = metas[g, 0:1, :], metas[g, 1:2, :], metas[g, 2:3, :]
        live = (k < count) & ((cols >> 5) == mine)
        member = jnp.where(live, 1.0, 0.0)
        order = dot(jnp.broadcast_to(member, (16, 128)).astype(BF), before)[0:1, :]
        position = order.astype(jnp.int32) + start
        value = ((g * 64 + (k >> 1)) << 14) + ((k & 1) << 12) + ((g * 16 + rows) << 6) + (cols & 31)
        row = jnp.where((rows_of == (position >> 7)) & live, 1.0, 0.0)
        lane = jnp.where(lanes_of == (position & 127), 1.0, 0.0).astype(BF)
        filled = filled + dot(row.astype(BF), lane, 1, 1)
        for shift in (0, 8, 16):
            byte = ((value >> shift) & 255).astype(F32)
            total = total + (dot((row * byte).astype(BF), lane, 1, 1).astype(jnp.int32) << shift)
        start = start + jnp.sum(member, axis=1, keepdims=True).astype(jnp.int32)
    list_ref[...] = jnp.where(filled > 0.5, total, 2 << 12)
    n_ref[...] = jnp.broadcast_to(start, (8, 128))


def silu(v):
    return v / (1.0 + jnp.exp(-v))


def mixer_kernel(
    dt_bias,
    a_log,
    skip_gain,
    acc_ref,
    raw_ref,
    conv_weight,
    conv_bias,
    norm_gain,
    w_ref,
    meta_ref,
    w_all,
    normed_all,
    list_ref,
    n_ref,
    chan_ref,
    metas,
    mixed,
    x_ref,
    inner,
    gate_ref,
    rim_out,
    rim_in,
    own_state,
    send0,
    recv0,
    send1,
    recv1,
    send3,
    recv3,
    recv4,
    prior,
    own_log,
    mate_log,
    chip_log,
    logs,
    factors,
    rim_sems,
    sems0,
    log_sems,
    all_sems,
    sems4,
    meta_sems,
    w_near,
    w_far,
    w_mate,
    w_own,
    n_near,
    n_far,
):
    s = lax.axis_index("seq")
    g = lax.axis_index("head")
    core = s % 2
    chip = s // 2
    mate = s + 1 - 2 * core
    after = (s + 1) % 64
    before = (s + 63) % 64
    barrier = pltpu.get_barrier_semaphore()

    def greet(i, carry):
        pl.semaphore_signal(barrier, inc=1, device_id=(lax.rem(s + 2 * i, 64), g), device_id_type=MESH)
        return carry

    lax.fori_loop(1, 32, greet, 0)
    for partner in (after, before, mate):
        pl.semaphore_signal(barrier, inc=1, device_id=(partner, g), device_id_type=MESH)
    for v in (1, 2, 3):
        pl.semaphore_signal(barrier, inc=1, device_id=(s, (g + v) % 4), device_id_type=MESH)

    def copy(src, dst, send_sem, recv_sem, to, group=g):
        return pltpu.make_async_remote_copy(
            src_ref=src,
            dst_ref=dst,
            send_sem=send_sem,
            recv_sem=recv_sem,
            device_id=(to, group),
            device_id_type=MESH,
        )

    def to_chips(source, target, k):
        def one(i, carry):
            copy(source(i), target.at[i - 1], all_sems.at[0, k], all_sems.at[1, k], lax.rem(s + 2 * i, 64)).start()
            return carry

        lax.fori_loop(1, 32, one, 0)

    def from_chips(target, k):
        return copy(target.at[pl.ds(0, 31)], target.at[pl.ds(0, 31)], all_sems.at[0, k], all_sems.at[1, k], mate)

    def place_of(j):
        return lax.rem(chip + 31 - j, 32)

    right, left = (g + 1) % 4, (g + 3) % 4
    far = (g + 2) % 4

    class Ring:
        def __init__(self, near, beyond, view):
            self.near = [
                [copy(view(g, i), view(g, i), near.at[0, w, i], near.at[1, w, i], s, to) for i in range(4)]
                for w, to in ((0, right), (1, left))
            ]
            self.far = [
                copy(view(left, i), view(left, i), beyond.at[0, i], beyond.at[1, i], s, right) for i in (0, 1)
            ] + [copy(view(right, i), view(right, i), beyond.at[0, i], beyond.at[1, i], s, left) for i in (2, 3)]

        def start(self, i):
            self.near[0][i].start()
            self.near[1][3 - i].start()

        def forward(self):
            for i in (0, 1):
                self.near[0][i].wait_recv()
                self.far[i].start()
                self.near[1][3 - i].wait_recv()
                self.far[3 - i].start()

        def arrived(self):
            for i in (2, 3):
                self.near[0][i].wait_recv()
                self.near[1][3 - i].wait_recv()

        def finish(self):
            for c in self.far:
                c.wait_recv()

        def sent(self):
            for c in self.near[0] + self.near[1] + self.far:
                c.wait_send()

    own_mixed = acc_ref[pl.ds(1024, 1280), :].astype(BF)
    mixed[...] = own_mixed.astype(F32)
    row16 = lax.broadcasted_iota(jnp.int32, (16, TOK), 0)
    lane16 = lax.broadcasted_iota(jnp.int32, (16, TOK), 1)
    pick = jnp.where((lane16 == row16 + 125) & (row16 < 3), 1.0, 0.0).astype(BF)
    rim_out[...] = dot(pick, own_mixed, 1, 1).astype(BF)
    own_copy = pltpu.make_async_copy(w_ref, w_all.at[g, core], w_own)
    own_copy.start()
    lane = lax.broadcasted_iota(jnp.int32, (TOK, TOK), 1)
    row = lax.broadcasted_iota(jnp.int32, (TOK, TOK), 0)
    bias = jnp.zeros((16, TOK), F32)
    log_rate = jnp.zeros((16, TOK), F32)
    for h in range(16):
        bias = jnp.where(row16 == h, dt_bias[h], bias)
        log_rate = jnp.where(row16 == h, a_log[h], log_rate)
    v = raw_ref[...] + bias
    step = jnp.maximum(v, 0.0) + jnp.log1p(jnp.exp(-jnp.abs(v)))
    rate = -jnp.exp(log_rate)
    pace = step * rate
    causal = row <= lane
    running = dot(pace, jnp.where(causal, 1.0, 0.0), precision=lax.Precision.HIGHEST)
    total = dot(pace, jnp.ones((TOK, TOK), F32), precision=lax.Precision.HIGHEST)
    own_log[...] = total
    for part in range(10):
        lanes = pl.ds(part * 128, 128)
        gain = norm_gain[lanes].reshape(1, 128) if part < 8 else jnp.zeros((1, 128), F32)
        stacked = [conv_weight[:, lanes], conv_bias[lanes].reshape(1, 128), gain, jnp.zeros((122, 128), F32)]
        chan_ref[lanes, :] = jnp.concatenate(stacked, axis=0).T
    tail = jnp.exp(total - running) * step
    lead = jnp.exp(running)
    columns = jnp.concatenate([running, step, jnp.zeros((96, TOK), F32)], axis=0).T
    gate_ref[...] = silu(acc_ref[pl.ds(0, 1024), :].astype(BF).astype(F32))
    share = w_ref.shape[0]
    metas[g] = meta_ref[...]
    own_copy.wait()
    pl.semaphore_wait(barrier, 37)
    rim_copy = copy(rim_out, rim_in, rim_sems.at[0], rim_sems.at[1], after)
    rim_copy.start()
    log_copy = copy(own_log, mate_log, log_sems.at[0], log_sems.at[1], mate)
    log_copy.start()
    meta_copies = [
        copy(meta_ref, metas.at[g], meta_sems.at[0, v - 1], meta_sems.at[1, v - 1], s, (g + v) % 4) for v in (1, 2, 3)
    ]
    for c in meta_copies:
        c.start()
    w_ring = Ring(w_near, w_far, lambda k, i: w_all.at[k, core, pl.ds(i * share // 4, share // 4)])
    for i in range(4):
        w_ring.start(i)

    def to_mate(k):
        return copy(w_all.at[k, core], w_all.at[k, core], w_mate.at[0, k], w_mate.at[1, k], mate)

    log_copy.wait_recv()
    half = pl.ds(pl.multiple_of(core * 8, 8), 8)
    chip_log[...] = own_log[half, :] + mate_log[half, :]
    logs[31] = chip_log[...]
    to_chips(lambda i: chip_log, logs, 0)

    rim_copy.wait_recv()
    keep = jnp.where(s > 0, 1.0, 0.0)
    place = jnp.where((lane16 == row16 + 125) & (row16 < 3), keep, 0.0).astype(BF)
    b_t = None
    c_t = None
    for part in range(10):
        rows = pl.ds(part * 128, 128)
        own = mixed[rows, :]
        rim = dot(rim_in[:, rows], place, 0, 0)
        total_v = jnp.broadcast_to(chan_ref[rows, 4:5], (128, TOK))
        for tap in range(4):
            shift = 3 - tap
            if shift:
                moved = pltpu.roll(jnp.where(lane >= TOK - shift, rim, own), shift, 1)
            else:
                moved = own
            total_v = total_v + chan_ref[rows, tap : tap + 1] * moved
        active = silu(total_v).astype(BF)
        if part < 8:
            x_ref[rows, :] = active
            for k in range(2):
                h = part * 2 + k
                piece = active[k * 64 : k * 64 + 64, :].astype(F32)
                send0[pl.ds(h * 64, 64), :] = (piece * tail[h : h + 1, :]).astype(BF)
        elif part == 8:
            b_t = active
        else:
            c_t = active
    own_state[...] = dot(send0[pl.ds(0, 1024), :], b_t, 1, 1)

    send0[pl.ds(0, 1024), :] = own_state[...].astype(BF)
    copy0 = copy(send0, recv0, sems0.at[0], sems0.at[1], mate)
    copy0.start()
    own_mate = to_mate(g)
    own_mate.start()

    scores = dot(b_t, c_t, 0, 0)

    def inner_heads(first, last):
        for h in range(first, last):
            gap = running[h : h + 1, :] - columns[:, h : h + 1]
            factor = jnp.exp(jnp.where(causal, gap, -jnp.inf))
            weights = (scores * factor * columns[:, 16 + h : 17 + h]).astype(BF)
            rows = pl.ds(h * 64, 64)
            xh = x_ref[rows, :]
            inner[rows, :] = dot(xh, weights) + skip_gain[h] * xh.astype(F32)

    inner_heads(0, 4)
    is_first = core == 0
    factors[0] = jnp.where(is_first, jnp.exp(mate_log[...]), 1.0)
    factors[1] = jnp.where(is_first, 1.0, jnp.exp(total))
    factors[2] = jnp.where(is_first, 1.0, jnp.exp(mate_log[...]))
    copy0.wait_recv()
    for j in range(8):
        h = core * 8 + j
        rows = pl.ds(pl.multiple_of(h * 64, 64), 64)
        both = factors[0, pl.ds(h, 1), :] * own_state[rows, :] + factors[1, pl.ds(h, 1), :] * recv0[rows, :].astype(F32)
        for k in range(4):
            send1[4 * j + k] = both[16 * k : 16 * k + 16, :].astype(BF)
    to_chips(lambda i: send1.at[lax.rem(chip + i, 32)], recv1, 1)
    recv1[31] = send1[chip]
    inner_heads(4, 11)
    from_chips(logs, 0).wait_recv()
    from_chips(recv1, 1).wait_recv()
    entering = jnp.zeros((16, TOK), F32)
    for j in range(32):
        send3[j] = entering.astype(BF)
        if j < 31:
            place = place_of(j)
            decay = jnp.exp(logs[place, pl.ds(chip // 4, 1), :])
            entering = decay * entering + recv1[place].astype(F32)
    to_chips(lambda i: send3.at[lax.rem(chip + i, 32)], recv3, 2)
    recv3[31] = send3[chip]
    w_ring.forward()
    w_ring.arrived()
    mates = [to_mate(left), to_mate(right)]
    for m in mates:
        m.start()
    inner_heads(11, 16)
    for c in meta_copies:
        c.wait_recv()
    list_for(metas, g, list_ref, n_ref)
    from_chips(recv3, 2).wait_recv()
    copy4 = copy(recv3, recv4, sems4.at[0], sems4.at[1], mate)
    copy4.start()
    with_state = jnp.where(is_first, 0.0, 1.0)

    def to_prior(half, source):
        for j in range(8):
            h = half * 8 + j
            rows = pl.ds(pl.multiple_of(h * 64, 64), 64)
            parts = [source[place_of(4 * j + k)].astype(F32) for k in range(4)]
            value = factors[2, pl.ds(h, 1), :] * jnp.concatenate(parts, axis=0)
            prior[rows, :] = (value + with_state * recv0[rows, :].astype(F32)).astype(BF)

    to_prior(core, recv3)
    w_ring.finish()
    mates.append(to_mate(far))
    mates[-1].start()
    copy4.wait_recv()
    to_prior(1 - core, recv4)

    squares = jnp.zeros((8, TOK), F32)
    for h in range(16):
        rows = pl.ds(h * 64, 64)
        carried = dot(prior[rows, :], c_t) * lead[h : h + 1, :]
        gated = (inner[rows, :] + carried) * gate_ref[rows, :]
        inner[rows, :] = gated
        squares = squares + jnp.sum((gated * gated).reshape(8, 8, TOK), axis=0)
    mean = jnp.sum(squares, axis=0, keepdims=True) * (1.0 / 1024.0)
    scale = lax.rsqrt(mean + EPS)
    order = block_order(64)
    ring = Ring(n_near, n_far, lambda k, i: normed_all.at[k, pl.ds(i * 256, 256)])
    for part in (0, 3, 1, 2):
        for h in range(4 * part, 4 * part + 4):
            rows = pl.ds(h * 64, 64)
            normed = (inner[rows, :] * scale * chan_ref[rows, 5:6]).astype(BF)
            normed_all[g, rows, :] = dot(order, normed).astype(BF)
        if part == 3:
            ring.start(0)
        if part == 2:
            for i in range(1, 4):
                ring.start(i)
    ring.forward()
    rim_copy.wait_send()
    copy0.wait_send()
    copy4.wait_send()
    log_copy.wait_send()
    from_chips(logs, 0).wait_send()
    from_chips(recv1, 1).wait_send()
    from_chips(recv3, 2).wait_send()
    for c in meta_copies:
        c.wait_send()
    w_ring.sent()
    for c in [own_mate] + mates:
        c.wait()
    ring.arrived()
    ring.finish()
    ring.sent()


def mixer(dt_bias, a_log, skip_gain, acc, raw, conv_weight, conv_bias, norm_gain, w_half, meta):
    dma = pltpu.SemaphoreType.DMA
    return pl.pallas_call(
        mixer_kernel,
        out_shape=[
            sds((4, 2) + w_half.shape, BF),
            sds((4, 1024, TOK), BF),
            sds((8, 128), jnp.int32),
            sds((8, 128), jnp.int32),
        ],
        in_specs=[SMEM] * 3 + [VMEM] * 7,
        out_specs=[VMEM] * 4,
        scratch_shapes=[
            pltpu.VMEM((1280, TOK), F32),
            pltpu.VMEM((4, 8, 128), jnp.int32),
            pltpu.VMEM((1280, TOK), F32),
            pltpu.VMEM((1024, TOK), BF),
            pltpu.VMEM((1024, TOK), F32),
            pltpu.VMEM((1024, TOK), F32),
            pltpu.VMEM((16, 1280), BF),
            pltpu.VMEM((16, 1280), BF),
            pltpu.VMEM((1024, TOK), F32),
            pltpu.VMEM((1024, TOK), BF),
            pltpu.VMEM((1024, TOK), BF),
            pltpu.VMEM((32, 16, TOK), BF),
            pltpu.VMEM((32, 16, TOK), BF),
            pltpu.VMEM((32, 16, TOK), BF),
            pltpu.VMEM((32, 16, TOK), BF),
            pltpu.VMEM((32, 16, TOK), BF),
            pltpu.VMEM((1024, TOK), BF),
            pltpu.VMEM((16, TOK), F32),
            pltpu.VMEM((16, TOK), F32),
            pltpu.VMEM((8, TOK), F32),
            pltpu.VMEM((32, 8, TOK), F32),
            pltpu.VMEM((3, 16, TOK), F32),
            dma((2,)),
            dma((2,)),
            dma((2,)),
            dma((2, 3)),
            dma((2,)),
            dma((2, 3)),
            dma((2, 2, 4)),
            dma((2, 4)),
            dma((2, 4)),
            dma,
            dma((2, 2, 4)),
            dma((2, 4)),
        ],
        compiler_params=pltpu.CompilerParams(
            collective_id=0, has_side_effects=True, vmem_limit_bytes=32 * 1024 * 1024
        ),
        cost_estimate=pl.CostEstimate(flops=1000000000, bytes_accessed=8000000, transcendentals=0),
    )(dt_bias, a_log, skip_gain, acc, raw, conv_weight, conv_bias, norm_gain, w_half, meta)


def turned(value, steps):
    count = lax.axis_size("head")
    return lax.ppermute(value, "head", [(i, (i + steps) % count) for i in range(count)])


def per_device(
    tokens,
    in_blocks,
    in_rows,
    in_cols,
    in_count,
    dt_weight,
    dt_bias,
    a_log,
    conv_weight,
    conv_bias,
    skip_gain,
    norm_gain,
    out_blocks,
    out_rows,
    out_cols,
    out_count,
):
    from_left = turned(tokens, 1)
    from_right = turned(tokens, -1)
    in_list, in_n, w_in, w_half, meta, *acc = first_projection(
        in_blocks, in_rows, in_cols, in_count, out_blocks, out_rows, out_cols, out_count, tokens, dt_weight
    )
    common = (in_list, in_n, w_in, dt_weight)
    half = tokens.shape[0] // 2
    opposite_a = turned(from_left[:half], 1)
    opposite_b = turned(from_right[half:], -1)
    acc = in_projection(*common, [from_left, from_right], [3, 1], acc, cost=20)
    acc, raw = in_projection(*common, [opposite_a, opposite_b], [2], acc, halves=True)
    w_all, normed, out_list, out_n = mixer(
        dt_bias, a_log, skip_gain, acc, raw, conv_weight, conv_bias, norm_gain, w_half, meta
    )
    return out_projection(out_list, out_n, w_all.reshape(-1, BLOCK, 2 * BLOCK), normed.reshape(-1, TOK))


def solution(mesh):
    return jax.shard_map(
        per_device,
        mesh=mesh,
        in_specs=(
            P("seq", "head"),
            P("head", None),
            P("head"),
            P("head"),
            P("head"),
            P("head", None),
            P("head"),
            P("head"),
            P(None, "head"),
            P("head"),
            P("head"),
            P("head"),
            P("head", None),
            P("head"),
            P("head"),
            P("head"),
        ),
        out_specs=P("seq", "head"),
        check_vma=False,
    )
```

```python
import functools

import jax
import jax.numpy as jnp
from jax import lax
from jax.experimental import pallas as pl
from jax.experimental.pallas import tpu as pltpu
from jax.sharding import PartitionSpec as P

MESH = pl.DeviceIdType.MESH
BF = jnp.bfloat16
F32 = jnp.float32
BLOCK = 64
TOK = 128
UNROLL = 16
EPS = 1e-05
VMEM = pl.BlockSpec(memory_space=pltpu.VMEM)
SMEM = pl.BlockSpec(memory_space=pltpu.SMEM)
HBM = pl.BlockSpec(memory_space=pltpu.HBM)


def sds(shape, dtype):
    return jax.ShapeDtypeStruct(shape, dtype)


def dot(a, b, ca=1, cb=0, precision=None):
    return lax.dot_general(
        a, b, (((ca,), (cb,)), ((), ())), preferred_element_type=F32, precision=precision
    )


def block_order(size):
    place = lax.broadcasted_iota(jnp.int32, (size, size), 0)
    feature = lax.broadcasted_iota(jnp.int32, (size, size), 1)
    source = (place & ~63) + 2 * (place & 31) + ((place >> 5) & 1)
    return jnp.where(feature == source, 1.0, 0.0).astype(BF)


def turn(x, turned_ref):
    order = block_order(128)
    for i in range(x.shape[1] // 128):
        rows = pl.ds(128 * i, 128)
        turned_ref[rows, :] = dot(order, x[:, 128 * i : 128 * i + 128], 1, 1).astype(BF)


def to_tiles(src, dst, unroll=1):
    lane = lax.broadcasted_iota(jnp.int32, (64, 128), 1)
    low = lane < 64

    def sixteen(g, carry):
        v = src[pl.ds(pl.multiple_of(g * 16, 16), 16), :].astype(F32)
        for s0 in (0, 8):
            t = jnp.swapaxes(jnp.stack([v[s0 : s0 + 8, 128 * j : 128 * j + 128] for j in range(32)], axis=0), 0, 1)
            for i in (0, 4):
                m = t[i : i + 4].reshape(128, 128).astype(BF).T.astype(F32)
                even, odd = m[:64], m[64:]
                k = g * 8 + (s0 + i) // 2
                dst[k] = jnp.where(low, even, pltpu.roll(odd, 64, 1)).astype(BF)
                dst[k + 1] = jnp.where(low, pltpu.roll(even, 64, 1), odd).astype(BF)
        return carry

    lax.fori_loop(0, src.shape[0] // 16, sixteen, 0, unroll=unroll)


def to_list(quarter, value, count, length, list_ref, n_ref):
    slots = quarter.shape[1]
    lists = list_ref.shape[0]
    live = lax.broadcasted_iota(jnp.int32, (1, slots), 1) < count
    one_of = lambda n, v: lax.broadcasted_iota(jnp.int32, (n, slots), 0) == v
    member = jnp.where(one_of(8, quarter) & live, 1.0, 0.0)
    before = jnp.where(
        lax.broadcasted_iota(jnp.int32, (slots, slots), 0) < lax.broadcasted_iota(jnp.int32, (slots, slots), 1), 1.0, 0.0
    ).astype(BF)
    order = dot(member.astype(BF), before)
    position = quarter * length + jnp.sum(member * order, axis=0, keepdims=True).astype(jnp.int32)
    row = jnp.where(one_of(lists, position >> 7) & live, 1.0, 0.0)
    lane = jnp.where(one_of(128, position & 127), 1.0, 0.0).astype(BF)
    filled = dot(row.astype(BF), lane, 1, 1)
    total = jnp.zeros((lists, 128), jnp.int32)
    for shift in (0, 8, 16):
        byte = ((value >> shift) & 255).astype(F32)
        total = total + (dot((row * byte).astype(BF), lane, 1, 1).astype(jnp.int32) << shift)
    list_ref[...] = jnp.where(filled > 0.5, total, 2 << 12)
    n_ref[...] = jnp.broadcast_to(jnp.sum(member, axis=1, keepdims=True), (8, 128)).astype(jnp.int32)


def fill_mask(mask):
    half = (lax.broadcasted_iota(jnp.int32, (BLOCK, 2 * BLOCK), 1) >> 5) & 1
    for k in range(3):
        mask[k] = jnp.where(half == k, 1.0, 0.0).astype(BF)


def accumulate(x_ref, w_ref, mask_ref, list_ref, base, count, acc_ref, scales=None):
    def turn(i, carry):
        parts = []
        for u in range(UNROLL):
            at = base + i * UNROLL + u
            e = list_ref[at >> 7, at & 127]
            r = pl.multiple_of(((e >> 6) & 63) * BLOCK, BLOCK)
            c = pl.multiple_of((e & 63) * BLOCK, BLOCK)
            w = w_ref[e >> 14] * mask_ref[(e >> 12) & 3]
            even = x_ref[pl.ds(r, BLOCK // 2), :]
            odd = x_ref[pl.ds(r + BLOCK // 2, BLOCK // 2), :]
            product = dot(w, jnp.concatenate([even, even, odd, odd], axis=0))
            if scales is not None:
                product = product * scales[(e >> 10) & 3, 0:1, :]
            parts.append((c, product))
        for c, product in parts:
            acc_ref[pl.ds(c, BLOCK), :] += product
        return carry

    lax.fori_loop(0, (count + UNROLL - 1) // UNROLL, turn, 0)


def first_kernel(
    in_count, out_count, in_rows, in_cols, out_rows, out_cols, in_blocks, out_blocks, tokens, dt_weight,
    in_list, in_n, w_in, w_out, meta, acc_ref, raw_ref,
    in_held, out_held, x_held, dt_held, xt, mask, rows_in, cols_in, rows_out, cols_out, list_held, n_held, sems,
):
    core = lax.axis_index("seq") % 2
    q = lax.axis_index("head")
    chunk = in_held.shape[0] // 4
    share = out_held.shape[0]
    pairs = [
        (in_rows, rows_in),
        (in_cols, cols_in),
        (out_rows, rows_out),
        (out_cols, cols_out),
    ]
    pairs += [(in_blocks.at[pl.ds(i * chunk, chunk)], in_held.at[pl.ds(i * chunk, chunk)]) for i in range(4)]
    columns = pl.ds(pl.multiple_of(q * 2048, 2048), 2048)
    pairs += [
        (tokens, x_held),
        (dt_weight.at[:, columns], dt_held),
        (out_blocks.at[pl.ds(pl.multiple_of(core * share, share), share)], out_held),
    ]
    copies = [pltpu.make_async_copy(a, b, sems.at[i]) for i, (a, b) in enumerate(pairs)]
    for c in copies:
        c.start()
    fill_mask(mask)
    acc_ref[...] = jnp.zeros_like(acc_ref)
    for c in copies[:4]:
        c.wait()
    slots = in_rows.shape[0]
    k = lax.broadcasted_iota(jnp.int32, (1, slots), 1)
    r = rows_in[...].reshape(1, slots)
    value = ((k >> 1) << 14) + ((k & 1) << 12) + ((r & 31) << 6) + cols_in[...].reshape(1, slots)
    to_list(r >> 5, value, in_count[0], slots + UNROLL, in_list, in_n)
    to_smem = [
        pltpu.make_async_copy(in_list, list_held, sems.at[13]),
        pltpu.make_async_copy(in_n, n_held, sems.at[14]),
    ]
    for c in to_smem:
        c.start()
    slots = out_rows.shape[0]
    meta[0:1, :] = rows_out[...].reshape(1, slots)
    meta[1:2, :] = cols_out[...].reshape(1, slots)
    meta[2:8, :] = jnp.broadcast_to(out_count[0], (6, slots))
    for i in range(4):
        copies[4 + i].wait()
        to_tiles(in_held.at[pl.ds(i * chunk, chunk)], w_in.at[pl.ds(i * chunk // 2, chunk // 2)], 2)
    for c in copies[8:] + to_smem:
        c.wait()
    x = x_held[...]
    turn(x, xt)
    raw_ref[...] = dot(dt_held[...], x, 1, 1)
    in_len = 2 * w_in.shape[0] + UNROLL
    accumulate(xt, w_in, mask, list_held, q * in_len, n_held[q, 0], acc_ref)
    to_tiles(out_held, w_out, 2)


def first_projection(in_blocks, in_rows, in_cols, in_count, out_blocks, out_rows, out_cols, out_count, tokens, dt_weight):
    a, b = in_rows.shape[0], out_rows.shape[0]
    operands = (in_rows, in_cols, out_rows, out_cols, in_blocks, out_blocks, tokens, dt_weight)
    return pl.pallas_call(
        first_kernel,
        out_shape=[
            sds((16, 128), jnp.int32),
            sds((8, 128), jnp.int32),
            sds((a // 2, BLOCK, 2 * BLOCK), BF),
            sds((b // 4, BLOCK, 2 * BLOCK), BF),
            sds((8, 128), jnp.int32),
            sds((2304, TOK), F32),
            sds((16, TOK), F32),
        ],
        in_specs=[SMEM] * 2 + [HBM] * 8,
        out_specs=[VMEM] * 7,
        scratch_shapes=[
            pltpu.VMEM(in_blocks.shape, BF),
            pltpu.VMEM((b // 2, out_blocks.shape[1]), BF),
            pltpu.VMEM(tokens.shape, BF),
            pltpu.VMEM((16, 2048), BF),
            pltpu.VMEM((2048, TOK), BF),
            pltpu.VMEM((3, BLOCK, 2 * BLOCK), BF),
            pltpu.VMEM((a,), jnp.int32),
            pltpu.VMEM((a,), jnp.int32),
            pltpu.VMEM((b,), jnp.int32),
            pltpu.VMEM((b,), jnp.int32),
            pltpu.SMEM((16, 128), jnp.int32),
            pltpu.SMEM((8, 128), jnp.int32),
            pltpu.SemaphoreType.DMA((15,)),
        ],
        compiler_params=pltpu.CompilerParams(vmem_limit_bytes=40 * 1024 * 1024),
        cost_estimate=pl.CostEstimate(flops=8000000000, bytes_accessed=12000000, transcendentals=0),
    )(in_count, out_count, *[pltpu.with_memory_space_constraint(v, pltpu.HBM) for v in operands])


def in_kernel(offsets, halves, list_ref, n_ref, w_ref, dt_ref, *rest):
    x_refs = rest[: len(offsets) * (2 if halves else 1)]
    acc_in, raw_in, acc_ref, raw_ref, xt, mask = rest[len(x_refs) :]
    fill_mask(mask)
    acc_ref[...] = acc_in[...]
    raw_ref[...] = raw_in[...]
    in_len = 2 * w_ref.shape[0] + UNROLL
    xs = [x_ref[...] for x_ref in x_refs]
    if halves:
        xs = [jnp.concatenate(xs, axis=0)]
    for x, offset in zip(xs, offsets):
        turn(x, xt)
        q = (lax.axis_index("head") + offset) % 4
        columns = pl.ds(pl.multiple_of(q * 2048, 2048), 2048)
        raw_ref[...] += dot(dt_ref[:, columns], x, 1, 1)
        accumulate(xt, w_ref, mask, list_ref, q * in_len, n_ref[q, 0], acc_ref)


def in_projection(in_list, in_n, w, dt_weight, xs, offsets, acc, halves=False, cost=1):
    return pl.pallas_call(
        functools.partial(in_kernel, offsets, halves),
        out_shape=[sds((2304, TOK), F32), sds((16, TOK), F32)],
        in_specs=[SMEM] * 2 + [VMEM] * (4 + len(xs)),
        out_specs=[VMEM] * 2,
        scratch_shapes=[pltpu.VMEM((2048, TOK), BF), pltpu.VMEM((3, BLOCK, 2 * BLOCK), BF)],
        compiler_params=pltpu.CompilerParams(vmem_limit_bytes=32 * 1024 * 1024),
        cost_estimate=pl.CostEstimate(flops=cost * 1000000000, bytes_accessed=cost * 8000000, transcendentals=0),
    )(in_list, in_n, w, dt_weight, *xs, *acc)


def out_kernel(list_ref, n_ref, w_ref, x_ref, scales, out_ref, acc, mask):
    fill_mask(mask)
    acc[...] = jnp.zeros_like(acc)
    accumulate(x_ref, w_ref, mask, list_ref, 0, n_ref[0, 0], acc, scales)
    for i in range(acc.shape[0] // 128):
        rows = pl.ds(128 * i, 128)
        out_ref[:, rows] = acc[rows, :].T.astype(BF)


def out_projection(out_list, out_n, w, normed, scales):
    return pl.pallas_call(
        out_kernel,
        out_shape=sds((TOK, 2048), BF),
        in_specs=[SMEM] * 2 + [VMEM] * 3,
        out_specs=VMEM,
        scratch_shapes=[pltpu.VMEM((2048, TOK), F32), pltpu.VMEM((3, BLOCK, 2 * BLOCK), BF)],
        compiler_params=pltpu.CompilerParams(vmem_limit_bytes=32 * 1024 * 1024),
        cost_estimate=pl.CostEstimate(flops=1000000000, bytes_accessed=8000000, transcendentals=0),
    )(out_list, out_n, w, normed, scales)


def list_for(metas, mine, list_ref, n_ref):
    before = jnp.where(
        lax.broadcasted_iota(jnp.int32, (128, 128), 0) < lax.broadcasted_iota(jnp.int32, (128, 128), 1), 1.0, 0.0
    ).astype(BF)
    k = lax.broadcasted_iota(jnp.int32, (1, 128), 1)
    lists = list_ref.shape[0]
    rows_of = lax.broadcasted_iota(jnp.int32, (lists, 128), 0)
    lanes_of = lax.broadcasted_iota(jnp.int32, (128, 128), 0)
    start = jnp.zeros((1, 1), jnp.int32)
    filled = jnp.zeros((lists, 128), F32)
    total = jnp.zeros((lists, 128), jnp.int32)
    for g in range(4):
        rows, cols, count = metas[g, 0:1, :], metas[g, 1:2, :], metas[g, 2:3, :]
        live = (k < count) & ((cols >> 5) == mine)
        member = jnp.where(live, 1.0, 0.0)
        order = dot(jnp.broadcast_to(member, (16, 128)).astype(BF), before)[0:1, :]
        position = order.astype(jnp.int32) + start
        value = ((g * 64 + (k >> 1)) << 14) + ((k & 1) << 12) + ((g * 16 + rows) << 6) + (cols & 31)
        row = jnp.where((rows_of == (position >> 7)) & live, 1.0, 0.0)
        lane = jnp.where(lanes_of == (position & 127), 1.0, 0.0).astype(BF)
        filled = filled + dot(row.astype(BF), lane, 1, 1)
        for shift in (0, 8, 16):
            byte = ((value >> shift) & 255).astype(F32)
            total = total + (dot((row * byte).astype(BF), lane, 1, 1).astype(jnp.int32) << shift)
        start = start + jnp.sum(member, axis=1, keepdims=True).astype(jnp.int32)
    list_ref[...] = jnp.where(filled > 0.5, total, 2 << 12)
    n_ref[...] = jnp.broadcast_to(start, (8, 128))


def hops(i):
    return min(i % 4, 4 - i % 4) + min(i // 4, 8 - i // 4)


FAR_FIRST = sorted(range(1, 32), key=hops, reverse=True)


def silu(v):
    return v / (1.0 + jnp.exp(-v))


def mixer_kernel(
    dt_bias,
    a_log,
    skip_gain,
    acc_ref,
    raw_ref,
    conv_weight,
    conv_bias,
    norm_gain,
    w_ref,
    meta_ref,
    w_all,
    normed_all,
    list_ref,
    n_ref,
    scales,
    chan_ref,
    metas,
    mixed,
    x_ref,
    inner,
    gate_ref,
    rim_out,
    rim_in,
    own_state,
    send0,
    recv0,
    send1,
    recv1,
    send3,
    recv3,
    recv4,
    prior,
    own_log,
    mate_log,
    chip_log,
    logs,
    factors,
    rim_sems,
    sems0,
    log_sems,
    all_sems,
    sems4,
    meta_sems,
    w_near,
    w_far,
    w_mate,
    w_own,
    n_near,
    n_far,
    scale_sems,
):
    s = lax.axis_index("seq")
    g = lax.axis_index("head")
    core = s % 2
    chip = s // 2
    mate = s + 1 - 2 * core
    after = (s + 1) % 64
    before = (s + 63) % 64
    barrier = pltpu.get_barrier_semaphore()

    def greet(i, carry):
        pl.semaphore_signal(barrier, inc=1, device_id=(lax.rem(s + 2 * i, 64), g), device_id_type=MESH)
        return carry

    lax.fori_loop(1, 32, greet, 0)
    for partner in (after, before, mate):
        pl.semaphore_signal(barrier, inc=1, device_id=(partner, g), device_id_type=MESH)
    for v in (1, 2, 3):
        pl.semaphore_signal(barrier, inc=1, device_id=(s, (g + v) % 4), device_id_type=MESH)

    def copy(src, dst, send_sem, recv_sem, to, group=g):
        return pltpu.make_async_remote_copy(
            src_ref=src,
            dst_ref=dst,
            send_sem=send_sem,
            recv_sem=recv_sem,
            device_id=(to, group),
            device_id_type=MESH,
        )

    def to_chips(source, target, k):
        for i in FAR_FIRST:
            copy(source(i), target.at[i - 1], all_sems.at[0, k], all_sems.at[1, k], lax.rem(s + 2 * i, 64)).start()

    def from_chips(target, k):
        return copy(target.at[pl.ds(0, 31)], target.at[pl.ds(0, 31)], all_sems.at[0, k], all_sems.at[1, k], mate)

    def place_of(j):
        return lax.rem(chip + 31 - j, 32)

    right, left = (g + 1) % 4, (g + 3) % 4
    far = (g + 2) % 4

    class Ring:
        def __init__(self, near, beyond, view):
            self.near = [
                [copy(view(g, i), view(g, i), near.at[0, w, i], near.at[1, w, i], s, to) for i in range(4)]
                for w, to in ((0, right), (1, left))
            ]
            self.far = [
                copy(view(k, i), view(k, i), beyond.at[0, i], beyond.at[1, i], s, to)
                for i, (k, to) in enumerate(((left, right), (right, left)) * 2)
            ]

        def start(self, i):
            self.near[0][i].start()
            self.near[1][i ^ 1].start()

        def forward(self):
            for i in (0, 2):
                self.near[0][i].wait_recv()
                self.far[i].start()
                self.near[1][i + 1].wait_recv()
                self.far[i + 1].start()

        def arrived(self):
            for i in (0, 2):
                self.near[0][i + 1].wait_recv()
                self.near[1][i].wait_recv()

        def finish(self):
            for c in self.far:
                c.wait_recv()

        def sent(self):
            for c in self.near[0] + self.near[1] + self.far:
                c.wait_send()

    own_mixed = acc_ref[pl.ds(1024, 1280), :].astype(BF)
    mixed[...] = own_mixed.astype(F32)
    row16 = lax.broadcasted_iota(jnp.int32, (16, TOK), 0)
    lane16 = lax.broadcasted_iota(jnp.int32, (16, TOK), 1)
    pick = jnp.where((lane16 == row16 + 125) & (row16 < 3), 1.0, 0.0).astype(BF)
    rim_out[...] = dot(pick, own_mixed, 1, 1).astype(BF)
    own_copy = pltpu.make_async_copy(w_ref, w_all.at[g, core], w_own)
    own_copy.start()
    lane = lax.broadcasted_iota(jnp.int32, (TOK, TOK), 1)
    row = lax.broadcasted_iota(jnp.int32, (TOK, TOK), 0)
    bias = jnp.zeros((16, TOK), F32)
    log_rate = jnp.zeros((16, TOK), F32)
    for h in range(16):
        bias = jnp.where(row16 == h, dt_bias[h], bias)
        log_rate = jnp.where(row16 == h, a_log[h], log_rate)
    v = raw_ref[...] + bias
    step = jnp.maximum(v, 0.0) + jnp.log1p(jnp.exp(-jnp.abs(v)))
    rate = -jnp.exp(log_rate)
    pace = step * rate
    causal = row <= lane
    running = dot(pace, jnp.where(causal, 1.0, 0.0), precision=lax.Precision.HIGHEST)
    total = dot(pace, jnp.ones((TOK, TOK), F32), precision=lax.Precision.HIGHEST)
    own_log[...] = total
    for part in range(10):
        lanes = pl.ds(part * 128, 128)
        gain = norm_gain[lanes].reshape(1, 128) if part < 8 else jnp.zeros((1, 128), F32)
        stacked = [conv_weight[:, lanes], conv_bias[lanes].reshape(1, 128), gain, jnp.zeros((2, 128), F32)]
        chan_ref[lanes, 0:8] = jnp.concatenate(stacked, axis=0).T
    tail = jnp.exp(total - running) * step
    lead = jnp.exp(running)
    columns = jnp.concatenate([running, step, jnp.zeros((96, TOK), F32)], axis=0).T
    gate_ref[...] = silu(acc_ref[pl.ds(0, 1024), :].astype(BF).astype(F32))
    share = w_ref.shape[0]
    metas[g] = meta_ref[...]
    own_copy.wait()
    pl.semaphore_wait(barrier, 37)
    rim_copy = copy(rim_out, rim_in, rim_sems.at[0], rim_sems.at[1], after)
    rim_copy.start()
    log_copy = copy(own_log, mate_log, log_sems.at[0], log_sems.at[1], mate)
    log_copy.start()
    meta_copies = [
        copy(meta_ref, metas.at[g], meta_sems.at[0, v - 1], meta_sems.at[1, v - 1], s, (g + v) % 4) for v in (1, 2, 3)
    ]
    for c in meta_copies:
        c.start()
    w_ring = Ring(w_near, w_far, lambda k, i: w_all.at[k, core, pl.ds(i * share // 4, share // 4)])
    for i in range(4):
        w_ring.start(i)

    def to_mate(k):
        return copy(w_all.at[k, core], w_all.at[k, core], w_mate.at[0, k], w_mate.at[1, k], mate)

    log_copy.wait_recv()
    half = pl.ds(pl.multiple_of(core * 8, 8), 8)
    chip_log[...] = own_log[half, :] + mate_log[half, :]
    logs[31] = chip_log[...]
    to_chips(lambda i: chip_log, logs, 0)

    rim_copy.wait_recv()
    keep = jnp.where(s > 0, 1.0, 0.0)
    place = jnp.where((lane16 == row16 + 125) & (row16 < 3), keep, 0.0).astype(BF)
    b_t = None
    c_t = None
    for part in range(10):
        rows = pl.ds(part * 128, 128)
        own = mixed[rows, :]
        rim = dot(rim_in[:, rows], place, 0, 0)
        total_v = jnp.broadcast_to(chan_ref[rows, 4:5], (128, TOK))
        for tap in range(4):
            shift = 3 - tap
            if shift:
                moved = pltpu.roll(jnp.where(lane >= TOK - shift, rim, own), shift, 1)
            else:
                moved = own
            total_v = total_v + chan_ref[rows, tap : tap + 1] * moved
        active = silu(total_v).astype(BF)
        if part < 8:
            x_ref[rows, :] = active
            for k in range(2):
                h = part * 2 + k
                piece = active[k * 64 : k * 64 + 64, :].astype(F32)
                send0[pl.ds(h * 64, 64), :] = (piece * tail[h : h + 1, :]).astype(BF)
        elif part == 8:
            b_t = active
        else:
            c_t = active
    own_state[...] = dot(send0[pl.ds(0, 1024), :], b_t, 1, 1)

    send0[pl.ds(0, 1024), :] = own_state[...].astype(BF)
    copy0 = copy(send0, recv0, sems0.at[0], sems0.at[1], mate)
    copy0.start()
    own_mate = to_mate(g)
    own_mate.start()

    scores = dot(b_t, c_t, 0, 0)

    def inner_heads(first, last):
        for h in range(first, last):
            gap = running[h : h + 1, :] - columns[:, h : h + 1]
            factor = jnp.exp(jnp.where(causal, gap, -jnp.inf))
            weights = (scores * factor * columns[:, 16 + h : 17 + h]).astype(BF)
            rows = pl.ds(h * 64, 64)
            xh = x_ref[rows, :]
            inner[rows, :] = dot(xh, weights) + skip_gain[h] * xh.astype(F32)

    inner_heads(0, 4)
    is_first = core == 0
    factors[0] = jnp.where(is_first, jnp.exp(mate_log[...]), 1.0)
    factors[1] = jnp.where(is_first, 1.0, jnp.exp(total))
    factors[3] = lead
    factors[2] = jnp.where(is_first, 1.0, jnp.exp(mate_log[...]))
    copy0.wait_recv()
    for j in range(8):
        h = core * 8 + j
        rows = pl.ds(pl.multiple_of(h * 64, 64), 64)
        both = factors[0, pl.ds(h, 1), :] * own_state[rows, :] + factors[1, pl.ds(h, 1), :] * recv0[rows, :].astype(F32)
        for k in range(4):
            send1[4 * j + k] = both[16 * k : 16 * k + 16, :].astype(BF)
    to_chips(lambda i: send1.at[lax.rem(chip + i, 32)], recv1, 1)
    recv1[31] = send1[chip]
    inner_heads(4, 11)
    from_chips(logs, 0).wait_recv()
    from_chips(recv1, 1).wait_recv()
    entering = jnp.zeros((16, TOK), F32)
    for j in range(32):
        send3[j] = entering.astype(BF)
        if j < 31:
            place = place_of(j)
            decay = jnp.exp(logs[place, pl.ds(chip // 4, 1), :])
            entering = decay * entering + recv1[place].astype(F32)
    to_chips(lambda i: send3.at[lax.rem(chip + i, 32)], recv3, 2)
    recv3[31] = send3[chip]
    w_ring.forward()
    w_ring.arrived()
    mates = [to_mate(left), to_mate(right)]
    for m in mates:
        m.start()
    inner_heads(11, 16)
    for c in meta_copies:
        c.wait_recv()
    list_for(metas, g, list_ref, n_ref)
    from_chips(recv3, 2).wait_recv()
    copy4 = copy(recv3, recv4, sems4.at[0], sems4.at[1], mate)
    copy4.start()
    with_state = jnp.where(is_first, 0.0, 1.0)

    def to_prior(half, source):
        for j in range(8):
            h = half * 8 + j
            rows = pl.ds(pl.multiple_of(h * 64, 64), 64)
            parts = [source[place_of(4 * j + k)].astype(F32) for k in range(4)]
            value = factors[2, pl.ds(h, 1), :] * jnp.concatenate(parts, axis=0)
            prior[rows, :] = (value + with_state * recv0[rows, :].astype(F32)).astype(BF)

    order = block_order(64)
    ring = Ring(
        n_near, n_far, lambda k, i: normed_all.at[k, pl.ds(pl.multiple_of((2 * core + i) % 4 * 256, 256), 256)]
    )

    def gated_half(half, squares):
        for j in range(8):
            h = half * 8 + j
            rows = pl.ds(pl.multiple_of(h * 64, 64), 64)
            carried = dot(prior[rows, :], c_t) * factors[3, pl.ds(h, 1), :]
            gated = (inner[rows, :] + carried) * gate_ref[rows, :]
            squares = squares + jnp.sum((gated * gated).reshape(8, 8, TOK), axis=0)
            scaled = (gated * chan_ref[rows, 5:6]).astype(BF)
            normed_all[g, rows, :] = dot(order, scaled).astype(BF)
        return squares

    to_prior(core, recv3)
    squares = gated_half(core, jnp.zeros((8, TOK), F32))
    ring.start(0)
    ring.start(1)
    w_ring.finish()
    mates.append(to_mate(far))
    mates[-1].start()
    copy4.wait_recv()
    to_prior(1 - core, recv4)
    squares = gated_half(1 - core, squares)
    ring.start(2)
    ring.start(3)
    mean = jnp.sum(squares, axis=0, keepdims=True) * (1.0 / 1024.0)
    scales[g] = jnp.broadcast_to(lax.rsqrt(mean + EPS), (8, TOK))
    scale_copies = [
        copy(scales.at[g], scales.at[g], scale_sems.at[0, v - 1], scale_sems.at[1, v - 1], s, (g + v) % 4)
        for v in (1, 2, 3)
    ]
    for c in scale_copies:
        c.start()
    ring.forward()
    for c in scale_copies:
        c.wait()
    rim_copy.wait_send()
    copy0.wait_send()
    copy4.wait_send()
    log_copy.wait_send()
    from_chips(logs, 0).wait_send()
    from_chips(recv1, 1).wait_send()
    from_chips(recv3, 2).wait_send()
    for c in meta_copies:
        c.wait_send()
    w_ring.sent()
    for c in [own_mate] + mates:
        c.wait()
    ring.arrived()
    ring.finish()
    ring.sent()


def mixer(dt_bias, a_log, skip_gain, acc, raw, conv_weight, conv_bias, norm_gain, w_half, meta):
    dma = pltpu.SemaphoreType.DMA
    return pl.pallas_call(
        mixer_kernel,
        out_shape=[
            sds((4, 2) + w_half.shape, BF),
            sds((4, 1024, TOK), BF),
            sds((8, 128), jnp.int32),
            sds((8, 128), jnp.int32),
            sds((4, 8, TOK), F32),
        ],
        in_specs=[SMEM] * 3 + [VMEM] * 7,
        out_specs=[VMEM] * 5,
        scratch_shapes=[
            pltpu.VMEM((1280, TOK), F32),
            pltpu.VMEM((4, 8, 128), jnp.int32),
            pltpu.VMEM((1280, TOK), F32),
            pltpu.VMEM((1024, TOK), BF),
            pltpu.VMEM((1024, TOK), F32),
            pltpu.VMEM((1024, TOK), F32),
            pltpu.VMEM((16, 1280), BF),
            pltpu.VMEM((16, 1280), BF),
            pltpu.VMEM((1024, TOK), F32),
            pltpu.VMEM((1024, TOK), BF),
            pltpu.VMEM((1024, TOK), BF),
            pltpu.VMEM((32, 16, TOK), BF),
            pltpu.VMEM((32, 16, TOK), BF),
            pltpu.VMEM((32, 16, TOK), BF),
            pltpu.VMEM((32, 16, TOK), BF),
            pltpu.VMEM((32, 16, TOK), BF),
            pltpu.VMEM((1024, TOK), BF),
            pltpu.VMEM((16, TOK), F32),
            pltpu.VMEM((16, TOK), F32),
            pltpu.VMEM((8, TOK), F32),
            pltpu.VMEM((32, 8, TOK), F32),
            pltpu.VMEM((4, 16, TOK), F32),
            dma((2,)),
            dma((2,)),
            dma((2,)),
            dma((2, 3)),
            dma((2,)),
            dma((2, 3)),
            dma((2, 2, 4)),
            dma((2, 4)),
            dma((2, 4)),
            dma,
            dma((2, 2, 4)),
            dma((2, 4)),
            dma((2, 3)),
        ],
        compiler_params=pltpu.CompilerParams(
            collective_id=0, has_side_effects=True, vmem_limit_bytes=32 * 1024 * 1024
        ),
        cost_estimate=pl.CostEstimate(flops=1000000000, bytes_accessed=8000000, transcendentals=0),
    )(dt_bias, a_log, skip_gain, acc, raw, conv_weight, conv_bias, norm_gain, w_half, meta)


def turned(value, steps):
    count = lax.axis_size("head")
    return lax.ppermute(value, "head", [(i, (i + steps) % count) for i in range(count)])


def per_device(
    tokens,
    in_blocks,
    in_rows,
    in_cols,
    in_count,
    dt_weight,
    dt_bias,
    a_log,
    conv_weight,
    conv_bias,
    skip_gain,
    norm_gain,
    out_blocks,
    out_rows,
    out_cols,
    out_count,
):
    from_left = turned(tokens, 1)
    from_right = turned(tokens, -1)
    in_list, in_n, w_in, w_half, meta, *acc = first_projection(
        in_blocks, in_rows, in_cols, in_count, out_blocks, out_rows, out_cols, out_count, tokens, dt_weight
    )
    common = (in_list, in_n, w_in, dt_weight)
    half = tokens.shape[0] // 2
    opposite_a = turned(from_left[:half], 1)
    opposite_b = turned(from_right[half:], -1)
    acc = in_projection(*common, [from_left, from_right], [3, 1], acc, cost=20)
    acc, raw = in_projection(*common, [opposite_a, opposite_b], [2], acc, halves=True)
    w_all, normed, out_list, out_n, scales = mixer(
        dt_bias, a_log, skip_gain, acc, raw, conv_weight, conv_bias, norm_gain, w_half, meta
    )
    return out_projection(out_list, out_n, w_all.reshape(-1, BLOCK, 2 * BLOCK), normed.reshape(-1, TOK), scales)


def solution(mesh):
    return jax.shard_map(
        per_device,
        mesh=mesh,
        in_specs=(
            P("seq", "head"),
            P("head", None),
            P("head"),
            P("head"),
            P("head"),
            P("head", None),
            P("head"),
            P("head"),
            P(None, "head"),
            P("head"),
            P("head"),
            P("head"),
            P("head", None),
            P("head"),
            P("head"),
            P("head"),
        ),
        out_specs=P("seq", "head"),
        check_vma=False,
    )
```

```python
import functools

import jax
import jax.numpy as jnp
from jax import lax
from jax.experimental import pallas as pl
from jax.experimental.pallas import tpu as pltpu
from jax.sharding import PartitionSpec as P

MESH = pl.DeviceIdType.MESH
BF = jnp.bfloat16
F32 = jnp.float32
BLOCK = 64
TOK = 128
UNROLL = 32
EPS = 1e-05
VMEM = pl.BlockSpec(memory_space=pltpu.VMEM)
SMEM = pl.BlockSpec(memory_space=pltpu.SMEM)
HBM = pl.BlockSpec(memory_space=pltpu.HBM)


def sds(shape, dtype):
    return jax.ShapeDtypeStruct(shape, dtype)


def dot(a, b, ca=1, cb=0, precision=None):
    return lax.dot_general(
        a, b, (((ca,), (cb,)), ((), ())), preferred_element_type=F32, precision=precision
    )


def block_order(size):
    place = lax.broadcasted_iota(jnp.int32, (size, size), 0)
    feature = lax.broadcasted_iota(jnp.int32, (size, size), 1)
    source = (place & ~63) + 2 * (place & 31) + ((place >> 5) & 1)
    return jnp.where(feature == source, 1.0, 0.0).astype(BF)


def turn(x, turned_ref):
    order = block_order(128)
    for i in range(x.shape[1] // 128):
        rows = pl.ds(128 * i, 128)
        turned_ref[rows, :] = dot(order, x[:, 128 * i : 128 * i + 128], 1, 1).astype(BF)


def to_tiles(src, dst, unroll=1):
    lane = lax.broadcasted_iota(jnp.int32, (64, 128), 1)
    low = lane < 64

    def sixteen(g, carry):
        v = src[pl.ds(pl.multiple_of(g * 16, 16), 16), :].astype(F32)
        for s0 in (0, 8):
            t = jnp.swapaxes(jnp.stack([v[s0 : s0 + 8, 128 * j : 128 * j + 128] for j in range(32)], axis=0), 0, 1)
            for i in (0, 4):
                m = t[i : i + 4].reshape(128, 128).astype(BF).T.astype(F32)
                even, odd = m[:64], m[64:]
                k = g * 8 + (s0 + i) // 2
                dst[k] = jnp.where(low, even, pltpu.roll(odd, 64, 1)).astype(BF)
                dst[k + 1] = jnp.where(low, pltpu.roll(even, 64, 1), odd).astype(BF)
        return carry

    lax.fori_loop(0, src.shape[0] // 16, sixteen, 0, unroll=unroll)


def to_list(quarter, value, count, length, list_ref, n_ref):
    slots = quarter.shape[1]
    lists = list_ref.shape[0]
    live = lax.broadcasted_iota(jnp.int32, (1, slots), 1) < count
    one_of = lambda n, v: lax.broadcasted_iota(jnp.int32, (n, slots), 0) == v
    member = jnp.where(one_of(8, quarter) & live, 1.0, 0.0)
    before = jnp.where(
        lax.broadcasted_iota(jnp.int32, (slots, slots), 0) < lax.broadcasted_iota(jnp.int32, (slots, slots), 1), 1.0, 0.0
    ).astype(BF)
    order = dot(member.astype(BF), before)
    position = quarter * length + jnp.sum(member * order, axis=0, keepdims=True).astype(jnp.int32)
    row = jnp.where(one_of(lists, position >> 7) & live, 1.0, 0.0)
    lane = jnp.where(one_of(128, position & 127), 1.0, 0.0).astype(BF)
    filled = dot(row.astype(BF), lane, 1, 1)
    total = jnp.zeros((lists, 128), jnp.int32)
    for shift in (0, 8, 16):
        byte = ((value >> shift) & 255).astype(F32)
        total = total + (dot((row * byte).astype(BF), lane, 1, 1).astype(jnp.int32) << shift)
    list_ref[...] = jnp.where(filled > 0.5, total, 2 << 12)
    n_ref[...] = jnp.broadcast_to(jnp.sum(member, axis=1, keepdims=True), (8, 128)).astype(jnp.int32)


def fill_mask(mask):
    half = (lax.broadcasted_iota(jnp.int32, (BLOCK, 2 * BLOCK), 1) >> 5) & 1
    for k in range(3):
        mask[k] = jnp.where(half == k, 1.0, 0.0).astype(BF)


def accumulate(x_ref, w_ref, mask_ref, list_ref, base, count, acc_ref, scales=None):
    def turn(i, carry):
        parts = []
        for u in range(UNROLL):
            at = base + i * UNROLL + u
            e = list_ref[at >> 7, at & 127]
            r = pl.multiple_of(((e >> 6) & 63) * BLOCK, BLOCK)
            c = pl.multiple_of((e & 63) * BLOCK, BLOCK)
            w = w_ref[e >> 14] * mask_ref[(e >> 12) & 3]
            even = x_ref[pl.ds(r, BLOCK // 2), :]
            odd = x_ref[pl.ds(r + BLOCK // 2, BLOCK // 2), :]
            product = dot(w, jnp.concatenate([even, even, odd, odd], axis=0))
            if scales is not None:
                product = product * scales[(e >> 10) & 3, 0:1, :]
            parts.append((c, product))
        for c, product in parts:
            acc_ref[pl.ds(c, BLOCK), :] += product
        return carry

    lax.fori_loop(0, (count + UNROLL - 1) // UNROLL, turn, 0)


def first_kernel(
    in_count, out_count, in_rows, in_cols, out_rows, out_cols, in_blocks, out_blocks, tokens, dt_weight,
    in_list, in_n, w_in, w_out, meta, acc_ref, raw_ref,
    in_held, out_held, x_held, dt_held, xt, mask, rows_in, cols_in, rows_out, cols_out, list_held, n_held, sems,
):
    core = lax.axis_index("seq") % 2
    q = lax.axis_index("head")
    chunk = in_held.shape[0] // 4
    share = out_held.shape[0]
    pairs = [
        (in_rows, rows_in),
        (in_cols, cols_in),
        (out_rows, rows_out),
        (out_cols, cols_out),
    ]
    pairs += [(in_blocks.at[pl.ds(i * chunk, chunk)], in_held.at[pl.ds(i * chunk, chunk)]) for i in range(4)]
    columns = pl.ds(pl.multiple_of(q * 2048, 2048), 2048)
    pairs += [
        (tokens, x_held),
        (dt_weight.at[:, columns], dt_held),
        (out_blocks.at[pl.ds(pl.multiple_of(core * share, share), share)], out_held),
    ]
    copies = [pltpu.make_async_copy(a, b, sems.at[i]) for i, (a, b) in enumerate(pairs)]
    for c in copies:
        c.start()
    fill_mask(mask)
    acc_ref[...] = jnp.zeros_like(acc_ref)
    for c in copies[:4]:
        c.wait()
    slots = in_rows.shape[0]
    k = lax.broadcasted_iota(jnp.int32, (1, slots), 1)
    r = rows_in[...].reshape(1, slots)
    value = ((k >> 1) << 14) + ((k & 1) << 12) + ((r & 31) << 6) + cols_in[...].reshape(1, slots)
    to_list(r >> 5, value, in_count[0], slots + UNROLL, in_list, in_n)
    to_smem = [
        pltpu.make_async_copy(in_list, list_held, sems.at[13]),
        pltpu.make_async_copy(in_n, n_held, sems.at[14]),
    ]
    for c in to_smem:
        c.start()
    slots = out_rows.shape[0]
    meta[0:1, :] = rows_out[...].reshape(1, slots)
    meta[1:2, :] = cols_out[...].reshape(1, slots)
    meta[2:8, :] = jnp.broadcast_to(out_count[0], (6, slots))
    for i in range(4):
        copies[4 + i].wait()
        to_tiles(in_held.at[pl.ds(i * chunk, chunk)], w_in.at[pl.ds(i * chunk // 2, chunk // 2)], 2)
    for c in copies[8:] + to_smem:
        c.wait()
    x = x_held[...]
    turn(x, xt)
    raw_ref[...] = dot(dt_held[...], x, 1, 1)
    in_len = 2 * w_in.shape[0] + UNROLL
    accumulate(xt, w_in, mask, list_held, q * in_len, n_held[q, 0], acc_ref)
    to_tiles(out_held, w_out, 2)


def first_projection(in_blocks, in_rows, in_cols, in_count, out_blocks, out_rows, out_cols, out_count, tokens, dt_weight):
    a, b = in_rows.shape[0], out_rows.shape[0]
    operands = (in_rows, in_cols, out_rows, out_cols, in_blocks, out_blocks, tokens, dt_weight)
    return pl.pallas_call(
        first_kernel,
        out_shape=[
            sds((16, 128), jnp.int32),
            sds((8, 128), jnp.int32),
            sds((a // 2, BLOCK, 2 * BLOCK), BF),
            sds((b // 4, BLOCK, 2 * BLOCK), BF),
            sds((8, 128), jnp.int32),
            sds((2304, TOK), F32),
            sds((16, TOK), F32),
        ],
        in_specs=[SMEM] * 2 + [HBM] * 8,
        out_specs=[VMEM] * 7,
        scratch_shapes=[
            pltpu.VMEM(in_blocks.shape, BF),
            pltpu.VMEM((b // 2, out_blocks.shape[1]), BF),
            pltpu.VMEM(tokens.shape, BF),
            pltpu.VMEM((16, 2048), BF),
            pltpu.VMEM((2048, TOK), BF),
            pltpu.VMEM((3, BLOCK, 2 * BLOCK), BF),
            pltpu.VMEM((a,), jnp.int32),
            pltpu.VMEM((a,), jnp.int32),
            pltpu.VMEM((b,), jnp.int32),
            pltpu.VMEM((b,), jnp.int32),
            pltpu.SMEM((16, 128), jnp.int32),
            pltpu.SMEM((8, 128), jnp.int32),
            pltpu.SemaphoreType.DMA((15,)),
        ],
        compiler_params=pltpu.CompilerParams(vmem_limit_bytes=40 * 1024 * 1024),
        cost_estimate=pl.CostEstimate(flops=8000000000, bytes_accessed=12000000, transcendentals=0),
    )(in_count, out_count, *[pltpu.with_memory_space_constraint(v, pltpu.HBM) for v in operands])


def in_kernel(offsets, halves, list_ref, n_ref, w_ref, dt_ref, *rest):
    x_refs = rest[: len(offsets) * (2 if halves else 1)]
    acc_in, raw_in, acc_ref, raw_ref, xt, mask = rest[len(x_refs) :]
    fill_mask(mask)
    acc_ref[...] = acc_in[...]
    raw_ref[...] = raw_in[...]
    in_len = 2 * w_ref.shape[0] + UNROLL
    xs = [x_ref[...] for x_ref in x_refs]
    if halves:
        xs = [jnp.concatenate(xs, axis=0)]
    for x, offset in zip(xs, offsets):
        turn(x, xt)
        q = (lax.axis_index("head") + offset) % 4
        columns = pl.ds(pl.multiple_of(q * 2048, 2048), 2048)
        raw_ref[...] += dot(dt_ref[:, columns], x, 1, 1)
        accumulate(xt, w_ref, mask, list_ref, q * in_len, n_ref[q, 0], acc_ref)


def in_projection(in_list, in_n, w, dt_weight, xs, offsets, acc, halves=False, cost=1):
    return pl.pallas_call(
        functools.partial(in_kernel, offsets, halves),
        out_shape=[sds((2304, TOK), F32), sds((16, TOK), F32)],
        in_specs=[SMEM] * 2 + [VMEM] * (4 + len(xs)),
        out_specs=[VMEM] * 2,
        scratch_shapes=[pltpu.VMEM((2048, TOK), BF), pltpu.VMEM((3, BLOCK, 2 * BLOCK), BF)],
        compiler_params=pltpu.CompilerParams(vmem_limit_bytes=32 * 1024 * 1024),
        cost_estimate=pl.CostEstimate(flops=cost * 1000000000, bytes_accessed=cost * 8000000, transcendentals=0),
    )(in_list, in_n, w, dt_weight, *xs, *acc)


def out_kernel(list_ref, n_ref, w_ref, x_ref, scales, out_ref, acc, mask):
    fill_mask(mask)
    acc[...] = jnp.zeros_like(acc)
    accumulate(x_ref, w_ref, mask, list_ref, 0, n_ref[0, 0], acc, scales)
    for i in range(acc.shape[0] // 128):
        rows = pl.ds(128 * i, 128)
        out_ref[:, rows] = acc[rows, :].astype(BF).T


def out_projection(out_list, out_n, w, normed, scales):
    return pl.pallas_call(
        out_kernel,
        out_shape=sds((TOK, 2048), BF),
        in_specs=[SMEM] * 2 + [VMEM] * 3,
        out_specs=VMEM,
        scratch_shapes=[pltpu.VMEM((2048, TOK), F32), pltpu.VMEM((3, BLOCK, 2 * BLOCK), BF)],
        compiler_params=pltpu.CompilerParams(vmem_limit_bytes=32 * 1024 * 1024),
        cost_estimate=pl.CostEstimate(flops=1000000000, bytes_accessed=8000000, transcendentals=0),
    )(out_list, out_n, w, normed, scales)


def list_for(metas, mine, list_ref, n_ref):
    before = jnp.where(
        lax.broadcasted_iota(jnp.int32, (128, 128), 0) < lax.broadcasted_iota(jnp.int32, (128, 128), 1), 1.0, 0.0
    ).astype(BF)
    k = lax.broadcasted_iota(jnp.int32, (1, 128), 1)
    lists = list_ref.shape[0]
    rows_of = lax.broadcasted_iota(jnp.int32, (lists, 128), 0)
    lanes_of = lax.broadcasted_iota(jnp.int32, (128, 128), 0)
    start = jnp.zeros((1, 1), jnp.int32)
    filled = jnp.zeros((lists, 128), F32)
    total = jnp.zeros((lists, 128), jnp.int32)
    for g in range(4):
        rows, cols, count = metas[g, 0:1, :], metas[g, 1:2, :], metas[g, 2:3, :]
        live = (k < count) & ((cols >> 5) == mine)
        member = jnp.where(live, 1.0, 0.0)
        order = dot(jnp.broadcast_to(member, (16, 128)).astype(BF), before)[0:1, :]
        position = order.astype(jnp.int32) + start
        value = ((g * 64 + (k >> 1)) << 14) + ((k & 1) << 12) + ((g * 16 + rows) << 6) + (cols & 31)
        row = jnp.where((rows_of == (position >> 7)) & live, 1.0, 0.0)
        lane = jnp.where(lanes_of == (position & 127), 1.0, 0.0).astype(BF)
        filled = filled + dot(row.astype(BF), lane, 1, 1)
        for shift in (0, 8, 16):
            byte = ((value >> shift) & 255).astype(F32)
            total = total + (dot((row * byte).astype(BF), lane, 1, 1).astype(jnp.int32) << shift)
        start = start + jnp.sum(member, axis=1, keepdims=True).astype(jnp.int32)
    list_ref[...] = jnp.where(filled > 0.5, total, 2 << 12)
    n_ref[...] = jnp.broadcast_to(start, (8, 128))


def hops(i):
    return min(i % 4, 4 - i % 4) + min(i // 4, 8 - i // 4)


FAR_FIRST = sorted(range(1, 32), key=hops, reverse=True)


def silu(v):
    return v / (1.0 + jnp.exp(-v))


def mixer_kernel(
    dt_bias,
    a_log,
    skip_gain,
    acc_ref,
    raw_ref,
    conv_weight,
    conv_bias,
    norm_gain,
    w_ref,
    meta_ref,
    w_all,
    normed_all,
    list_ref,
    n_ref,
    scales,
    chan_ref,
    metas,
    mixed,
    x_ref,
    inner,
    gate_ref,
    rim_out,
    rim_in,
    own_state,
    send0,
    recv0,
    send1,
    recv1,
    send3,
    recv3,
    recv4,
    prior,
    own_log,
    mate_log,
    chip_log,
    logs,
    factors,
    rim_sems,
    sems0,
    log_sems,
    all_sems,
    sems4,
    meta_sems,
    w_near,
    w_far,
    w_mate,
    w_own,
    n_near,
    n_far,
    scale_sems,
):
    s = lax.axis_index("seq")
    g = lax.axis_index("head")
    core = s % 2
    chip = s // 2
    mate = s + 1 - 2 * core
    after = (s + 1) % 64
    before = (s + 63) % 64
    barrier = pltpu.get_barrier_semaphore()

    def greet(i, carry):
        pl.semaphore_signal(barrier, inc=1, device_id=(lax.rem(s + 2 * i, 64), g), device_id_type=MESH)
        return carry

    lax.fori_loop(1, 32, greet, 0)
    for partner in (after, before, mate):
        pl.semaphore_signal(barrier, inc=1, device_id=(partner, g), device_id_type=MESH)
    for v in (1, 2, 3):
        pl.semaphore_signal(barrier, inc=1, device_id=(s, (g + v) % 4), device_id_type=MESH)

    def copy(src, dst, send_sem, recv_sem, to, group=g):
        return pltpu.make_async_remote_copy(
            src_ref=src,
            dst_ref=dst,
            send_sem=send_sem,
            recv_sem=recv_sem,
            device_id=(to, group),
            device_id_type=MESH,
        )

    def to_chips(source, target, k):
        for i in FAR_FIRST:
            copy(source(i), target.at[i - 1], all_sems.at[0, k], all_sems.at[1, k], lax.rem(s + 2 * i, 64)).start()

    def from_chips(target, k):
        return copy(target.at[pl.ds(0, 31)], target.at[pl.ds(0, 31)], all_sems.at[0, k], all_sems.at[1, k], mate)

    def place_of(j):
        return lax.rem(chip + 31 - j, 32)

    right, left = (g + 1) % 4, (g + 3) % 4
    far = (g + 2) % 4

    class Ring:
        def __init__(self, near, beyond, view):
            self.near = [
                [copy(view(g, i), view(g, i), near.at[0, w, i], near.at[1, w, i], s, to) for i in range(4)]
                for w, to in ((0, right), (1, left))
            ]
            self.far = [
                copy(view(k, i), view(k, i), beyond.at[0, i], beyond.at[1, i], s, to)
                for i, (k, to) in enumerate(((left, right), (right, left)) * 2)
            ]

        def start(self, i):
            self.near[0][i].start()
            self.near[1][i ^ 1].start()

        def forward(self):
            for i in (0, 2):
                self.near[0][i].wait_recv()
                self.far[i].start()
                self.near[1][i + 1].wait_recv()
                self.far[i + 1].start()

        def arrived(self):
            for i in (0, 2):
                self.near[0][i + 1].wait_recv()
                self.near[1][i].wait_recv()

        def finish(self):
            for c in self.far:
                c.wait_recv()

        def sent(self):
            for c in self.near[0] + self.near[1] + self.far:
                c.wait_send()

    own_mixed = acc_ref[pl.ds(1024, 1280), :].astype(BF)
    mixed[...] = own_mixed.astype(F32)
    row16 = lax.broadcasted_iota(jnp.int32, (16, TOK), 0)
    lane16 = lax.broadcasted_iota(jnp.int32, (16, TOK), 1)
    pick = jnp.where((lane16 == row16 + 125) & (row16 < 3), 1.0, 0.0).astype(BF)
    rim_out[...] = dot(pick, own_mixed, 1, 1).astype(BF)
    own_copy = pltpu.make_async_copy(w_ref, w_all.at[g, core], w_own)
    own_copy.start()
    lane = lax.broadcasted_iota(jnp.int32, (TOK, TOK), 1)
    row = lax.broadcasted_iota(jnp.int32, (TOK, TOK), 0)
    bias = jnp.zeros((16, TOK), F32)
    log_rate = jnp.zeros((16, TOK), F32)
    for h in range(16):
        bias = jnp.where(row16 == h, dt_bias[h], bias)
        log_rate = jnp.where(row16 == h, a_log[h], log_rate)
    v = raw_ref[...] + bias
    step = jnp.maximum(v, 0.0) + jnp.log1p(jnp.exp(-jnp.abs(v)))
    rate = -jnp.exp(log_rate)
    pace = step * rate
    causal = row <= lane
    running = dot(pace, jnp.where(causal, 1.0, 0.0), precision=lax.Precision.HIGHEST)
    total = dot(pace, jnp.ones((TOK, TOK), F32), precision=lax.Precision.HIGHEST)
    own_log[...] = total
    for part in range(10):
        lanes = pl.ds(part * 128, 128)
        gain = norm_gain[lanes].reshape(1, 128) if part < 8 else jnp.zeros((1, 128), F32)
        stacked = [conv_weight[:, lanes], conv_bias[lanes].reshape(1, 128), gain, jnp.zeros((2, 128), F32)]
        chan_ref[lanes, 0:8] = jnp.concatenate(stacked, axis=0).T
    tail = jnp.exp(total - running) * step
    lead = jnp.exp(running)
    columns = jnp.concatenate([running, step, jnp.zeros((96, TOK), F32)], axis=0).T
    gate_ref[...] = silu(acc_ref[pl.ds(0, 1024), :].astype(BF).astype(F32))
    share = w_ref.shape[0]
    metas[g] = meta_ref[...]
    own_copy.wait()
    pl.semaphore_wait(barrier, 37)
    rim_copy = copy(rim_out, rim_in, rim_sems.at[0], rim_sems.at[1], after)
    rim_copy.start()
    log_copy = copy(own_log, mate_log, log_sems.at[0], log_sems.at[1], mate)
    log_copy.start()
    meta_copies = [
        copy(meta_ref, metas.at[g], meta_sems.at[0, v - 1], meta_sems.at[1, v - 1], s, (g + v) % 4) for v in (1, 2, 3)
    ]
    for c in meta_copies:
        c.start()
    w_ring = Ring(w_near, w_far, lambda k, i: w_all.at[k, core, pl.ds(i * share // 4, share // 4)])
    for i in range(4):
        w_ring.start(i)

    def to_mate(k):
        return copy(w_all.at[k, core], w_all.at[k, core], w_mate.at[0, k], w_mate.at[1, k], mate)

    log_copy.wait_recv()
    half = pl.ds(pl.multiple_of(core * 8, 8), 8)
    chip_log[...] = own_log[half, :] + mate_log[half, :]
    logs[31] = chip_log[...]
    to_chips(lambda i: chip_log, logs, 0)

    rim_copy.wait_recv()
    keep = jnp.where(s > 0, 1.0, 0.0)
    place = jnp.where((lane16 == row16 + 125) & (row16 < 3), keep, 0.0).astype(BF)
    b_t = None
    c_t = None
    for part in range(10):
        rows = pl.ds(part * 128, 128)
        own = mixed[rows, :]
        rim = dot(rim_in[:, rows], place, 0, 0)
        total_v = jnp.broadcast_to(chan_ref[rows, 4:5], (128, TOK))
        for tap in range(4):
            shift = 3 - tap
            if shift:
                moved = pltpu.roll(jnp.where(lane >= TOK - shift, rim, own), shift, 1)
            else:
                moved = own
            total_v = total_v + chan_ref[rows, tap : tap + 1] * moved
        active = silu(total_v).astype(BF)
        if part < 8:
            x_ref[rows, :] = active
            for k in range(2):
                h = part * 2 + k
                piece = active[k * 64 : k * 64 + 64, :].astype(F32)
                send0[pl.ds(h * 64, 64), :] = (piece * tail[h : h + 1, :]).astype(BF)
        elif part == 8:
            b_t = active
        else:
            c_t = active
    own_state[...] = dot(send0[pl.ds(0, 1024), :], b_t, 1, 1)

    send0[pl.ds(0, 1024), :] = own_state[...].astype(BF)
    copy0 = copy(send0, recv0, sems0.at[0], sems0.at[1], mate)
    copy0.start()
    own_mate = to_mate(g)
    own_mate.start()

    scores = dot(b_t, c_t, 0, 0)

    def inner_heads(first, last):
        for h in range(first, last):
            gap = running[h : h + 1, :] - columns[:, h : h + 1]
            factor = jnp.exp(jnp.where(causal, gap, -jnp.inf))
            weights = (scores * factor * columns[:, 16 + h : 17 + h]).astype(BF)
            rows = pl.ds(h * 64, 64)
            xh = x_ref[rows, :]
            inner[rows, :] = dot(xh, weights) + skip_gain[h] * xh.astype(F32)

    inner_heads(0, 4)
    is_first = core == 0
    factors[0] = jnp.where(is_first, jnp.exp(mate_log[...]), 1.0)
    factors[1] = jnp.where(is_first, 1.0, jnp.exp(total))
    factors[3] = lead
    factors[2] = jnp.where(is_first, 1.0, jnp.exp(mate_log[...]))
    copy0.wait_recv()
    for j in range(8):
        h = core * 8 + j
        rows = pl.ds(pl.multiple_of(h * 64, 64), 64)
        both = factors[0, pl.ds(h, 1), :] * own_state[rows, :] + factors[1, pl.ds(h, 1), :] * recv0[rows, :].astype(F32)
        for k in range(4):
            send1[4 * j + k] = both[16 * k : 16 * k + 16, :].astype(BF)
    to_chips(lambda i: send1.at[lax.rem(chip + i, 32)], recv1, 1)
    recv1[31] = send1[chip]
    inner_heads(4, 11)
    from_chips(logs, 0).wait_recv()
    from_chips(recv1, 1).wait_recv()
    entering = jnp.zeros((16, TOK), F32)
    for j in range(32):
        send3[j] = entering.astype(BF)
        if j < 31:
            place = place_of(j)
            decay = jnp.exp(logs[place, pl.ds(chip // 4, 1), :])
            entering = decay * entering + recv1[place].astype(F32)
    to_chips(lambda i: send3.at[lax.rem(chip + i, 32)], recv3, 2)
    recv3[31] = send3[chip]
    w_ring.forward()
    w_ring.arrived()
    mates = [to_mate(left), to_mate(right)]
    for m in mates:
        m.start()
    inner_heads(11, 16)
    for c in meta_copies:
        c.wait_recv()
    list_for(metas, g, list_ref, n_ref)
    from_chips(recv3, 2).wait_recv()
    copy4 = copy(recv3, recv4, sems4.at[0], sems4.at[1], mate)
    copy4.start()
    with_state = jnp.where(is_first, 0.0, 1.0)

    def to_prior(half, source):
        for j in range(8):
            h = half * 8 + j
            rows = pl.ds(pl.multiple_of(h * 64, 64), 64)
            parts = [source[place_of(4 * j + k)].astype(F32) for k in range(4)]
            value = factors[2, pl.ds(h, 1), :] * jnp.concatenate(parts, axis=0)
            prior[rows, :] = (value + with_state * recv0[rows, :].astype(F32)).astype(BF)

    order = block_order(64)
    ring = Ring(
        n_near, n_far, lambda k, i: normed_all.at[k, pl.ds(pl.multiple_of((2 * core + i) % 4 * 256, 256), 256)]
    )

    def gated_half(half, squares):
        for j in range(8):
            h = half * 8 + j
            rows = pl.ds(pl.multiple_of(h * 64, 64), 64)
            carried = dot(prior[rows, :], c_t) * factors[3, pl.ds(h, 1), :]
            gated = (inner[rows, :] + carried) * gate_ref[rows, :]
            squares = squares + jnp.sum((gated * gated).reshape(8, 8, TOK), axis=0)
            scaled = (gated * chan_ref[rows, 5:6]).astype(BF)
            normed_all[g, rows, :] = dot(order, scaled).astype(BF)
        return squares

    to_prior(core, recv3)
    squares = gated_half(core, jnp.zeros((8, TOK), F32))
    ring.start(0)
    ring.start(1)
    w_ring.finish()
    mates.append(to_mate(far))
    mates[-1].start()
    copy4.wait_recv()
    to_prior(1 - core, recv4)
    squares = gated_half(1 - core, squares)
    ring.start(2)
    ring.start(3)
    mean = jnp.sum(squares, axis=0, keepdims=True) * (1.0 / 1024.0)
    scales[g] = jnp.broadcast_to(lax.rsqrt(mean + EPS), (8, TOK))
    scale_copies = [
        copy(scales.at[g], scales.at[g], scale_sems.at[0, v - 1], scale_sems.at[1, v - 1], s, (g + v) % 4)
        for v in (1, 2, 3)
    ]
    for c in scale_copies:
        c.start()
    ring.forward()
    for c in scale_copies:
        c.wait()
    rim_copy.wait_send()
    copy0.wait_send()
    copy4.wait_send()
    log_copy.wait_send()
    from_chips(logs, 0).wait_send()
    from_chips(recv1, 1).wait_send()
    from_chips(recv3, 2).wait_send()
    for c in meta_copies:
        c.wait_send()
    w_ring.sent()
    for c in [own_mate] + mates:
        c.wait()
    ring.arrived()
    ring.finish()
    ring.sent()


def mixer(dt_bias, a_log, skip_gain, acc, raw, conv_weight, conv_bias, norm_gain, w_half, meta):
    dma = pltpu.SemaphoreType.DMA
    return pl.pallas_call(
        mixer_kernel,
        out_shape=[
            sds((4, 2) + w_half.shape, BF),
            sds((4, 1024, TOK), BF),
            sds((8, 128), jnp.int32),
            sds((8, 128), jnp.int32),
            sds((4, 8, TOK), F32),
        ],
        in_specs=[SMEM] * 3 + [VMEM] * 7,
        out_specs=[VMEM] * 5,
        scratch_shapes=[
            pltpu.VMEM((1280, TOK), F32),
            pltpu.VMEM((4, 8, 128), jnp.int32),
            pltpu.VMEM((1280, TOK), F32),
            pltpu.VMEM((1024, TOK), BF),
            pltpu.VMEM((1024, TOK), F32),
            pltpu.VMEM((1024, TOK), F32),
            pltpu.VMEM((16, 1280), BF),
            pltpu.VMEM((16, 1280), BF),
            pltpu.VMEM((1024, TOK), F32),
            pltpu.VMEM((1024, TOK), BF),
            pltpu.VMEM((1024, TOK), BF),
            pltpu.VMEM((32, 16, TOK), BF),
            pltpu.VMEM((32, 16, TOK), BF),
            pltpu.VMEM((32, 16, TOK), BF),
            pltpu.VMEM((32, 16, TOK), BF),
            pltpu.VMEM((32, 16, TOK), BF),
            pltpu.VMEM((1024, TOK), BF),
            pltpu.VMEM((16, TOK), F32),
            pltpu.VMEM((16, TOK), F32),
            pltpu.VMEM((8, TOK), F32),
            pltpu.VMEM((32, 8, TOK), F32),
            pltpu.VMEM((4, 16, TOK), F32),
            dma((2,)),
            dma((2,)),
            dma((2,)),
            dma((2, 3)),
            dma((2,)),
            dma((2, 3)),
            dma((2, 2, 4)),
            dma((2, 4)),
            dma((2, 4)),
            dma,
            dma((2, 2, 4)),
            dma((2, 4)),
            dma((2, 3)),
        ],
        compiler_params=pltpu.CompilerParams(
            collective_id=0, has_side_effects=True, vmem_limit_bytes=32 * 1024 * 1024
        ),
        cost_estimate=pl.CostEstimate(flops=1000000000, bytes_accessed=8000000, transcendentals=0),
    )(dt_bias, a_log, skip_gain, acc, raw, conv_weight, conv_bias, norm_gain, w_half, meta)


def turned(value, steps):
    count = lax.axis_size("head")
    return lax.ppermute(value, "head", [(i, (i + steps) % count) for i in range(count)])


def per_device(
    tokens,
    in_blocks,
    in_rows,
    in_cols,
    in_count,
    dt_weight,
    dt_bias,
    a_log,
    conv_weight,
    conv_bias,
    skip_gain,
    norm_gain,
    out_blocks,
    out_rows,
    out_cols,
    out_count,
):
    from_left = turned(tokens, 1)
    from_right = turned(tokens, -1)
    in_list, in_n, w_in, w_half, meta, *acc = first_projection(
        in_blocks, in_rows, in_cols, in_count, out_blocks, out_rows, out_cols, out_count, tokens, dt_weight
    )
    common = (in_list, in_n, w_in, dt_weight)
    half = tokens.shape[0] // 2
    opposite_a = turned(from_left[:half], 1)
    opposite_b = turned(from_right[half:], -1)
    acc = in_projection(*common, [from_left, from_right], [3, 1], acc, cost=20)
    acc, raw = in_projection(*common, [opposite_a, opposite_b], [2], acc, halves=True)
    w_all, normed, out_list, out_n, scales = mixer(
        dt_bias, a_log, skip_gain, acc, raw, conv_weight, conv_bias, norm_gain, w_half, meta
    )
    return out_projection(out_list, out_n, w_all.reshape(-1, BLOCK, 2 * BLOCK), normed.reshape(-1, TOK), scales)


def solution(mesh):
    return jax.shard_map(
        per_device,
        mesh=mesh,
        in_specs=(
            P("seq", "head"),
            P("head", None),
            P("head"),
            P("head"),
            P("head"),
            P("head", None),
            P("head"),
            P("head"),
            P(None, "head"),
            P("head"),
            P("head"),
            P("head"),
            P("head", None),
            P("head"),
            P("head"),
            P("head"),
        ),
        out_specs=P("seq", "head"),
        check_vma=False,
    )
```
